32 devices in a mesh: dp: 8 (over z, y), blk: 4 (over x, core).
Axes of the slice: x: 2, y: 2, z: 4, core: 2. Of those that a mesh axis runs over, the one named last changes fastest.
Arguments:
- tokens: bfloat16 [8, 768, 2048], P('dp', 'blk'), may hold values from -6 to 6
- noise_table: bfloat16 [1000, 2048], replicated, may hold values from -6 to 6
- mod_weight: bfloat16 [2048, 12288], P(None, ('dp', 'blk')), may hold values from -0.125 to 0.125
- qkv_weight: bfloat16 [2048, 6144], P(('dp', 'blk')), may hold values from -0.125 to 0.125
- out_weight: bfloat16 [2048, 2048], P(('dp', 'blk')), may hold values from -0.75 to 0.75
- up_weight: bfloat16 [2048, 8192], P(('dp', 'blk')), may hold values from -0.125 to 0.125
- down_weight: bfloat16 [2048, 8192], P(('dp', 'blk')), may hold values from -0.0625 to 0.0625
- segment: int32 [8, 768], P('dp'), may hold values from 0 to 2, never falling along the last dimension, each value on 1 to 672 neighbouring positions
- key_valid: int32 [8, 768], P('dp'), may hold values 0 or 1
- noise_level: int32 [8, 3], replicated, may hold values from 0 to 999
- cotangent: bfloat16 [8, 768, 2048], P('dp', 'blk'), may hold values from -6 to 6
Outputs:
- block_out: bfloat16 [8, 768, 2048], P('dp', 'blk')
- grad_tokens: float32 [8, 768, 2048], P('dp', 'blk')
- grad_table: float32 [1000, 2048], replicated
- grad_mod_weight: float32 [2048, 12288], P(None, ('dp', 'blk'))
- grad_qkv_weight: float32 [2048, 6144], P(('dp', 'blk'))
- grad_out_weight: float32 [2048, 2048], P(('dp', 'blk'))
- grad_up_weight: float32 [2048, 8192], P(('dp', 'blk'))
- grad_down_weight: float32 [2048, 8192], P(('dp', 'blk'))
The draws below stay inside these ranges and needn't reach their ends.
Inputs may be any that keep to these rules, and one draw needn't show every extreme that they name: In each group segment numbers never fall along the positions, every number 0 to 2 occurs, and one image of each group covers exactly 672 positions.
All inputs are finite; a program needn't handle non-finite values. No bound on the sum of `key_valid` on one device may be relied on, other than what follows from the above.
Results may differ from the reference program's by a relative error of at most 0.013.
Values may be sent and summed in bfloat16 or wider, within the bound.
A program may use at most 640 MiB of HBM per device.

```python
import math
import jax
import jax.numpy as jnp
import numpy as np
from jax import lax

D = 2048
FF = 8192
HEADS = 16
HEAD_DIM = 128
TOK_DEV = 192
IMAGES = 3
LEVELS = 1000
GROUP = 768
N_DP = 8


def plant(drawn, stream_key, smallest, top_value):
    extent = drawn.shape
    place = [jax.random.randint(jax.random.fold_in(stream_key, axis), (), 0, extent[axis]) for axis in range(len(extent))]
    drawn = drawn.at[tuple(place)].set(smallest)
    longest = extent.index(max(extent))
    place[longest] = (place[longest] + 1) % extent[longest]
    return drawn.at[tuple(place)].set(top_value)


def strengthened(values, own_key, source, target, blocks, factor):
    def block_of(position):
        return (jnp.arange(values.shape[position]) // (values.shape[position] // blocks)).reshape((-1,) + (1,) * (values.ndim - 1 - position))

    first = jax.random.permutation(own_key, blocks)[block_of(target)]
    second = (block_of(target) + blocks // 2) % blocks
    return jnp.where((block_of(source) == first) | (block_of(source) == second), factor * values, values)


def block_scale(key, dims, cuts, least, largest):
    factor_of = 1.0
    for dim, blocks in cuts:
        heights = jax.random.uniform(jax.random.fold_in(jax.random.fold_in(key, 6), dim), (blocks,), jnp.float32, least / len(cuts), largest / len(cuts))
        factor_of = factor_of * jnp.repeat(jnp.exp(heights), dims[dim] // blocks).reshape((-1,) + (1,) * (len(dims) - 1 - dim))
    return factor_of


def profile(count, total, most, skew):
    loads = [(1 << 20) // math.isqrt(standing ** skew) + 1 for standing in range(2, count + 1)]
    spare, counts = total - most - (count - 1), [1] * (count - 1)
    while spare > 0:
        candidates = [i for i in range(count - 1) if counts[i] < most]
        whole, left = sum([loads[i] for i in candidates]), spare
        for i in candidates:
            extra = min(most - counts[i], max(1, left * loads[i] // whole), spare)
            counts[i] = counts[i] + extra
            spare = spare - extra
    return np.array([most] + counts)


def ragged(key, amount, total, limit, slope):
    if amount == 2:
        one = jax.random.randint(key, (), max(1, total - limit), min(limit, total - 1) + 1)
        return jnp.stack([one, total - one])
    tallies = jnp.asarray(profile(amount, total, limit, slope), jnp.int32)
    pairs = (amount - 1) // 2
    donor, taker = tallies[1:1 + 2 * pairs:2], tallies[2:2 + 2 * pairs:2]
    slack = jnp.minimum(donor - 1, limit - taker)
    moved = jax.random.randint(jax.random.fold_in(key, 1), (pairs,), 0, 1 << 20) % (slack + 1)
    tallies = tallies.at[1:1 + 2 * pairs:2].set(donor - moved).at[2:2 + 2 * pairs:2].set(taker + moved)
    return tallies[jax.random.permutation(jax.random.fold_in(key, 2), amount)]


def bell_draw(own_key, shape, scale, limit, cuts=(), kind=jnp.bfloat16):
    drawn = scale * jax.random.normal(own_key, shape, jnp.float32)
    if cuts:
        drawn = drawn * block_scale(own_key, shape, cuts, -0.22, 0.18)
    return jnp.clip(drawn, -limit, limit).astype(kind)


def heavy_noise(stream_key, extent, scale, most, shards, heavy, kind=jnp.bfloat16):
    values = scale * jax.random.normal(stream_key, extent, jnp.float32)
    if shards:
        values = values * block_scale(stream_key, extent, shards, -0.22, 0.18)
    return jnp.clip(strengthened(values, jax.random.fold_in(stream_key, 3), *heavy), -most, most).astype(kind)


def setup_inputs(seed: int = 0) -> dict:
    streams_of = jax.random.split(jax.random.key(seed), 12)
    return {
        "tokens": bell_draw(streams_of[0], (N_DP, GROUP, D), 1.0, 6.0, ((0, 8), (1, 4))),
        "noise_table": bell_draw(streams_of[1], (LEVELS, D), 1.0, 6.0),
        "mod_weight": heavy_noise(streams_of[2], (D, 6 * D), (4 * D) ** -0.5, 0.125, ((1, 32),), (1, 0, 32, 2.75)),
        "qkv_weight": bell_draw(streams_of[3], (D, 3 * D), D ** -0.5, 0.125, ((0, 32),)),
        "out_weight": bell_draw(streams_of[4], (D, D), (D // 32) ** -0.5, 0.75, ((0, 32),)),
        "up_weight": bell_draw(streams_of[5], (D, FF), D ** -0.5, 0.125, ((0, 32),)),
        "down_weight": bell_draw(streams_of[6], (D, FF), FF ** -0.5, 0.0625, ((0, 32),)),
        "segment": jax.vmap(lambda own: jnp.searchsorted(jnp.cumsum(ragged(own, IMAGES, GROUP, GROUP - TOK_DEV // 2, 2)), jnp.arange(GROUP), side="right"))(jax.random.split(streams_of[7], N_DP)).reshape((N_DP, GROUP)).astype(jnp.int32),
        "key_valid": plant((jax.random.randint(streams_of[8], (N_DP, GROUP), 0, 8) < 7).astype(jnp.int32), jax.random.fold_in(streams_of[8], 1), 0, 1),
        "noise_level": plant(jax.random.randint(streams_of[9], (N_DP, IMAGES), 0, LEVELS), jax.random.fold_in(streams_of[9], 1), 0, LEVELS - 1).astype(jnp.int32),
        "cotangent": bell_draw(streams_of[10], (N_DP, GROUP, D), 1.0, 6.0, ((0, 8), (1, 4))),
    }


EPS = 1e-06
NEG = -1e+30
HIGH = lax.Precision.HIGHEST

@jax.custom_vjp
def low(v):
    return lax.optimization_barrier(v.astype(jnp.bfloat16)).astype(jnp.float32)

@jax.custom_vjp
def low_back(v):
    return v

def low_keep(v):
    return (low(v), None)

def low_pass(kept, grad):
    return (grad,)

def back_keep(v):
    return (v, None)

def back_low(kept, grad):
    return (low(grad),)
low.defvjp(low_keep, low_pass)
low_back.defvjp(back_keep, back_low)

def norm_mod(value, shift, scale):
    normed = value * lax.rsqrt(lax.optimization_barrier(jnp.mean(value * value, axis=-1, keepdims=True)) + EPS)
    return normed * (1.0 + scale) + shift

def attend(queries, key_rows, val_rows, seg_group, valid_group):
    count = queries.shape[0]
    q_heads = queries.reshape(count, HEADS, HEAD_DIM)
    k_heads = key_rows.reshape(count, HEADS, HEAD_DIM)
    v_heads = val_rows.reshape(count, HEADS, HEAD_DIM)
    positions = jnp.arange(count, dtype=jnp.int32)
    block = math.gcd(count, 512)
    factor = 1.0 / math.sqrt(HEAD_DIM)

    def one_block(start):
        q_block = lax.dynamic_slice_in_dim(q_heads, start, block, 0)
        seg_block = lax.dynamic_slice_in_dim(seg_group, start, block, 0)
        q_pos = start + jnp.arange(block, dtype=jnp.int32)
        scores = jnp.einsum('qhd,khd->hqk', q_block, k_heads, precision=HIGH) * factor
        scores = low_back(scores)
        allowed = (seg_block[:, None] == seg_group[None, :]) & ((valid_group[None, :] == 1) | (q_pos[:, None] == positions[None, :]))
        masked = jnp.where(allowed[None], scores, NEG)
        top = lax.optimization_barrier(jnp.max(masked, axis=-1, keepdims=True))
        expo = jnp.where(allowed[None], jnp.exp(masked - top), 0.0)
        prob = expo / lax.optimization_barrier(jnp.sum(expo, axis=-1, keepdims=True))
        mixed = jnp.einsum('hqk,khd->qhd', low(prob), v_heads, precision=HIGH)
        return mixed.reshape(block, HEADS * HEAD_DIM)
    starts = jnp.arange(0, count, block, dtype=jnp.int32)
    outs = lax.map(jax.checkpoint(one_block), starts)
    return outs.reshape(count, HEADS * HEAD_DIM)

def group_forward(x_group, seg_group, valid_group, mod_group, qkv_w, out_w, up_w, down_w):
    tok_mod = mod_group[seg_group]
    shift1, scale1, gate1, shift2, scale2, gate2 = jnp.split(tok_mod, 6, axis=-1)
    first = low(norm_mod(x_group, shift1, scale1))
    qkv = low_back(low(jnp.dot(first, qkv_w, precision=HIGH)))
    queries, key_rows, val_rows = jnp.split(qkv, 3, axis=-1)
    mixed = low_back(low(attend(queries, key_rows, val_rows, seg_group, valid_group)))
    attn = low_back(jnp.dot(mixed, out_w, precision=HIGH))
    x_mid = x_group + gate1 * attn
    second = low(norm_mod(x_mid, shift2, scale2))
    hidden_pre = low_back(jnp.dot(second, up_w, precision=HIGH))
    hidden = low(jax.nn.gelu(hidden_pre))
    branch = low_back(lax.dot_general(hidden, down_w, (((1,), (1,)), ((), ())), precision=HIGH))
    return x_mid + gate2 * branch

def reference(tokens, noise_table, mod_weight, qkv_weight, out_weight, up_weight, down_weight, segment, key_valid, noise_level, cotangent):

    def forward(x_all, table, mod_w, qkv_w, out_w, up_w, down_w):
        cond = table[noise_level]
        mods = jnp.einsum('gid,de->gie', cond, mod_w, precision=HIGH)

        def step(carry, item):
            x_group, seg_group, valid_group, mod_group = item
            result = jax.checkpoint(group_forward)(x_group, seg_group, valid_group, mod_group, qkv_w, out_w, up_w, down_w)
            return (carry, result)
        _, outs = lax.scan(step, jnp.zeros((), jnp.float32), (x_all, segment, key_valid, mods))
        return outs
    primals = (tokens.astype(jnp.float32), noise_table.astype(jnp.float32), mod_weight.astype(jnp.float32), qkv_weight.astype(jnp.float32), out_weight.astype(jnp.float32), up_weight.astype(jnp.float32), down_weight.astype(jnp.float32))
    outs, pullback = jax.vjp(forward, *primals)
    grads = pullback(cotangent.astype(jnp.float32))
    return (outs.astype(jnp.bfloat16), grads[0], grads[1], grads[2], grads[3], grads[4], grads[5], grads[6])
```

```python
import functools
import math

import jax
import jax.numpy as jnp
from jax import lax
from jax.experimental import pallas as pl
from jax.experimental.pallas import tpu as pltpu
from jax.sharding import Mesh
from jax.sharding import PartitionSpec as P

HEADS = 16
HEAD_DIM = 128
EPS = 1e-06
NEG = -1e30
HIGH = lax.Precision.HIGHEST
PLANE = 8
BF = jnp.bfloat16
F32 = jnp.float32
ALL = ("z", "y", "blk")
MIB = 1 << 20


def peer(k):
    y, b = lax.axis_index("y"), lax.axis_index("blk")
    high, low = lax.div(b, 2), lax.rem(b, 2)
    if k & 4:
        y = 1 - y
    if k & 2:
        high = 1 - high
    if k & 1:
        low = 1 - low
    return {"y": y, "blk": high * 2 + low}


def place(k):
    where = peer(k)
    return where["y"] * 4 + where["blk"]


def greet(peers):
    barrier = pltpu.get_barrier_semaphore()
    for k in peers:
        pl.semaphore_signal(
            barrier, inc=1, device_id=peer(k), device_id_type=pl.DeviceIdType.MESH
        )
    pl.semaphore_wait(barrier, len(peers))


def send(src, dst, ssem, rsem, k):
    copy = pltpu.make_async_remote_copy(
        src_ref=src,
        dst_ref=dst,
        send_sem=ssem,
        recv_sem=rsem,
        device_id=peer(k),
        device_id_type=pl.DeviceIdType.MESH,
    )
    copy.start()
    return copy


def call(kernel, ins, outs, scratch, ident, vmem=16, moved=0):
    return pl.pallas_call(
        kernel,
        out_shape=outs,
        in_specs=[pl.BlockSpec(memory_space=pl.ANY)] * len(ins),
        out_specs=jax.tree.map(lambda _: pl.BlockSpec(memory_space=pl.ANY), outs),
        scratch_shapes=scratch,
        compiler_params=pltpu.CompilerParams(
            collective_id=ident, has_side_effects=True, vmem_limit_bytes=vmem * MIB
        ),
        cost_estimate=pl.CostEstimate(flops=0, bytes_accessed=moved, transcendentals=0),
    )(*ins)


def gather_kernel(x, o, lsem, ssem, rsem):
    rows = x.shape[0]
    half = rows // 2
    top, bot = pl.ds(0, half), pl.ds(half, half)
    greet((1, 2, 4))
    own = pltpu.make_async_copy(x, o.at[0], lsem)
    own.start()
    go = lambda i, src, dst, k: send(src, dst, ssem.at[i], rsem.at[i], k)
    x_bot = go(0, x.at[bot], o.at[2, bot], 2)
    y_top = go(1, x.at[top], o.at[4, top], 4)
    x_top = go(2, x.at[top], o.at[2, top], 2)
    y_bot = go(3, x.at[bot], o.at[4, bot], 4)
    sib = go(4, x, o.at[1], 1)
    x_bot.wait_recv()
    dy = go(5, o.at[2, bot], o.at[6, bot], 4)
    c0 = go(6, o.at[2, bot], o.at[3, bot], 1)
    y_top.wait_recv()
    dx = go(7, o.at[4, top], o.at[6, top], 2)
    c1 = go(8, o.at[4, top], o.at[5, top], 1)
    x_top.wait_recv()
    c2 = go(9, o.at[2, top], o.at[3, top], 1)
    y_bot.wait_recv()
    c3 = go(10, o.at[4, bot], o.at[5, bot], 1)
    dx.wait_recv()
    c4 = go(11, o.at[6, top], o.at[7, top], 1)
    dy.wait_recv()
    c5 = go(12, o.at[6, bot], o.at[7, bot], 1)
    for copy in (sib, c0, c1, c2, c3, c4, c5):
        copy.wait_recv()
    for copy in (x_bot, y_top, x_top, y_bot, sib, dy, c0, dx, c1, c2, c3, c4, c5):
        copy.wait_send()
    own.wait()


def plane_gather(x, ident):
    out = jax.ShapeDtypeStruct((PLANE,) + x.shape, x.dtype)
    dma = pltpu.SemaphoreType.DMA
    return call(
        gather_kernel, (x,), out, [dma, dma((13,)), dma((13,))], ident, 4, 8 * x.size * 16
    )


def rows_loop(rows, body):
    step = 16

    def one(i, carry):
        body(pl.ds(pl.multiple_of(i * step, step), step))
        return carry

    lax.fori_loop(0, rows // step, one, 0)


def scatter_kernel(p, o, pv, rc, q6, q2, q4, d6, rx, ry, ov, lsem, ssem, rsem):
    rows = o.shape[0]
    half = rows // 2
    top, bot = pl.ds(0, half), pl.ds(half, half)
    greet((1, 2, 4))
    go = lambda i, src, dst, k: send(src, dst, ssem.at[i], rsem.at[i], k)
    load = [pltpu.make_async_copy(p.at[2 * i], pv.at[i], lsem.at[i]) for i in range(4)]
    c7t = go(0, p.at[7, top], rc.at[3, top], 1)
    load[3].start()
    c7b = go(1, p.at[7, bot], rc.at[3, bot], 1)
    load[1].start()
    c3 = go(2, p.at[3], rc.at[1], 1)
    load[2].start()
    c5 = go(3, p.at[5], rc.at[2], 1)
    load[0].start()
    c1 = go(4, p.at[1], rc.at[0], 1)

    def add2(dst, i, start):
        def body(r):
            s = pl.ds(pl.multiple_of(start + r.start, 16), r.size)
            dst[r, :] = (pv[i, s, :].astype(F32) + rc[i, s, :].astype(F32)).astype(BF)

        rows_loop(half, body)

    def add3(dst, i, start, more):
        def body(r):
            s = pl.ds(pl.multiple_of(start + r.start, 16), r.size)
            total = pv[i, s, :].astype(F32) + rc[i, s, :].astype(F32) + more[r, :].astype(F32)
            dst[r, :] = total.astype(BF)

        rows_loop(half, body)

    load[3].wait()
    c7t.wait_recv()
    add2(q6.at[0], 3, 0)
    s6t = go(5, q6.at[0], d6.at[0], 2)
    c7b.wait_recv()
    add2(q6.at[1], 3, half)
    s6b = go(6, q6.at[1], d6.at[1], 4)
    load[1].wait()
    c3.wait_recv()
    add2(q2.at[0], 1, 0)
    s2t = go(7, q2.at[0], rx.at[0], 2)
    load[2].wait()
    c5.wait_recv()
    add2(q4.at[1], 2, half)
    s4b = go(8, q4.at[1], ry.at[1], 4)
    s6t.wait_recv()
    add3(q4.at[0], 2, 0, d6.at[0])
    s4t = go(9, q4.at[0], ry.at[0], 4)
    s6b.wait_recv()
    add3(q2.at[1], 1, half, d6.at[1])
    s2b = go(10, q2.at[1], rx.at[1], 2)
    load[0].wait()
    c1.wait_recv()
    s2t.wait_recv()
    s4t.wait_recv()

    def finish(n, start):
        def body(r):
            s = pl.ds(pl.multiple_of(start + r.start, 16), r.size)
            total = pv[0, s, :].astype(F32) + rc[0, s, :].astype(F32)
            ov[s, :] = total + rx[n, r, :].astype(F32) + ry[n, r, :].astype(F32)

        rows_loop(half, body)

    finish(0, 0)
    out0 = pltpu.make_async_copy(ov.at[top], o.at[top], lsem.at[4])
    out0.start()
    s2b.wait_recv()
    s4b.wait_recv()
    finish(1, half)
    out1 = pltpu.make_async_copy(ov.at[bot], o.at[bot], lsem.at[5])
    out1.start()
    for copy in (c7t, c7b, c3, c5, c1, s6t, s6b, s2t, s4b, s4t, s2b):
        copy.wait_send()
    out0.wait()
    out1.wait()


def plane_scatter(p, ident):
    _, rows, width = p.shape
    half = rows // 2
    dma = pltpu.SemaphoreType.DMA
    pair = pltpu.VMEM((2, half, width), BF)
    scratch = [
        pltpu.VMEM((4, rows, width), BF),
        pltpu.VMEM((4, rows, width), BF),
        pair,
        pair,
        pair,
        pair,
        pair,
        pair,
        pltpu.VMEM((rows, width), F32),
        dma((6,)),
        dma((11,)),
        dma((11,)),
    ]
    out = jax.ShapeDtypeStruct((rows, width), F32)
    return call(scatter_kernel, (p,), out, scratch, ident, 24, 8 * p.size * 2)


def spread_kernel(plan, count, *refs):
    ins, outs = refs[:count], refs[count : 2 * count]
    lsem, ssem, rsem = refs[2 * count :]
    greet(range(1, PLANE))
    mine = place(0)
    locals_, remotes = [], []
    for n, (w, base, width, col) in enumerate(plan):
        rows = ins[w].shape[0]
        here = pl.ds(pl.multiple_of(mine * rows, 16), rows)
        for k in range(1, PLANE):
            cols = pl.ds(pl.multiple_of(base + place(k) * width, 128), width)
            remotes.append(
                send(
                    ins[w].at[:, cols],
                    outs[w].at[here, pl.ds(col, width)],
                    ssem.at[n, k],
                    rsem.at[n, k],
                    k,
                )
            )
        cols = pl.ds(pl.multiple_of(base + mine * width, 128), width)
        copy = pltpu.make_async_copy(
            ins[w].at[:, cols], outs[w].at[here, pl.ds(col, width)], lsem.at[n]
        )
        copy.start()
        locals_.append(copy)
    for copy in remotes:
        copy.wait()
    for copy in locals_:
        copy.wait()


def spread(weights, ident, blocks=1):
    plan, outs = [], []
    for i, w in enumerate(weights):
        rows, cols = w.shape
        each = cols // blocks
        for b in range(blocks):
            plan.append((i, b * each, each // PLANE, b * (each // PLANE)))
        outs.append(jax.ShapeDtypeStruct((rows * PLANE, cols // PLANE), w.dtype))
    dma = pltpu.SemaphoreType.DMA
    n = len(plan)
    return call(
        functools.partial(spread_kernel, plan, len(weights)),
        tuple(weights),
        outs,
        [dma((n,)), dma((n, PLANE)), dma((n, PLANE))],
        ident,
        4,
        sum(w.size for w in weights) * 16,
    )


def collect_kernel(plan, count, *refs):
    ins, outs = refs[:count], refs[count : 2 * count]
    lsem, ssem, rsem = refs[2 * count :]
    greet(range(1, PLANE))
    mine = place(0)
    locals_, remotes = [], []
    for n, (w, base, width, col) in enumerate(plan):
        rows = outs[w].shape[0]
        cols = pl.ds(pl.multiple_of(base + mine * width, 128), width)
        for k in range(1, PLANE):
            there = pl.ds(pl.multiple_of(place(k) * rows, 16), rows)
            remotes.append(
                send(
                    ins[w].at[there, pl.ds(col, width)],
                    outs[w].at[:, cols],
                    ssem.at[n, k],
                    rsem.at[n, k],
                    k,
                )
            )
        here = pl.ds(pl.multiple_of(mine * rows, 16), rows)
        copy = pltpu.make_async_copy(
            ins[w].at[here, pl.ds(col, width)], outs[w].at[:, cols], lsem.at[n]
        )
        copy.start()
        locals_.append(copy)
    for copy in remotes:
        copy.wait()
    for copy in locals_:
        copy.wait()


def collect(grads, ident, blocks=1):
    plan, outs = [], []
    for i, g in enumerate(grads):
        rows, cols = g.shape
        each = cols * PLANE // blocks
        for b in range(blocks):
            plan.append((i, b * each, each // PLANE, b * (each // PLANE)))
        outs.append(jax.ShapeDtypeStruct((rows // PLANE, cols * PLANE), g.dtype))
    dma = pltpu.SemaphoreType.DMA
    n = len(plan)
    return call(
        functools.partial(collect_kernel, plan, len(grads)),
        tuple(grads),
        outs,
        [dma((n,)), dma((n, PLANE)), dma((n, PLANE))],
        ident,
        4,
        sum(g.size for g in grads) * 16,
    )


def chain_gather(x, nz):
    z = lax.axis_index("z")
    right, left, rights, lefts = x, x, [], []
    for s in range(1, nz):
        right = lax.ppermute(right, "z", [(i, i + 1) for i in range(s - 1, nz - 1)])
        left = lax.ppermute(left, "z", [(i, i - 1) for i in range(1, nz - s + 1)])
        rights.append(right)
        lefts.append(left)
    out = jnp.zeros((nz,) + x.shape, x.dtype)
    out = lax.dynamic_update_index_in_dim(out, x, z, 0)
    for s in range(1, nz):
        piece = jnp.where(z >= s, rights[s - 1], lefts[nz - s - 1])
        out = lax.dynamic_update_index_in_dim(out, piece, lax.rem(z - s + nz, nz), 0)
    return out.reshape((nz * x.shape[0],) + x.shape[1:]), (rights[-1], lefts[-1])


def chain_scatter(g, nz):
    z = lax.axis_index("z")
    parts = g.reshape((nz, g.shape[0] // nz) + g.shape[1:])

    def take(t):
        t = jnp.clip(t, 0, nz - 1)
        return lax.dynamic_index_in_dim(parts, t, 0, keepdims=False).astype(F32)

    right = left = None
    for s in range(1, nz):
        to_right, to_left = take(z + nz - s), take(z - nz + s)
        if s > 1:
            to_right, to_left = to_right + right.astype(F32), to_left + left.astype(F32)
        right = lax.ppermute(to_right.astype(BF), "z", [(i, i + 1) for i in range(s)])
        left = lax.ppermute(to_left.astype(BF), "z", [(i, i - 1) for i in range(nz - s, nz)])
    return take(z) + right.astype(F32) + left.astype(F32)


def norm_mod(value, shift, scale):
    normed = value * lax.rsqrt(jnp.mean(value * value, axis=-1, keepdims=True) + EPS)
    return normed * (1.0 + scale) + shift


def dot(a, b):
    return jnp.dot(a, b, preferred_element_type=F32)


def over_rows(left, right):
    return lax.dot_general(left, right, (((0,), (0,)), ((), ())), preferred_element_type=F32)


def times_t(left, right):
    return lax.dot_general(left, right, (((1,), (1,)), ((), ())), preferred_element_type=F32)


def after(value, *others):
    return lax.optimization_barrier((value,) + others)[0]


def on_device(
    tokens,
    noise_table,
    mod_weight,
    qkv_weight,
    out_weight,
    up_weight,
    down_weight,
    segment,
    key_valid,
    noise_level,
    cotangent,
):
    rows, width = tokens.shape[1:]
    images = noise_level.shape[1]
    nz = lax.axis_size("z")
    blks = lax.axis_size("blk")
    z, y, blk = (lax.axis_index(a) for a in ALL)
    devices = nz * PLANE
    group = rows * blks
    local = HEADS // PLANE
    factor = 1.0 / math.sqrt(HEAD_DIM)

    levels = noise_level.reshape(-1)
    cond = jnp.take(noise_table, levels, axis=0)
    cols = dot(cond, mod_weight)
    planes = cols.reshape(nz, 1, 2 * images, -1)
    planes = jnp.broadcast_to(planes, (nz, PLANE) + planes.shape[2:])
    mods = lax.all_to_all(
        planes.reshape((devices,) + planes.shape[2:]), ALL, 0, 0, tiled=True
    )
    mods = mods.transpose(1, 0, 2).reshape(2, images, 6, width)
    mods = jnp.where(y == 0, mods, mods[::-1])

    both = jnp.concatenate([segment, key_valid], axis=0)
    other = lax.ppermute(both, "y", [(0, 1), (1, 0)])
    order = lambda a: jnp.stack(
        [
            lax.dynamic_index_in_dim(
                a.reshape(2, blks, rows),
                (lax.div(blk, 2) ^ (k >> 1)) * 2 + (lax.rem(blk, 2) ^ (k & 1)),
                1,
                keepdims=False,
            )
            for k in range(blks)
        ],
        axis=1,
    ).reshape(2, group)
    both, other = order(both), order(other)
    seg = jnp.stack([both[0], other[0]])
    valid = jnp.stack([both[1], other[1]])
    seg_own = seg[0, :rows]

    def pick(which):
        m = mods[:, :, which]
        s = seg[:, :, None]
        out = m[:, images - 1][:, None]
        for i in range(images - 2, -1, -1):
            out = jnp.where(s == i, m[:, i][:, None], out)
        return out

    def pick_own(which):
        m = mods[0, :, which]
        s = seg_own[:, None]
        out = m[images - 1][None]
        for i in range(images - 2, -1, -1):
            out = jnp.where(s == i, m[i][None], out)
        return out

    (qkv_part,) = spread([qkv_weight], 1, blocks=3)
    qkv_w, last = chain_gather(qkv_part, nz)
    x_all = plane_gather(after(tokens[0], qkv_part), 2).reshape(2, group, width)
    move = [(nz * k + i, i * PLANE + k) for k in range(PLANE) for i in range(nz)]
    outp = lax.ppermute(out_weight, ALL, move)
    (up_part,) = spread([after(up_weight, x_all)], 3)
    outp, up_part = lax.optimization_barrier((outp, up_part) + last)[:2]
    outp_w, _ = chain_gather(outp, nz)
    up_w, last = chain_gather(up_part, nz)
    (down_part,) = spread([after(down_weight, up_part)], 4)
    down_part = after(down_part, *last)
    down_w, _ = chain_gather(down_part, nz)
    g_all = plane_gather(after(cotangent[0], down_part), 5).reshape(2, group, width)

    x_f = x_all.astype(F32)
    first = norm_mod(x_f, pick(0), pick(1)).astype(BF).reshape(2 * group, width)
    qkv = dot(first, qkv_w).astype(BF)
    heads = qkv.reshape(2, group, 3, local, HEAD_DIM)
    q_h, k_h, v_h = heads[:, :, 0], heads[:, :, 1], heads[:, :, 2]
    eye = jnp.arange(group)[:, None] == jnp.arange(group)[None, :]
    allowed = (seg[:, :, None] == seg[:, None, :]) & ((valid[:, None, :] == 1) | eye[None])
    allowed = allowed[:, None]
    scores = jnp.einsum("gqhd,gkhd->ghqk", q_h, k_h, preferred_element_type=F32) * factor
    masked = jnp.where(allowed, scores, NEG)
    top = jnp.max(masked, axis=-1)
    expo = jnp.where(allowed, jnp.exp(masked - top[..., None]), 0.0)
    total = jnp.sum(expo, axis=-1)
    prob = expo / total[..., None]
    prob_b = prob.astype(BF)
    mixed = jnp.einsum("ghqk,gkhd->gqhd", prob_b, v_h, preferred_element_type=F32)
    mixed = mixed.astype(BF).reshape(2 * group, local * HEAD_DIM)
    part = dot(mixed, outp_w).astype(BF).reshape(PLANE, rows, width)
    attn = plane_scatter(part, 6)
    x_in = tokens[0].astype(F32)
    shift1, scale1, gate1 = pick_own(0), pick_own(1), pick_own(2)
    shift2, scale2, gate2 = pick_own(3), pick_own(4), pick_own(5)
    x_mid = x_in + gate1 * attn
    second_f, second_back = jax.vjp(norm_mod, x_mid, shift2, scale2)
    second = plane_gather(second_f.astype(BF), 7).reshape(2 * group, width)
    hidden_pre = dot(second, up_w)
    hidden_f, gelu_back = jax.vjp(jax.nn.gelu, hidden_pre)
    hidden = hidden_f.astype(BF)

    d_branch = (pick(5) * g_all.astype(F32)).astype(BF).reshape(2 * group, width)
    d_down = over_rows(d_branch, hidden).astype(BF)
    d_down = chain_scatter(d_down, nz)
    part = times_t(hidden, down_w).astype(BF).reshape(PLANE, rows, width)
    branch = plane_scatter(part, 8)
    block_out = (x_mid + gate2 * branch).astype(BF)
    grad_in = cotangent[0].astype(F32)
    d_gate2 = grad_in * branch
    d_pre = gelu_back(dot(d_branch, down_w))[0].astype(BF)
    part = times_t(d_pre, up_w).astype(BF).reshape(PLANE, rows, width)
    d_up = chain_scatter(over_rows(second, d_pre).astype(BF), nz)
    d_second = plane_scatter(part, 9)
    d_mid_norm, d_shift2, d_scale2 = second_back(d_second)
    d_mid = grad_in + d_mid_norm
    d_attn = (gate1 * d_mid).astype(BF)
    d_gate1 = d_mid * attn
    d_attn_all = plane_gather(d_attn, 10).reshape(2 * group, width)
    d_outp = chain_scatter(over_rows(mixed, d_attn_all).astype(BF), nz)
    d_mixed = times_t(d_attn_all, outp_w).astype(BF).reshape(2, group, local, HEAD_DIM)
    d_prob = jnp.einsum("gqhd,gkhd->ghqk", d_mixed, v_h, preferred_element_type=F32)
    delta = jnp.sum(prob * d_prob, axis=-1, keepdims=True)
    d_scores = (prob * (d_prob - delta)).astype(BF)
    dq = jnp.einsum("ghqk,gkhd->gqhd", d_scores, k_h, preferred_element_type=F32) * factor
    dk = jnp.einsum("ghqk,gqhd->gkhd", d_scores, q_h, preferred_element_type=F32) * factor
    dv = jnp.einsum("ghqk,gqhd->gkhd", prob_b, d_mixed, preferred_element_type=F32)
    d_qkv = jnp.stack([dq, dk, dv], axis=2).astype(BF).reshape(2 * group, -1)
    part = times_t(d_qkv, qkv_w).astype(BF).reshape(PLANE, rows, width)
    d_qkv_w = chain_scatter(over_rows(first, d_qkv).astype(BF), nz)
    d_first = plane_scatter(part, 11)
    _, first_back = jax.vjp(norm_mod, x_in, shift1, scale1)
    d_in_norm, d_shift1, d_scale1 = first_back(d_first)
    grad_tokens = d_mid + d_in_norm

    tok_grads = jnp.concatenate([d_shift1, d_scale1, d_gate1, d_shift2, d_scale2, d_gate2], axis=1)
    picker = (seg_own[:, None] == jnp.arange(images, dtype=jnp.int32)[None, :]).astype(F32)
    image_grads = lax.dot_general(picker, tok_grads, (((0,), (0,)), ((), ())), precision=HIGH)
    sent = image_grads.reshape(images, devices, -1).transpose(1, 0, 2)
    got = lax.all_to_all(sent, ALL, 0, 0, tiled=True)
    mod_grads = got.reshape(2 * nz, blks, images, -1).sum(axis=1).reshape(2 * nz * images, -1)
    grad_mod = lax.dot_general(
        cond.astype(F32), mod_grads, (((0,), (0,)), ((), ())), precision=HIGH
    )
    cond_part = lax.dot_general(
        mod_grads, mod_weight.astype(F32), (((1,), (1,)), ((), ())), precision=HIGH
    )
    count = cond_part.shape[0]
    sent = cond_part.reshape(count, devices, -1).transpose(1, 0, 2)
    mine = lax.all_to_all(sent, ALL, 0, 0, tiled=True).sum(axis=0)
    sent = jnp.broadcast_to(mine[None], (devices,) + mine.shape)
    cond_grads = lax.all_to_all(sent, ALL, 0, 0, tiled=True)
    cond_grads = cond_grads.transpose(1, 0, 2).reshape(count, width)
    grad_table = jax.ops.segment_sum(cond_grads, levels, num_segments=noise_table.shape[0])

    d_up, d_down = collect([d_up.astype(BF), d_down.astype(BF)], 12)
    (d_qkv_w,) = collect([d_qkv_w.astype(BF)], 13, blocks=3)
    d_outp = lax.ppermute(d_outp, ALL, [(b, a) for a, b in move])
    return (
        block_out[None],
        grad_tokens[None],
        grad_table,
        grad_mod,
        d_qkv_w.astype(F32),
        d_outp,
        d_up.astype(F32),
        d_down.astype(F32),
    )


def solution(mesh):
    groups, blks = mesh.shape["dp"], mesh.shape["blk"]
    planes = Mesh(mesh.devices.reshape(groups // 2, 2, blks), ALL)
    dp = ("z", "y")
    whole = ("z", "y", "blk")
    placed = (
        P(dp, "blk", None),
        P(),
        P(None, whole),
        P(whole, None),
        P(whole, None),
        P(whole, None),
        P(whole, None),
        P(dp, None),
        P(dp, None),
        P(),
        P(dp, "blk", None),
    )
    return jax.shard_map(
        on_device,
        mesh=planes,
        in_specs=placed,
        out_specs=(
            P(dp, "blk", None),
            P(dp, "blk", None),
            P(),
            P(None, whole),
            P(whole, None),
            P(whole, None),
            P(whole, None),
            P(whole, None),
        ),
        check_vma=False,
    )
```

```python
import functools
import math

import jax
import jax.numpy as jnp
from jax import lax
from jax.experimental import pallas as pl
from jax.experimental.pallas import tpu as pltpu
from jax.sharding import Mesh
from jax.sharding import PartitionSpec as P

HEADS = 16
HEAD_DIM = 128
EPS = 1e-06
NEG = -1e30
HIGH = lax.Precision.HIGHEST
PLANE = 8
BF = jnp.bfloat16
F32 = jnp.float32
ALL = ("z", "y", "blk")
MIB = 1 << 20


def peer(k):
    y, b = lax.axis_index("y"), lax.axis_index("blk")
    high, low = lax.div(b, 2), lax.rem(b, 2)
    if k & 4:
        y = 1 - y
    if k & 2:
        high = 1 - high
    if k & 1:
        low = 1 - low
    return {"y": y, "blk": high * 2 + low}


def place(k):
    where = peer(k)
    return where["y"] * 4 + where["blk"]


def greet(peers):
    barrier = pltpu.get_barrier_semaphore()
    for k in peers:
        pl.semaphore_signal(
            barrier, inc=1, device_id=peer(k), device_id_type=pl.DeviceIdType.MESH
        )
    pl.semaphore_wait(barrier, len(peers))


def send(src, dst, ssem, rsem, k):
    copy = pltpu.make_async_remote_copy(
        src_ref=src,
        dst_ref=dst,
        send_sem=ssem,
        recv_sem=rsem,
        device_id=peer(k),
        device_id_type=pl.DeviceIdType.MESH,
    )
    copy.start()
    return copy


def call(kernel, ins, outs, scratch, ident, vmem=16, micros=10):
    return pl.pallas_call(
        kernel,
        out_shape=outs,
        in_specs=[pl.BlockSpec(memory_space=pl.ANY)] * len(ins),
        out_specs=jax.tree.map(lambda _: pl.BlockSpec(memory_space=pl.ANY), outs),
        scratch_shapes=scratch,
        compiler_params=pltpu.CompilerParams(
            collective_id=ident, has_side_effects=True, vmem_limit_bytes=vmem * MIB
        ),
        cost_estimate=pl.CostEstimate(
            flops=0, bytes_accessed=int(micros * 3.6e6), transcendentals=0
        ),
    )(*ins)


def gather_kernel(x, o, xv, lsem, ssem, rsem):
    rows = x.shape[0]
    half = rows // 2
    top, bot = pl.ds(0, half), pl.ds(half, half)
    load = pltpu.make_async_copy(x, xv, lsem.at[0])
    load.start()
    greet((1, 2, 4))
    load.wait()
    go = lambda i, src, dst, k: send(src, dst, ssem.at[i], rsem.at[i], k)
    x_bot = go(0, xv.at[bot], o.at[2, bot], 2)
    y_top = go(1, xv.at[top], o.at[4, top], 4)
    x_top = go(2, xv.at[top], o.at[2, top], 2)
    y_bot = go(3, xv.at[bot], o.at[4, bot], 4)
    sib = go(4, xv, o.at[1], 1)
    own = pltpu.make_async_copy(xv, o.at[0], lsem.at[1])
    own.start()
    x_bot.wait_recv()
    dy = go(5, o.at[2, bot], o.at[6, bot], 4)
    c0 = go(6, o.at[2, bot], o.at[3, bot], 1)
    y_top.wait_recv()
    dx = go(7, o.at[4, top], o.at[6, top], 2)
    c1 = go(8, o.at[4, top], o.at[5, top], 1)
    x_top.wait_recv()
    c2 = go(9, o.at[2, top], o.at[3, top], 1)
    y_bot.wait_recv()
    c3 = go(10, o.at[4, bot], o.at[5, bot], 1)
    dx.wait_recv()
    c4 = go(11, o.at[6, top], o.at[7, top], 1)
    dy.wait_recv()
    c5 = go(12, o.at[6, bot], o.at[7, bot], 1)
    for copy in (sib, c0, c1, c2, c3, c4, c5):
        copy.wait_recv()
    for copy in (x_bot, y_top, x_top, y_bot, sib, dy, c0, dx, c1, c2, c3, c4, c5):
        copy.wait_send()
    own.wait()


def plane_gather(x, ident):
    out = jax.ShapeDtypeStruct((PLANE,) + x.shape, x.dtype)
    dma = pltpu.SemaphoreType.DMA
    scratch = [pltpu.VMEM(x.shape, x.dtype), dma((2,)), dma((13,)), dma((13,))]
    return call(gather_kernel, (x,), out, scratch, ident, 8, 30)


def rows_loop(rows, body):
    step = 16

    def one(i, carry):
        body(pl.ds(pl.multiple_of(i * step, step), step))
        return carry

    lax.fori_loop(0, rows // step, one, 0)


def scatter_kernel(p, o, pv, rc, q6, q2, q4, d6, rx, ry, ov, lsem, ssem, rsem):
    rows = o.shape[0]
    half = rows // 2
    top, bot = pl.ds(0, half), pl.ds(half, half)
    greet((1, 2, 4))
    go = lambda i, src, dst, k: send(src, dst, ssem.at[i], rsem.at[i], k)
    load = [pltpu.make_async_copy(p.at[2 * i], pv.at[i], lsem.at[i]) for i in range(4)]
    c7t = go(0, p.at[7, top], rc.at[3, top], 1)
    load[3].start()
    c7b = go(1, p.at[7, bot], rc.at[3, bot], 1)
    load[1].start()
    c3 = go(2, p.at[3], rc.at[1], 1)
    load[2].start()
    c5 = go(3, p.at[5], rc.at[2], 1)
    load[0].start()
    c1 = go(4, p.at[1], rc.at[0], 1)

    def add2(dst, i, start):
        def body(r):
            s = pl.ds(pl.multiple_of(start + r.start, 16), r.size)
            dst[r, :] = (pv[i, s, :].astype(F32) + rc[i, s, :].astype(F32)).astype(BF)

        rows_loop(half, body)

    def add3(dst, i, start, more):
        def body(r):
            s = pl.ds(pl.multiple_of(start + r.start, 16), r.size)
            total = pv[i, s, :].astype(F32) + rc[i, s, :].astype(F32) + more[r, :].astype(F32)
            dst[r, :] = total.astype(BF)

        rows_loop(half, body)

    load[3].wait()
    c7t.wait_recv()
    add2(q6.at[0], 3, 0)
    s6t = go(5, q6.at[0], d6.at[0], 2)
    c7b.wait_recv()
    add2(q6.at[1], 3, half)
    s6b = go(6, q6.at[1], d6.at[1], 4)
    load[1].wait()
    c3.wait_recv()
    add2(q2.at[0], 1, 0)
    s2t = go(7, q2.at[0], rx.at[0], 2)
    load[2].wait()
    c5.wait_recv()
    add2(q4.at[1], 2, half)
    s4b = go(8, q4.at[1], ry.at[1], 4)
    s6t.wait_recv()
    add3(q4.at[0], 2, 0, d6.at[0])
    s4t = go(9, q4.at[0], ry.at[0], 4)
    s6b.wait_recv()
    add3(q2.at[1], 1, half, d6.at[1])
    s2b = go(10, q2.at[1], rx.at[1], 2)
    load[0].wait()
    c1.wait_recv()
    s2t.wait_recv()
    s4t.wait_recv()

    def finish(n, start):
        def body(r):
            s = pl.ds(pl.multiple_of(start + r.start, 16), r.size)
            total = pv[0, s, :].astype(F32) + rc[0, s, :].astype(F32)
            ov[s, :] = total + rx[n, r, :].astype(F32) + ry[n, r, :].astype(F32)

        rows_loop(half, body)

    finish(0, 0)
    out0 = pltpu.make_async_copy(ov.at[top], o.at[top], lsem.at[4])
    out0.start()
    s2b.wait_recv()
    s4b.wait_recv()
    finish(1, half)
    out1 = pltpu.make_async_copy(ov.at[bot], o.at[bot], lsem.at[5])
    out1.start()
    for copy in (c7t, c7b, c3, c5, c1, s6t, s6b, s2t, s4b, s4t, s2b):
        copy.wait_send()
    out0.wait()
    out1.wait()


def plane_scatter(p, ident):
    _, rows, width = p.shape
    half = rows // 2
    dma = pltpu.SemaphoreType.DMA
    pair = pltpu.VMEM((2, half, width), BF)
    scratch = [
        pltpu.VMEM((4, rows, width), BF),
        pltpu.VMEM((4, rows, width), BF),
        pair,
        pair,
        pair,
        pair,
        pair,
        pair,
        pltpu.VMEM((rows, width), F32),
        dma((6,)),
        dma((11,)),
        dma((11,)),
    ]
    out = jax.ShapeDtypeStruct((rows, width), F32)
    return call(scatter_kernel, (p,), out, scratch, ident, 24, 31)


def cut(weights, blocks):
    plan = []
    for i, cols in enumerate(weights):
        each = cols // blocks
        for b in range(blocks):
            plan.append((i, b * each, each // PLANE, b * (each // PLANE)))
    return plan


def spread_kernel(plan, count, *refs):
    ins, outs, held = refs[:count], refs[count : 2 * count], refs[2 * count : 3 * count]
    lsem, ssem, rsem = refs[3 * count :]
    loads = [pltpu.make_async_copy(a, v, lsem.at[i]) for i, (a, v) in enumerate(zip(ins, held))]
    for copy in loads:
        copy.start()
    greet(range(1, PLANE))
    mine = place(0)
    remotes = []
    for w, load in enumerate(loads):
        load.wait()
        rows = ins[w].shape[0]
        here = pl.ds(pl.multiple_of(mine * rows, 16), rows)
        for n, (i, base, width, col) in enumerate(plan):
            if i != w:
                continue
            for k in (6, 7, 2, 3, 4, 5, 1):
                cols = pl.ds(pl.multiple_of(base + place(k) * width, 128), width)
                remotes.append(
                    send(
                        held[w].at[:, cols],
                        outs[w].at[here, pl.ds(col, width)],
                        ssem.at[n, k],
                        rsem.at[n, k],
                        k,
                    )
                )
            cols = pl.ds(pl.multiple_of(base + mine * width, 128), width)
            copy = pltpu.make_async_copy(
                held[w].at[:, cols], outs[w].at[here, pl.ds(col, width)], ssem.at[n, 0]
            )
            copy.start()
            remotes.append(copy)
    for copy in remotes:
        copy.wait()


def spread(weights, ident, blocks=1):
    plan = cut([w.shape[1] for w in weights], blocks)
    outs = [
        jax.ShapeDtypeStruct((w.shape[0] * PLANE, w.shape[1] // PLANE), w.dtype) for w in weights
    ]
    dma = pltpu.SemaphoreType.DMA
    n = len(plan)
    scratch = [pltpu.VMEM(w.shape, w.dtype) for w in weights]
    return call(
        functools.partial(spread_kernel, plan, len(weights)),
        tuple(weights),
        outs,
        scratch + [dma((len(weights),)), dma((n, PLANE)), dma((n, PLANE))],
        ident,
        8,
        sum(w.size for w in weights) / 3e4,
    )


def collect_kernel(plan, count, *refs):
    ins, outs, held = refs[:count], refs[count : 2 * count], refs[2 * count : 3 * count]
    lsem, ssem, rsem = refs[3 * count :]
    loads = [pltpu.make_async_copy(a, v, lsem.at[i]) for i, (a, v) in enumerate(zip(ins, held))]
    for copy in loads:
        copy.start()
    greet(range(1, PLANE))
    mine = place(0)
    remotes = []
    for w, load in enumerate(loads):
        load.wait()
        rows = outs[w].shape[0]
        for n, (i, base, width, col) in enumerate(plan):
            if i != w:
                continue
            cols = pl.ds(pl.multiple_of(base + mine * width, 128), width)
            for k in (6, 7, 2, 3, 4, 5, 1):
                there = pl.ds(pl.multiple_of(place(k) * rows, 16), rows)
                remotes.append(
                    send(
                        held[w].at[there, pl.ds(col, width)],
                        outs[w].at[:, cols],
                        ssem.at[n, k],
                        rsem.at[n, k],
                        k,
                    )
                )
            here = pl.ds(pl.multiple_of(mine * rows, 16), rows)
            copy = pltpu.make_async_copy(
                held[w].at[here, pl.ds(col, width)], outs[w].at[:, cols], ssem.at[n, 0]
            )
            copy.start()
            remotes.append(copy)
    for copy in remotes:
        copy.wait()


def collect(grads, ident, blocks=1):
    plan = cut([g.shape[1] * PLANE for g in grads], blocks)
    outs = [
        jax.ShapeDtypeStruct((g.shape[0] // PLANE, g.shape[1] * PLANE), g.dtype) for g in grads
    ]
    dma = pltpu.SemaphoreType.DMA
    n = len(plan)
    scratch = [pltpu.VMEM(g.shape, g.dtype) for g in grads]
    return call(
        functools.partial(collect_kernel, plan, len(grads)),
        tuple(grads),
        outs,
        scratch + [dma((len(grads),)), dma((n, PLANE)), dma((n, PLANE))],
        ident,
        8,
        sum(g.size for g in grads) / 3e4,
    )


def flat_place():
    return lax.axis_index("z") * PLANE + lax.axis_index("y") * 4 + lax.axis_index("blk")


def flat_id(d):
    return {"z": lax.div(d, PLANE), "y": lax.rem(lax.div(d, 4), 2), "blk": lax.rem(d, 4)}


def greet_all(count):
    barrier = pltpu.get_barrier_semaphore()
    me = flat_place()

    def one(i, carry):
        pl.semaphore_signal(
            barrier,
            inc=1,
            device_id=flat_id(lax.rem(me + i, count)),
            device_id_type=pl.DeviceIdType.MESH,
        )
        return carry

    lax.fori_loop(1, count, one, 0)
    pl.semaphore_wait(barrier, count - 1)


def to_all(count, source, target, ssem, rsem):
    me = flat_place()

    def copy(i):
        d = lax.rem(me + i, count)
        return pltpu.make_async_remote_copy(
            src_ref=source(d),
            dst_ref=target.at[me],
            send_sem=ssem.at[i],
            recv_sem=rsem.at[i],
            device_id=flat_id(d),
            device_id_type=pl.DeviceIdType.MESH,
        )

    def begin(i, carry):
        copy(i).start()
        return carry

    def finish(i, carry):
        copy(i).wait()
        return carry

    lax.fori_loop(1, count, begin, 0)
    target[me] = source(me)[...]
    lax.fori_loop(1, count, finish, 0)


def exchange_kernel(count, x, o, ssem, rsem):
    greet_all(count)
    to_all(count, lambda d: x.at[d], o, ssem, rsem)


def small_call(kernel, ins, outs, scratch, ident, micros):
    vmem = pl.BlockSpec(memory_space=pltpu.VMEM)
    return pl.pallas_call(
        kernel,
        out_shape=outs,
        in_specs=[vmem] * len(ins),
        out_specs=jax.tree.map(lambda _: vmem, outs),
        scratch_shapes=scratch,
        compiler_params=pltpu.CompilerParams(
            collective_id=ident, has_side_effects=True, vmem_limit_bytes=32 * MIB
        ),
        cost_estimate=pl.CostEstimate(
            flops=0, bytes_accessed=int(micros * 3.6e6), transcendentals=0
        ),
    )(*ins)


def exchange(x, ident):
    dma = pltpu.SemaphoreType.DMA((x.shape[0],))
    return small_call(
        functools.partial(exchange_kernel, x.shape[0]),
        (x,),
        jax.ShapeDtypeStruct(x.shape, x.dtype),
        [dma, dma],
        ident,
        8,
    )


def mods_back_kernel(count, x, w, o, t, got, part, mine, s0, r0, s1, r1, s2, r2):
    greet_all(count)
    to_all(count, lambda d: x.at[d], got, s0, r0)
    groups = o.shape[0]
    for g in range(groups):
        o[g] = got[4 * g] + got[4 * g + 1] + got[4 * g + 2] + got[4 * g + 3]
    own = o[...].reshape(groups * 8, o.shape[2])
    high = own.astype(BF)
    rest = own - high.astype(F32)
    low = rest.astype(BF)
    quarter = w.shape[0] // 4
    for q in range(4):
        piece = w[q * quarter : (q + 1) * quarter, :]
        product = times_t(high, piece) + times_t(low, piece)
        for g in range(groups):
            part[4 * g + q] = product[8 * g : 8 * g + 8]
    to_all(count, lambda d: part.at[d], mine, s1, r1)

    def add(i, total):
        return total + mine[i]

    part[flat_place()] = lax.fori_loop(0, count, add, jnp.zeros(mine.shape[1:], F32))
    to_all(count, lambda d: part.at[flat_place()], t, s2, r2)


def mods_back(x, w, ident):
    count, eight, cols = x.shape
    width = w.shape[0]
    dma = pltpu.SemaphoreType.DMA((count,))
    pieces = jax.ShapeDtypeStruct((count, eight, width // 4), F32)
    return small_call(
        functools.partial(mods_back_kernel, count),
        (x, w),
        (jax.ShapeDtypeStruct((count // 4, eight, cols), F32), pieces),
        [pltpu.VMEM(x.shape, F32), pltpu.VMEM(pieces.shape, F32), pltpu.VMEM(pieces.shape, F32)]
        + [dma] * 6,
        ident,
        20,
    )


def swap(x, k):
    devices = PLANE * lax.axis_size("z")
    return lax.ppermute(x, ALL, [(i, i ^ k) for i in range(devices)])


def quiet_gather(x):
    even = jnp.stack([x] + [swap(x, k) for k in (2, 4, 6)])
    return jnp.stack([even, swap(even, 1)], axis=1).reshape((PLANE,) + x.shape)


def quiet_scatter(p):
    pairs = p.reshape((4, 2) + p.shape[1:])
    here, there = pairs[:, 0], pairs[:, 1]
    q = (here.astype(F32) + swap(there, 1).astype(F32)).astype(BF)
    x, y, xy = swap(q[1], 2), swap(q[2], 4), swap(q[3], 6)
    return q[0].astype(F32) + x.astype(F32) + y.astype(F32) + xy.astype(F32)


def z_gather(x):
    return lax.all_gather(x, "z", axis=0, tiled=True)


def z_scatter(g):
    return lax.psum_scatter(g, "z", scatter_dimension=0, tiled=True)


def norm_mod(value, shift, scale):
    normed = value * lax.rsqrt(jnp.mean(value * value, axis=-1, keepdims=True) + EPS)
    return normed * (1.0 + scale) + shift


def dot(a, b):
    return jnp.dot(a, b, preferred_element_type=F32)


def over_rows(left, right):
    return lax.dot_general(left, right, (((0,), (0,)), ((), ())), preferred_element_type=F32)


def times_t(left, right):
    return lax.dot_general(left, right, (((1,), (1,)), ((), ())), preferred_element_type=F32)


def softmax_rows(q, k, bias, factor):
    scores = times_t(q, k) * factor + bias.astype(F32)
    expo = jnp.exp(scores - jnp.max(scores, axis=-1, keepdims=True))
    return expo / jnp.sum(expo, axis=-1, keepdims=True)


def row_blocks(count):
    step = math.gcd(count, 256)
    return [slice(i, i + step) for i in range(0, count, step)]


def attend_kernel(factor, qkv, bias, o):
    n = o.shape[1]
    for c in range(0, n, HEAD_DIM):
        k = qkv[:, n + c : n + c + HEAD_DIM]
        v = qkv[:, 2 * n + c : 2 * n + c + HEAD_DIM]
        for r in row_blocks(o.shape[0]):
            prob = softmax_rows(qkv[r, c : c + HEAD_DIM], k, bias[0, r, :], factor)
            o[r, c : c + HEAD_DIM] = dot(prob.astype(BF), v).astype(BF)


def attend_back_kernel(factor, qkv, bias, d_o, d_qkv):
    n = d_o.shape[1]
    for c in range(0, n, HEAD_DIM):
        k = qkv[:, n + c : n + c + HEAD_DIM]
        v = qkv[:, 2 * n + c : 2 * n + c + HEAD_DIM]
        dk = dv = 0.0
        for r in row_blocks(d_o.shape[0]):
            q = qkv[r, c : c + HEAD_DIM]
            out = d_o[r, c : c + HEAD_DIM]
            prob = softmax_rows(q, k, bias[0, r, :], factor)
            d_prob = times_t(out, v)
            delta = jnp.sum(prob * d_prob, axis=-1, keepdims=True)
            d_scores = (prob * (d_prob - delta)).astype(BF)
            d_qkv[r, c : c + HEAD_DIM] = (dot(d_scores, k) * factor).astype(BF)
            dk = dk + over_rows(d_scores, q)
            dv = dv + over_rows(prob.astype(BF), out)
        d_qkv[:, n + c : n + c + HEAD_DIM] = (dk * factor).astype(BF)
        d_qkv[:, 2 * n + c : 2 * n + c + HEAD_DIM] = dv.astype(BF)


def per_group(kernel, ins, bias, columns, group, flops):
    block = lambda c: pl.BlockSpec((group, c), lambda i: (i, 0))
    return pl.pallas_call(
        kernel,
        grid=(bias.shape[0],),
        out_shape=jax.ShapeDtypeStruct((bias.shape[0] * group, columns), BF),
        in_specs=[block(ins[0].shape[1]), pl.BlockSpec((1, group, group), lambda i: (i, 0, 0))]
        + [block(a.shape[1]) for a in ins[1:]],
        out_specs=block(columns),
        compiler_params=pltpu.CompilerParams(vmem_limit_bytes=48 * MIB),
        cost_estimate=pl.CostEstimate(flops=flops, bytes_accessed=0, transcendentals=0),
    )(ins[0], bias, *ins[1:])


def after(value, *others):
    return lax.optimization_barrier((value,) + others)[0]


def on_device(
    tokens,
    noise_table,
    mod_weight,
    qkv_weight,
    out_weight,
    up_weight,
    down_weight,
    segment,
    key_valid,
    noise_level,
    cotangent,
):
    rows, width = tokens.shape[1:]
    images = noise_level.shape[1]
    nz = lax.axis_size("z")
    blks = lax.axis_size("blk")
    z, y, blk = (lax.axis_index(a) for a in ALL)
    devices = nz * PLANE
    group = rows * blks
    local = HEADS // PLANE
    factor = 1.0 / math.sqrt(HEAD_DIM)

    levels = noise_level.reshape(-1)
    cond = jnp.take(noise_table, levels, axis=0)
    cols = dot(cond, mod_weight).reshape(2 * nz, 1, images, -1)
    sent = jnp.broadcast_to(cols, (2 * nz, blks) + cols.shape[2:])
    sent = jnp.pad(sent.reshape((devices,) + cols.shape[2:]), ((0, 0), (0, 8 - images), (0, 0)))

    mods = exchange(sent, 14)[:, :images]

    (qkv_part,) = spread([after(qkv_weight, mods)], 1, blocks=3)
    mods = mods.transpose(1, 0, 2).reshape(images, 6, width)
    qkv_w = z_gather(qkv_part)
    move = [(nz * k + i, i * PLANE + k) for k in range(PLANE) for i in range(nz)]
    outp = lax.ppermute(after(out_weight, qkv_part), ALL, move)

    both = jnp.concatenate([segment, key_valid], axis=0)
    other = lax.ppermute(both, "y", [(0, 1), (1, 0)])
    order = lambda a: jnp.stack(
        [
            lax.dynamic_index_in_dim(
                a.reshape(2, blks, rows),
                (lax.div(blk, 2) ^ (k >> 1)) * 2 + (lax.rem(blk, 2) ^ (k & 1)),
                1,
                keepdims=False,
            )
            for k in range(blks)
        ],
        axis=1,
    ).reshape(2, group)
    both, other = order(both), order(other)
    seg = jnp.stack([both[0], other[0]])
    valid = jnp.stack([both[1], other[1]])
    seg_own = seg[0, :rows]
    eye = jnp.arange(group)[:, None] == jnp.arange(group)[None, :]
    allowed = (seg[:, :, None] == seg[:, None, :]) & ((valid[:, None, :] == 1) | eye[None])
    bias = jnp.where(allowed, 0.0, NEG).astype(BF)

    def pick(which):
        m = mods[:, which]
        s = seg_own[:, None]
        out = m[images - 1][None]
        for i in range(images - 2, -1, -1):
            out = jnp.where(s == i, m[i][None], out)
        return out

    x_in = tokens[0].astype(F32)
    grad_in = cotangent[0].astype(F32)
    shift1, scale1, gate1, shift2, scale2, gate2 = (pick(i) for i in range(6))
    first_f, first_back = jax.vjp(norm_mod, x_in, shift1, scale1)
    d_branch_own = (gate2 * grad_in).astype(BF)
    first = plane_gather(after(first_f.astype(BF), qkv_part), 2).reshape(2 * group, width)
    up_part, down_part = spread([after(up_weight, first), down_weight], 3)
    outp_w, up_w, down_w = z_gather(outp), z_gather(up_part), z_gather(down_part)

    qkv = dot(first, qkv_w).astype(BF)
    own_cols = local * HEAD_DIM
    cost = 4 * 2 * group * group * own_cols
    mixed = per_group(
        functools.partial(attend_kernel, factor), [qkv], bias, own_cols, group, 5 * cost
    )
    part = dot(mixed, outp_w).astype(BF).reshape(PLANE, rows, width)
    attn = plane_scatter(part, 6)
    x_mid = x_in + gate1 * attn
    second_f, second_back = jax.vjp(norm_mod, x_mid, shift2, scale2)
    second = plane_gather(second_f.astype(BF), 7).reshape(2 * group, width)
    hidden_pre = dot(second, up_w)
    hidden_f, gelu_back = jax.vjp(jax.nn.gelu, hidden_pre)
    hidden = hidden_f.astype(BF)

    d_branch = plane_gather(after(d_branch_own, hidden), 5).reshape(2 * group, width)
    d_down = over_rows(d_branch, hidden).astype(BF)
    d_down, d_branch = lax.optimization_barrier((d_down, d_branch))
    d_down = z_scatter(d_down)
    d_pre = gelu_back(dot(d_branch, down_w))[0].astype(BF)
    d_up = over_rows(second, d_pre).astype(BF)
    d_up, d_pre = lax.optimization_barrier((d_up, d_pre))
    d_up = z_scatter(d_up)
    part = times_t(d_pre, up_w).astype(BF).reshape(PLANE, rows, width)
    d_second = plane_scatter(part, 9)
    d_mid_norm, d_shift2, d_scale2 = second_back(d_second)
    d_mid = grad_in + d_mid_norm
    d_attn = (gate1 * d_mid).astype(BF)
    d_gate1 = d_mid * attn
    d_attn_all = plane_gather(d_attn, 10).reshape(2 * group, width)
    d_mixed = times_t(d_attn_all, outp_w).astype(BF)
    d_qkv = per_group(
        functools.partial(attend_back_kernel, factor),
        [qkv, d_mixed],
        bias,
        3 * own_cols,
        group,
        10 * cost,
    )
    d_qkv_w = over_rows(first, d_qkv).astype(BF)
    d_qkv_w, d_qkv, d_attn_all = lax.optimization_barrier((d_qkv_w, d_qkv, d_attn_all))
    d_qkv_w = z_scatter(d_qkv_w)
    d_outp = over_rows(mixed, d_attn_all).astype(BF)
    d_outp, d_qkv = lax.optimization_barrier((d_outp, d_qkv))
    d_outp = z_scatter(d_outp)
    part = times_t(d_qkv, qkv_w).astype(BF).reshape(PLANE, rows, width)
    d_first = plane_scatter(part, 11)
    d_in_norm, d_shift1, d_scale1 = first_back(d_first)
    grad_tokens = d_mid + d_in_norm
    part = times_t(after(hidden, d_first), down_w).astype(BF).reshape(PLANE, rows, width)
    branch = plane_scatter(part, 8)
    block_out = (x_mid + gate2 * branch).astype(BF)
    d_gate2 = grad_in * branch

    tok_grads = jnp.concatenate([d_shift1, d_scale1, d_gate1, d_shift2, d_scale2, d_gate2], axis=1)
    picker = (seg_own[:, None] == jnp.arange(8, dtype=jnp.int32)[None, :]).astype(F32)
    image_grads = lax.dot_general(picker, tok_grads, (((0,), (0,)), ((), ())), precision=HIGH)
    sent = image_grads.reshape(8, devices, -1).transpose(1, 0, 2)
    mod_grads, cond_grads = mods_back(sent, mod_weight, 15)
    mod_grads = mod_grads[:, :images].reshape(2 * nz * images, -1)
    grad_mod = lax.dot_general(
        cond.astype(F32), mod_grads, (((0,), (0,)), ((), ())), precision=HIGH
    )
    cond_grads = cond_grads.reshape(2 * nz, 4, 8, width // 4)[:, :, :images]
    cond_grads = cond_grads.transpose(0, 2, 1, 3).reshape(2 * nz * images, width)
    grad_table = jax.ops.segment_sum(cond_grads, levels, num_segments=noise_table.shape[0])

    d_down = after(d_down, sent)
    d_up, d_down = collect([d_up, d_down], 12)
    (d_qkv_w,) = collect([after(d_qkv_w, d_up)], 13, blocks=3)
    d_outp = lax.ppermute(d_outp, ALL, [(b, a) for a, b in move])
    return (
        block_out[None],
        grad_tokens[None],
        grad_table,
        grad_mod,
        d_qkv_w.astype(F32),
        d_outp.astype(F32),
        d_up.astype(F32),
        d_down.astype(F32),
    )


def solution(mesh):
    groups, blks = mesh.shape["dp"], mesh.shape["blk"]
    planes = Mesh(mesh.devices.reshape(groups // 2, 2, blks), ALL)
    dp = ("z", "y")
    whole = ("z", "y", "blk")
    placed = (
        P(dp, "blk", None),
        P(),
        P(None, whole),
        P(whole, None),
        P(whole, None),
        P(whole, None),
        P(whole, None),
        P(dp, None),
        P(dp, None),
        P(),
        P(dp, "blk", None),
    )
    return jax.shard_map(
        on_device,
        mesh=planes,
        in_specs=placed,
        out_specs=(
            P(dp, "blk", None),
            P(dp, "blk", None),
            P(),
            P(None, whole),
            P(whole, None),
            P(whole, None),
            P(whole, None),
            P(whole, None),
        ),
        check_vma=False,
    )
```

```python
import functools
import math

import jax
import jax.numpy as jnp
from jax import lax
from jax.experimental import pallas as pl
from jax.experimental.pallas import tpu as pltpu
from jax.sharding import Mesh
from jax.sharding import PartitionSpec as P

HEADS = 16
HEAD_DIM = 128
EPS = 1e-06
NEG = -1e30
HIGH = lax.Precision.HIGHEST
PLANE = 8
BF = jnp.bfloat16
F32 = jnp.float32
ALL = ("z", "y", "blk")
MIB = 1 << 20


def peer(k):
    y, b = lax.axis_index("y"), lax.axis_index("blk")
    high, low = lax.div(b, 2), lax.rem(b, 2)
    if k & 4:
        y = 1 - y
    if k & 2:
        high = 1 - high
    if k & 1:
        low = 1 - low
    return {"y": y, "blk": high * 2 + low}


def place(k):
    where = peer(k)
    return where["y"] * 4 + where["blk"]


def greet(peers):
    barrier = pltpu.get_barrier_semaphore()
    for k in peers:
        pl.semaphore_signal(
            barrier, inc=1, device_id=peer(k), device_id_type=pl.DeviceIdType.MESH
        )
    pl.semaphore_wait(barrier, len(peers))


def send(src, dst, ssem, rsem, k):
    copy = pltpu.make_async_remote_copy(
        src_ref=src,
        dst_ref=dst,
        send_sem=ssem,
        recv_sem=rsem,
        device_id=peer(k),
        device_id_type=pl.DeviceIdType.MESH,
    )
    copy.start()
    return copy


def call(kernel, ins, outs, scratch, ident, vmem=16, micros=10):
    return pl.pallas_call(
        kernel,
        out_shape=outs,
        in_specs=[pl.BlockSpec(memory_space=pl.ANY)] * len(ins),
        out_specs=jax.tree.map(lambda _: pl.BlockSpec(memory_space=pl.ANY), outs),
        scratch_shapes=scratch,
        compiler_params=pltpu.CompilerParams(
            collective_id=ident, has_side_effects=True, vmem_limit_bytes=vmem * MIB
        ),
        cost_estimate=pl.CostEstimate(
            flops=0, bytes_accessed=int(micros * 3.6e6), transcendentals=0
        ),
    )(*ins)


class Gather:
    shapes = staticmethod(lambda dma: [dma((1,)), dma((13,)), dma((13,))])

    def __init__(self, xv, o, sems):
        self.xv, self.o = xv, o
        self.lsem, self.ssem, self.rsem = sems
        self.rows = xv.shape[0]
        self.all = []

    def block(self, k, part=None):
        half = self.rows // 2
        first = k * self.rows + (half if part == 1 else 0)
        return self.o.at[pl.ds(first, self.rows if part is None else half)]

    def mine(self, part):
        half = self.rows // 2
        return self.xv.at[pl.ds(part * half, half)]

    def go(self, src, dst, k):
        i = len(self.all)
        self.all.append(send(src, dst, self.ssem.at[i], self.rsem.at[i], k))
        return self.all[-1]

    def begin(self):
        self.x_bot = self.go(self.mine(1), self.block(2, 1), 2)
        self.y_top = self.go(self.mine(0), self.block(4, 0), 4)
        self.x_top = self.go(self.mine(0), self.block(2, 0), 2)
        self.y_bot = self.go(self.mine(1), self.block(4, 1), 4)
        self.sib = self.go(self.xv, self.block(1), 1)
        self.own = pltpu.make_async_copy(self.xv, self.block(0), self.lsem.at[0])
        self.own.start()

    def relay(self):
        self.x_bot.wait_recv()
        self.dy = self.go(self.block(2, 1), self.block(6, 1), 4)
        self.late = [self.go(self.block(2, 1), self.block(3, 1), 1)]
        self.y_top.wait_recv()
        self.dx = self.go(self.block(4, 0), self.block(6, 0), 2)
        self.late.append(self.go(self.block(4, 0), self.block(5, 0), 1))

    def finish(self):
        self.x_top.wait_recv()
        self.late.append(self.go(self.block(2, 0), self.block(3, 0), 1))
        self.y_bot.wait_recv()
        self.late.append(self.go(self.block(4, 1), self.block(5, 1), 1))
        self.dx.wait_recv()
        self.late.append(self.go(self.block(6, 0), self.block(7, 0), 1))
        self.dy.wait_recv()
        self.late.append(self.go(self.block(6, 1), self.block(7, 1), 1))
        for copy in [self.sib] + self.late:
            copy.wait_recv()
        for copy in self.all:
            copy.wait_send()
        self.own.wait()


def gather_kernel(x, o, xv, load_sem, *sems):
    load = pltpu.make_async_copy(x, xv, load_sem)
    load.start()
    greet((1, 2, 4))
    load.wait()
    gather = Gather(xv, o, sems)
    gather.begin()
    gather.relay()
    gather.finish()


def plane_gather(x, ident):
    out = jax.ShapeDtypeStruct((PLANE * x.shape[0],) + x.shape[1:], x.dtype)
    dma = pltpu.SemaphoreType.DMA
    scratch = [pltpu.VMEM(x.shape, x.dtype), dma] + Gather.shapes(dma)
    return call(gather_kernel, (x,), out, scratch, ident, 8, 30)


def rows_loop(rows, body, step=16):
    def one(i, carry):
        body(pl.multiple_of(i * step, step), step)
        return carry

    lax.fori_loop(0, rows // step, one, 0)


class Scatter:
    @staticmethod
    def shapes(rows, width, dma):
        whole = pltpu.VMEM((4, rows, width), BF)
        pair = pltpu.VMEM((2, rows // 2, width), BF)
        return [whole, whole] + [pair] * 6 + [dma((4,)), dma((11,)), dma((11,))]

    def __init__(self, p, ov, scratch):
        self.p, self.ov = p, ov
        self.pv, self.rc, self.q6, self.q2, self.q4, self.d6, self.rx, self.ry = scratch[:8]
        self.lsem, self.ssem, self.rsem = scratch[8:]
        self.rows = ov.shape[0]
        self.half = self.rows // 2

    def block(self, k, first=0, count=None):
        return self.p.at[pl.ds(k * self.rows + first, count or self.rows)]

    def go(self, i, src, dst, k):
        return send(src, dst, self.ssem.at[i], self.rsem.at[i], k)

    def begin(self):
        half = self.half
        top, bot = pl.ds(0, half), pl.ds(half, half)
        self.c7t = self.go(0, self.block(7, 0, half), self.rc.at[3, top], 1)
        self.c7b = self.go(1, self.block(7, half, half), self.rc.at[3, bot], 1)
        self.c3 = self.go(2, self.block(3), self.rc.at[1], 1)
        self.c5 = self.go(3, self.block(5), self.rc.at[2], 1)
        self.c1 = self.go(4, self.block(1), self.rc.at[0], 1)

    def load(self):
        self.loads = [
            pltpu.make_async_copy(self.block(2 * i), self.pv.at[i], self.lsem.at[i])
            for i in range(4)
        ]
        for i in (3, 1, 2, 0):
            self.loads[i].start()

    def add(self, dst, i, start, more=None):
        def body(r, n):
            s = pl.ds(pl.multiple_of(start + r, 16), n)
            total = self.pv[i, s, :].astype(F32) + self.rc[i, s, :].astype(F32)
            if more is not None:
                total = total + more[pl.ds(r, n), :].astype(F32)
            dst[pl.ds(r, n), :] = total.astype(BF)

        rows_loop(self.half, body)

    def middle(self):
        half = self.half
        self.loads[3].wait()
        self.c7t.wait_recv()
        self.add(self.q6.at[0], 3, 0)
        self.s6t = self.go(5, self.q6.at[0], self.d6.at[0], 2)
        self.c7b.wait_recv()
        self.add(self.q6.at[1], 3, half)
        self.s6b = self.go(6, self.q6.at[1], self.d6.at[1], 4)
        self.loads[1].wait()
        self.c3.wait_recv()
        self.add(self.q2.at[0], 1, 0)
        self.s2t = self.go(7, self.q2.at[0], self.rx.at[0], 2)
        self.loads[2].wait()
        self.c5.wait_recv()
        self.add(self.q4.at[1], 2, half)
        self.s4b = self.go(8, self.q4.at[1], self.ry.at[1], 4)

    def relay(self):
        self.s6t.wait_recv()
        self.add(self.q4.at[0], 2, 0, self.d6.at[0])
        self.s4t = self.go(9, self.q4.at[0], self.ry.at[0], 4)
        self.s6b.wait_recv()
        self.add(self.q2.at[1], 1, self.half, self.d6.at[1])
        self.s2b = self.go(10, self.q2.at[1], self.rx.at[1], 2)

    def total(self, n):
        def body(r, count):
            s = pl.ds(pl.multiple_of(n * self.half + r, 16), count)
            r = pl.ds(r, count)
            total = self.pv[0, s, :].astype(F32) + self.rc[0, s, :].astype(F32)
            total = total + self.rx[n, r, :].astype(F32) + self.ry[n, r, :].astype(F32)
            self.ov[s, :] = total

        rows_loop(self.half, body)

    def finish(self):
        self.loads[0].wait()
        self.c1.wait_recv()
        self.s2t.wait_recv()
        self.s4t.wait_recv()
        self.total(0)
        self.s2b.wait_recv()
        self.s4b.wait_recv()
        self.total(1)
        for copy in (self.c7t, self.c7b, self.c3, self.c5, self.c1, self.s6t, self.s6b):
            copy.wait_send()
        for copy in (self.s2t, self.s4b, self.s4t, self.s2b):
            copy.wait_send()


def scatter_kernel(p, o, ov, osem, *scratch):
    greet((1, 2, 4))
    scatter = Scatter(p, ov, scratch)
    scatter.begin()
    scatter.load()
    scatter.middle()
    scatter.relay()
    scatter.finish()
    out = pltpu.make_async_copy(ov, o, osem)
    out.start()
    out.wait()


def plane_scatter(p, ident):
    rows, width = p.shape[0] // PLANE, p.shape[1]
    dma = pltpu.SemaphoreType.DMA
    scratch = [pltpu.VMEM((rows, width), F32), dma] + Scatter.shapes(rows, width, dma)
    out = jax.ShapeDtypeStruct((rows, width), F32)
    return call(scatter_kernel, (p,), out, scratch, ident, 24, 31)


def cut(weights, blocks):
    plan = []
    for i, cols in enumerate(weights):
        each = cols // blocks
        for b in range(blocks):
            plan.append((i, b * each, each // PLANE, b * (each // PLANE)))
    return plan


def spread_kernel(plan, count, *refs):
    ins, outs, held = refs[:count], refs[count : 2 * count], refs[2 * count : 3 * count]
    lsem, ssem, rsem = refs[3 * count :]
    loads = [pltpu.make_async_copy(a, v, lsem.at[i]) for i, (a, v) in enumerate(zip(ins, held))]
    for copy in loads:
        copy.start()
    greet(range(1, PLANE))
    mine = place(0)
    remotes = []
    for w, load in enumerate(loads):
        load.wait()
        rows = ins[w].shape[0]
        here = pl.ds(pl.multiple_of(mine * rows, 16), rows)
        for n, (i, base, width, col) in enumerate(plan):
            if i != w:
                continue
            for k in (6, 7, 2, 3, 4, 5, 1):
                cols = pl.ds(pl.multiple_of(base + place(k) * width, 128), width)
                remotes.append(
                    send(
                        held[w].at[:, cols],
                        outs[w].at[here, pl.ds(col, width)],
                        ssem.at[n, k],
                        rsem.at[n, k],
                        k,
                    )
                )
            cols = pl.ds(pl.multiple_of(base + mine * width, 128), width)
            copy = pltpu.make_async_copy(
                held[w].at[:, cols], outs[w].at[here, pl.ds(col, width)], ssem.at[n, 0]
            )
            copy.start()
            remotes.append(copy)
    for copy in remotes:
        copy.wait()


def spread(weights, ident, blocks=1):
    plan = cut([w.shape[1] for w in weights], blocks)
    outs = [
        jax.ShapeDtypeStruct((w.shape[0] * PLANE, w.shape[1] // PLANE), w.dtype) for w in weights
    ]
    dma = pltpu.SemaphoreType.DMA
    n = len(plan)
    scratch = [pltpu.VMEM(w.shape, w.dtype) for w in weights]
    return call(
        functools.partial(spread_kernel, plan, len(weights)),
        tuple(weights),
        outs,
        scratch + [dma((len(weights),)), dma((n, PLANE)), dma((n, PLANE))],
        ident,
        8,
        sum(w.size for w in weights) / 3e4,
    )


def collect_kernel(plan, count, *refs):
    ins, outs, held = refs[:count], refs[count : 2 * count], refs[2 * count : 3 * count]
    lsem, ssem, rsem = refs[3 * count :]
    loads = [pltpu.make_async_copy(a, v, lsem.at[i]) for i, (a, v) in enumerate(zip(ins, held))]
    for copy in loads:
        copy.start()
    greet(range(1, PLANE))
    mine = place(0)
    remotes = []
    for w, load in enumerate(loads):
        load.wait()
        rows = outs[w].shape[0]
        for n, (i, base, width, col) in enumerate(plan):
            if i != w:
                continue
            cols = pl.ds(pl.multiple_of(base + mine * width, 128), width)
            for k in (6, 7, 2, 3, 4, 5, 1):
                there = pl.ds(pl.multiple_of(place(k) * rows, 16), rows)
                remotes.append(
                    send(
                        held[w].at[there, pl.ds(col, width)],
                        outs[w].at[:, cols],
                        ssem.at[n, k],
                        rsem.at[n, k],
                        k,
                    )
                )
            here = pl.ds(pl.multiple_of(mine * rows, 16), rows)
            copy = pltpu.make_async_copy(
                held[w].at[here, pl.ds(col, width)], outs[w].at[:, cols], ssem.at[n, 0]
            )
            copy.start()
            remotes.append(copy)
    for copy in remotes:
        copy.wait()


def collect(grads, ident, blocks=1):
    plan = cut([g.shape[1] * PLANE for g in grads], blocks)
    outs = [
        jax.ShapeDtypeStruct((g.shape[0] // PLANE, g.shape[1] * PLANE), g.dtype) for g in grads
    ]
    dma = pltpu.SemaphoreType.DMA
    n = len(plan)
    scratch = [pltpu.VMEM(g.shape, g.dtype) for g in grads]
    return call(
        functools.partial(collect_kernel, plan, len(grads)),
        tuple(grads),
        outs,
        scratch + [dma((len(grads),)), dma((n, PLANE)), dma((n, PLANE))],
        ident,
        8,
        sum(g.size for g in grads) / 3e4,
    )


def flat_place():
    return lax.axis_index("z") * PLANE + lax.axis_index("y") * 4 + lax.axis_index("blk")


def flat_id(d):
    return {"z": lax.div(d, PLANE), "y": lax.rem(lax.div(d, 4), 2), "blk": lax.rem(d, 4)}


def greet_all(count):
    barrier = pltpu.get_barrier_semaphore()
    me = flat_place()

    def one(i, carry):
        pl.semaphore_signal(
            barrier,
            inc=1,
            device_id=flat_id(lax.rem(me + i, count)),
            device_id_type=pl.DeviceIdType.MESH,
        )
        return carry

    lax.fori_loop(1, count, one, 0)
    pl.semaphore_wait(barrier, count - 1)


def to_all(count, source, target, ssem, rsem):
    me = flat_place()

    def copy(i):
        d = lax.rem(me + i, count)
        return pltpu.make_async_remote_copy(
            src_ref=source(d),
            dst_ref=target.at[me],
            send_sem=ssem.at[i],
            recv_sem=rsem.at[i],
            device_id=flat_id(d),
            device_id_type=pl.DeviceIdType.MESH,
        )

    def begin(i, carry):
        copy(i).start()
        return carry

    def finish(i, carry):
        copy(i).wait()
        return carry

    lax.fori_loop(1, count, begin, 0)
    target[me] = source(me)[...]
    lax.fori_loop(1, count, finish, 0)


def exchange_kernel(count, x, o, ssem, rsem):
    greet_all(count)
    to_all(count, lambda d: x.at[d], o, ssem, rsem)


def small_call(kernel, ins, outs, scratch, ident, micros):
    vmem = pl.BlockSpec(memory_space=pltpu.VMEM)
    return pl.pallas_call(
        kernel,
        out_shape=outs,
        in_specs=[vmem] * len(ins),
        out_specs=jax.tree.map(lambda _: vmem, outs),
        scratch_shapes=scratch,
        compiler_params=pltpu.CompilerParams(
            collective_id=ident, has_side_effects=True, vmem_limit_bytes=32 * MIB
        ),
        cost_estimate=pl.CostEstimate(
            flops=0, bytes_accessed=int(micros * 3.6e6), transcendentals=0
        ),
    )(*ins)


def exchange(x, ident):
    dma = pltpu.SemaphoreType.DMA((x.shape[0],))
    return small_call(
        functools.partial(exchange_kernel, x.shape[0]),
        (x,),
        jax.ShapeDtypeStruct(x.shape, x.dtype),
        [dma, dma],
        ident,
        8,
    )


def mods_back_kernel(count, x, w, o, t, got, part, mine, s0, r0, s1, r1, s2, r2):
    greet_all(count)
    to_all(count, lambda d: x.at[d], got, s0, r0)
    groups = o.shape[0]
    for g in range(groups):
        o[g] = got[4 * g] + got[4 * g + 1] + got[4 * g + 2] + got[4 * g + 3]
    own = o[...].reshape(groups * 8, o.shape[2])
    high = own.astype(BF)
    rest = own - high.astype(F32)
    low = rest.astype(BF)
    quarter = w.shape[0] // 4
    for q in range(4):
        piece = w[q * quarter : (q + 1) * quarter, :]
        product = times_t(high, piece) + times_t(low, piece)
        for g in range(groups):
            part[4 * g + q] = product[8 * g : 8 * g + 8]
    to_all(count, lambda d: part.at[d], mine, s1, r1)

    def add(i, total):
        return total + mine[i]

    part[flat_place()] = lax.fori_loop(0, count, add, jnp.zeros(mine.shape[1:], F32))
    to_all(count, lambda d: part.at[flat_place()], t, s2, r2)


def mods_back(x, w, ident):
    count, eight, cols = x.shape
    width = w.shape[0]
    dma = pltpu.SemaphoreType.DMA((count,))
    pieces = jax.ShapeDtypeStruct((count, eight, width // 4), F32)
    return small_call(
        functools.partial(mods_back_kernel, count),
        (x, w),
        (jax.ShapeDtypeStruct((count // 4, eight, cols), F32), pieces),
        [pltpu.VMEM(x.shape, F32), pltpu.VMEM(pieces.shape, F32), pltpu.VMEM(pieces.shape, F32)]
        + [dma] * 6,
        ident,
        20,
    )


def z_gather(x):
    return lax.all_gather(x, "z", axis=0, tiled=True)


def z_scatter(g):
    return lax.psum_scatter(g, "z", scatter_dimension=0, tiled=True)


def z_peer(m):
    z = lax.axis_index("z")
    if m == 1:
        z = z + 1 - 2 * lax.rem(z, 2)
    elif m == 2:
        z = lax.rem(z + 2, 4)
    else:
        z = 3 - z
    return z


def greet_more():
    barrier = pltpu.get_barrier_semaphore()
    ids = [peer(k) for k in range(1, PLANE)] + [{"z": z_peer(m)} for m in (1, 2, 3)]
    for where in ids:
        pl.semaphore_signal(
            barrier, inc=1, device_id=where, device_id_type=pl.DeviceIdType.MESH
        )
    pl.semaphore_wait(barrier, len(ids))


class PlaneSum:
    @staticmethod
    def shapes(m, c, dma):
        return [pltpu.VMEM((m, c), BF), dma((4,)), dma((4,))]

    def __init__(self, g, landing, scratch, temps):
        self.g, self.landing, self.temps = g, landing, temps
        self.q, self.ssem, self.rsem = scratch
        self.m, self.c = g.shape[1:]
        z = lax.axis_index("z")
        self.inner = (z == 1) | (z == 2)
        self.outer = (z == 0) | (z == 3)

    def copy(self, src, slot, m):
        return pltpu.make_async_remote_copy(
            src_ref=src,
            dst_ref=self.landing.at[slot],
            send_sem=self.ssem.at[slot],
            recv_sem=self.rsem.at[slot],
            device_id={"z": z_peer(m)},
            device_id_type=pl.DeviceIdType.MESH,
        )

    def begin(self):
        far = self.g.at[z_peer(3)]
        pl.when(self.outer)(lambda: self.copy(far, 2, 1).start())
        pl.when(self.inner)(lambda: self.copy(far, 3, 3).start())

    def temp(self, i):
        return self.temps.at[i, pl.ds(0, self.m), pl.ds(0, self.c)]

    def load(self, src, i):
        copy = pltpu.make_async_copy(src, self.temp(i), self.tsem.at[i])
        copy.start()
        return copy

    def hop(self, tsem):
        self.tsem = tsem
        across = self.g.at[z_peer(2)]

        @pl.when(self.outer)
        def _():
            self.copy(across, 1, 2).start()

        @pl.when(self.inner)
        def _():
            first = self.load(across, 0)
            self.copy(across, 2, 1).wait_recv()
            second = self.load(self.landing.at[2], 1)
            first.wait()
            second.wait()

            def body(r, n):
                r = (pl.ds(r, n), pl.ds(0, self.c))
                total = self.temps[(0,) + r].astype(F32) + self.temps[(1,) + r].astype(F32)
                self.q[r] = total.astype(BF)

            rows_loop(self.m, body)
            self.copy(self.q, 1, 2).start()

        self.near = self.copy(self.g.at[z_peer(1)], 0, 1)
        self.near.start()

    def finish(self, tsem):
        self.tsem = tsem
        loads = [self.load(self.g.at[lax.axis_index("z")], 0)]
        self.near.wait_recv()
        loads.append(self.load(self.landing.at[0], 1))
        far = self.copy(self.q, 1, 2)
        far.wait_recv()
        loads.append(self.load(self.landing.at[1], 2))
        pl.when(self.inner)(lambda: self.copy(self.g.at[0], 3, 3).wait_recv())
        pl.when(self.inner)(lambda: self.load(self.landing.at[3], 3).wait())
        for copy in loads:
            copy.wait()
        far.wait_send()
        self.near.wait_send()
        pl.when(self.outer)(lambda: self.copy(self.g.at[0], 2, 1).wait_send())
        pl.when(self.inner)(lambda: self.copy(self.g.at[0], 3, 3).wait_send())

        def three(r, n):
            r = (pl.ds(r, n), pl.ds(0, self.c))
            total = self.temps[(0,) + r].astype(F32) + self.temps[(1,) + r].astype(F32)
            return r, total + self.temps[(2,) + r].astype(F32)

        def outer(r, n):
            r, total = three(r, n)
            self.q[r] = total.astype(BF)

        def inner(r, n):
            r, total = three(r, n)
            self.q[r] = (total + self.temps[(3,) + r].astype(F32)).astype(BF)

        pl.when(self.outer)(lambda: rows_loop(self.m, outer))
        pl.when(self.inner)(lambda: rows_loop(self.m, inner))


def deal(src, out, blocks, ssem, rsem):
    rows = out.shape[0]
    mine = place(0)
    copies = []
    for n, (_, base, width, col) in enumerate(cut([out.shape[1]], blocks)):
        cols = pl.ds(pl.multiple_of(base + mine * width, 128), width)
        for k in (6, 7, 2, 3, 4, 5, 1, 0):
            there = pl.ds(pl.multiple_of(place(k) * rows, 16), rows)
            piece = src.at[there, pl.ds(col, width)]
            if k:
                copies.append(send(piece, out.at[:, cols], ssem.at[n, k], rsem.at[n, k], k))
            else:
                copies.append(pltpu.make_async_copy(piece, out.at[:, cols], ssem.at[n, 0]))
                copies[-1].start()
    return copies


def pipe(body, steps, ins, outs):
    spec = lambda a: pl.BlockSpec(a[1], a[2])
    pltpu.emit_pipeline(
        body, grid=(steps,), in_specs=[spec(a) for a in ins], out_specs=[spec(a) for a in outs]
    )(*[a[0] for a in ins], *[a[0] for a in outs])


def whole(a):
    return (a, a.shape, lambda i: (0,) * len(a.shape))


def some_rows(a, n, pick=lambda i: i):
    return (a, (n, a.shape[1]), lambda i: (pick(i), 0))


def grads_mm(a, b, g):
    m = g.shape[1]

    def body(a, b, g):
        g[0] = over_rows(a[...], b[...]).astype(BF)

    pipe(
        body,
        g.shape[0],
        [(a, (a.shape[0], m), lambda i: (0, i)), whole(b)],
        [(g, (1,) + g.shape[1:], lambda i: (i, 0, 0))],
    )


def rows_mm(a, b, o, n, steps, pick=lambda i: i, transposed=False):
    def body(a, b, o):
        o[...] = (times_t if transposed else dot)(a[...], b[...]).astype(BF)

    pipe(body, steps, [some_rows(a, n, pick), whole(b)], [some_rows(o, n, pick)])


def back_kernel(factor, nz, *refs):
    ins, refs = refs[:16], refs[16:]
    (dy, hid, slope, second, first, mixed, qkv, bias, up, down, outw, qkvw) = ins[:12]
    (x_mid, scale2, gate1, grad_in) = ins[12:]
    (e2, e1, y, c_down, c_up, c_qkv, c_out), refs = refs[:7], refs[7:]
    (du, part, part_y, dat, dmix, dqkv, g_down, g_up, g_qkv, g_out), refs = refs[:10], refs[10:]
    lands, refs = refs[:4], refs[4:]
    (xv, temps, temps_out, tsem), refs = refs[:4], refs[4:]
    sc_a, sc_b, refs = refs[:11], refs[11:22], refs[22:]
    ga, refs = refs[:3], refs[3:]
    zs, refs = [refs[3 * i : 3 * i + 3] for i in range(4)], refs[12:]
    deal_sems = refs
    rows, width = e2.shape
    tokens = dy.shape[0]
    group = bias.shape[1]
    planes = nz == 4
    sums = [
        PlaneSum(g, land, z, t)
        for g, land, z, t in zip(
            (g_down, g_up, g_qkv, g_out), lands, zs, (temps, temps, temps, temps_out)
        )
    ]
    s_down, s_up, s_qkv, s_out = sums if planes else [None] * 4
    begin = lambda s: s and s.begin()
    hop = lambda s: s and s.hop(tsem)
    odd, even = (lambda i: 2 * i + 1), (lambda i: 2 * i)

    if planes:
        greet_more()
    else:
        greet(range(1, PLANE))
    grads_mm(dy, hid, g_down)
    begin(s_down)

    def du_body(a, b, s, o):
        o[...] = (dot(a[...], b[...]) * s[...]).astype(BF)

    n = math.gcd(tokens, 256)
    pipe(
        du_body,
        tokens // n,
        [some_rows(dy, n), whole(down), some_rows(slope, n)],
        [some_rows(du, n)],
    )
    grads_mm(second, du, g_up)
    rows_mm(du, up, part, rows, 4, odd, True)
    ra = Scatter(part, e2, sc_a)
    ra.begin()
    rows_mm(du, up, part, rows, 4, even, True)
    hop(s_down)
    begin(s_up)
    ra.load()
    ra.middle()
    ra.relay()
    ra.finish()

    def norm_back(r, n):
        r = pl.ds(r, n)
        x = x_mid[r, :]
        inv = lax.rsqrt(jnp.mean(x * x, axis=-1, keepdims=True) + EPS)
        normed = x * inv
        d_normed = e2[r, :] * (1.0 + scale2[r, :])
        slant = jnp.mean(d_normed * normed, axis=-1, keepdims=True)
        d_mid = grad_in[r, :].astype(F32) + inv * (d_normed - normed * slant)
        xv[r, :] = (gate1[r, :] * d_mid).astype(BF)

    rows_loop(rows, norm_back)
    gather = Gather(xv, dat, ga)
    gather.begin()
    rows_mm(hid, down, part_y, rows, 8, transposed=True)
    gather.relay()
    hop(s_up)
    gather.finish()
    ry = Scatter(part_y, y, sc_b)
    ry.begin()
    ry.load()
    rows_mm(dat, outw, dmix, 2 * rows, 4, transposed=True)
    ry.middle()

    def attend_body(qkv, bias, d_o, out):
        attend_back_kernel(factor, qkv, bias, d_o, out)

    pipe(
        attend_body,
        2,
        [
            some_rows(qkv, group),
            (bias, (1, group, group), lambda i: (i, 0, 0)),
            some_rows(dmix, group),
        ],
        [some_rows(dqkv, group)],
    )
    ry.relay()
    grads_mm(first, dqkv, g_qkv)
    begin(s_qkv)

    def out_body(a, b, g):
        g[...] = over_rows(a[...], b[...]).astype(BF).reshape(g.shape)

    step = math.gcd(width, 512)
    pipe(
        out_body,
        width // step,
        [whole(mixed), (dat, (tokens, step), lambda i: (0, i))],
        [(g_out, g_out.shape[:2] + (step,), lambda i: (0, 0, i))],
    )
    begin(s_out)
    ry.finish()
    rows_mm(dqkv, qkvw, part, rows, 4, odd, True)
    rb = Scatter(part, e1, sc_a)
    rb.begin()
    rows_mm(dqkv, qkvw, part, rows, 4, even, True)
    rb.load()
    rb.middle()
    hop(s_qkv)
    hop(s_out)
    rb.relay()
    rb.finish()
    if planes:
        dealt = []
        for s, out, blocks, sems in (
            (s_down, c_down, 1, deal_sems[:2]),
            (s_up, c_up, 1, deal_sems[2:4]),
            (s_qkv, c_qkv, 3, deal_sems[4:6]),
        ):
            s.finish(tsem)
            dealt += deal(s.q, out, blocks, *sems)
        s_out.finish(tsem)
        last = pltpu.make_async_copy(s_out.q, c_out, tsem.at[0])
        last.start()
        for copy in dealt + [last]:
            copy.wait()


def backward(ins, factor, nz, ident):
    dy, hid, slope, second, first, mixed, qkv, bias, up, down, outw, qkvw = ins[:12]
    rows, width = ins[12].shape
    tokens, wide = hid.shape
    part = qkvw.shape[1]
    heads = outw.shape[0]
    m = width // nz
    struct = jax.ShapeDtypeStruct
    own = struct((rows, width), F32)
    grads = [(nz, m, wide), (nz, m, wide), (nz, m, part), (nz, heads // nz, width)]
    lands = [(4,) + g[1:] for g in grads]
    shares = m // PLANE
    outs = [own] * 3 + [
        struct((shares, wide * PLANE), BF),
        struct((shares, wide * PLANE), BF),
        struct((shares, part * PLANE), BF),
        struct((heads // nz, width), BF),
        struct((tokens, wide), BF),
        struct((tokens, width), BF),
        struct((tokens, width), BF),
        struct((tokens, width), BF),
        struct((tokens, heads), BF),
        struct((tokens, part), BF),
    ]
    outs += [struct(g, BF) for g in grads + lands]
    dma = pltpu.SemaphoreType.DMA
    scratch = [
        pltpu.VMEM((rows, width), BF),
        pltpu.VMEM((4, m, max(wide, part)), BF),
        pltpu.VMEM((4,) + grads[3][1:], BF),
        dma((4,)),
    ]
    scratch += Scatter.shapes(rows, width, dma) * 2 + Gather.shapes(dma)
    for g in grads:
        scratch += PlaneSum.shapes(g[1], g[2], dma)
    for blocks in (1, 1, 3):
        scratch += [dma((blocks, PLANE))] * 2
    vmem = pl.BlockSpec(memory_space=pltpu.VMEM)
    anywhere = pl.BlockSpec(memory_space=pl.ANY)
    return pl.pallas_call(
        functools.partial(back_kernel, factor, nz),
        out_shape=outs,
        in_specs=[anywhere] * 12 + [vmem] * 4,
        out_specs=[vmem] * 3 + [anywhere] * (len(outs) - 3),
        scratch_shapes=scratch,
        compiler_params=pltpu.CompilerParams(
            collective_id=ident, has_side_effects=True, vmem_limit_bytes=62 * MIB
        ),
        cost_estimate=pl.CostEstimate(
            flops=0, bytes_accessed=int(220 * 3.6e6), transcendentals=0
        ),
    )(*ins)


def norm_mod(value, shift, scale):
    normed = value * lax.rsqrt(jnp.mean(value * value, axis=-1, keepdims=True) + EPS)
    return normed * (1.0 + scale) + shift


def dot(a, b):
    return jnp.dot(a, b, preferred_element_type=F32)


def over_rows(left, right):
    return lax.dot_general(left, right, (((0,), (0,)), ((), ())), preferred_element_type=F32)


def times_t(left, right):
    return lax.dot_general(left, right, (((1,), (1,)), ((), ())), preferred_element_type=F32)


def softmax_rows(q, k, bias, factor):
    scores = times_t(q, k) * factor + bias.astype(F32)
    expo = jnp.exp(scores - jnp.max(scores, axis=-1, keepdims=True))
    return expo / jnp.sum(expo, axis=-1, keepdims=True)


def row_blocks(count):
    step = math.gcd(count, 256)
    return [slice(i, i + step) for i in range(0, count, step)]


def attend_kernel(factor, qkv, bias, o):
    n = o.shape[1]
    for c in range(0, n, HEAD_DIM):
        k = qkv[:, n + c : n + c + HEAD_DIM]
        v = qkv[:, 2 * n + c : 2 * n + c + HEAD_DIM]
        for r in row_blocks(o.shape[0]):
            prob = softmax_rows(qkv[r, c : c + HEAD_DIM], k, bias[0, r, :], factor)
            o[r, c : c + HEAD_DIM] = dot(prob.astype(BF), v).astype(BF)


def attend_back_kernel(factor, qkv, bias, d_o, d_qkv):
    n = d_o.shape[1]
    for c in range(0, n, HEAD_DIM):
        k = qkv[:, n + c : n + c + HEAD_DIM]
        v = qkv[:, 2 * n + c : 2 * n + c + HEAD_DIM]
        dk = dv = 0.0
        for r in row_blocks(d_o.shape[0]):
            q = qkv[r, c : c + HEAD_DIM]
            out = d_o[r, c : c + HEAD_DIM]
            prob = softmax_rows(q, k, bias[0, r, :], factor)
            d_prob = times_t(out, v)
            delta = jnp.sum(prob * d_prob, axis=-1, keepdims=True)
            d_scores = (prob * (d_prob - delta)).astype(BF)
            d_qkv[r, c : c + HEAD_DIM] = (dot(d_scores, k) * factor).astype(BF)
            dk = dk + over_rows(d_scores, q)
            dv = dv + over_rows(prob.astype(BF), out)
        d_qkv[:, n + c : n + c + HEAD_DIM] = (dk * factor).astype(BF)
        d_qkv[:, 2 * n + c : 2 * n + c + HEAD_DIM] = dv.astype(BF)


def per_group(kernel, ins, bias, columns, group, flops):
    block = lambda c: pl.BlockSpec((group, c), lambda i: (i, 0))
    return pl.pallas_call(
        kernel,
        grid=(bias.shape[0],),
        out_shape=jax.ShapeDtypeStruct((bias.shape[0] * group, columns), BF),
        in_specs=[block(ins[0].shape[1]), pl.BlockSpec((1, group, group), lambda i: (i, 0, 0))]
        + [block(a.shape[1]) for a in ins[1:]],
        out_specs=block(columns),
        compiler_params=pltpu.CompilerParams(vmem_limit_bytes=48 * MIB),
        cost_estimate=pl.CostEstimate(flops=flops, bytes_accessed=0, transcendentals=0),
    )(ins[0], bias, *ins[1:])


def after(value, *others):
    return lax.optimization_barrier((value,) + others)[0]


def on_device(
    tokens,
    noise_table,
    mod_weight,
    qkv_weight,
    out_weight,
    up_weight,
    down_weight,
    segment,
    key_valid,
    noise_level,
    cotangent,
):
    rows, width = tokens.shape[1:]
    images = noise_level.shape[1]
    nz = lax.axis_size("z")
    blks = lax.axis_size("blk")
    z, y, blk = (lax.axis_index(a) for a in ALL)
    devices = nz * PLANE
    group = rows * blks
    local = HEADS // PLANE
    factor = 1.0 / math.sqrt(HEAD_DIM)

    levels = noise_level.reshape(-1)
    cond = jnp.take(noise_table, levels, axis=0)
    cols = dot(cond, mod_weight).reshape(2 * nz, 1, images, -1)
    sent = jnp.broadcast_to(cols, (2 * nz, blks) + cols.shape[2:])
    sent = jnp.pad(sent.reshape((devices,) + cols.shape[2:]), ((0, 0), (0, 8 - images), (0, 0)))

    mods = exchange(sent, 14)[:, :images]

    (qkv_part,) = spread([after(qkv_weight, mods)], 1, blocks=3)
    mods = mods.transpose(1, 0, 2).reshape(images, 6, width)
    qkv_w = z_gather(qkv_part)
    move = [(nz * k + i, i * PLANE + k) for k in range(PLANE) for i in range(nz)]
    outp = lax.ppermute(after(out_weight, qkv_part), ALL, move)

    both = jnp.concatenate([segment, key_valid], axis=0)
    other = lax.ppermute(both, "y", [(0, 1), (1, 0)])
    order = lambda a: jnp.stack(
        [
            lax.dynamic_index_in_dim(
                a.reshape(2, blks, rows),
                (lax.div(blk, 2) ^ (k >> 1)) * 2 + (lax.rem(blk, 2) ^ (k & 1)),
                1,
                keepdims=False,
            )
            for k in range(blks)
        ],
        axis=1,
    ).reshape(2, group)
    both, other = order(both), order(other)
    seg = jnp.stack([both[0], other[0]])
    valid = jnp.stack([both[1], other[1]])
    seg_own = seg[0, :rows]
    eye = jnp.arange(group)[:, None] == jnp.arange(group)[None, :]
    allowed = (seg[:, :, None] == seg[:, None, :]) & ((valid[:, None, :] == 1) | eye[None])
    bias = jnp.where(allowed, 0.0, NEG).astype(BF)

    def pick(which):
        m = mods[:, which]
        s = seg_own[:, None]
        out = m[images - 1][None]
        for i in range(images - 2, -1, -1):
            out = jnp.where(s == i, m[i][None], out)
        return out

    x_in = tokens[0].astype(F32)
    grad_in = cotangent[0].astype(F32)
    shift1, scale1, gate1, shift2, scale2, gate2 = (pick(i) for i in range(6))
    first_f, first_back = jax.vjp(norm_mod, x_in, shift1, scale1)
    d_branch_own = (gate2 * grad_in).astype(BF)
    first = plane_gather(after(first_f.astype(BF), qkv_part), 2)
    up_part, down_part = spread([after(up_weight, first), down_weight], 3)
    outp_w, up_w, down_w = z_gather(outp), z_gather(up_part), z_gather(down_part)

    qkv = dot(first, qkv_w).astype(BF)
    own_cols = local * HEAD_DIM
    cost = 4 * 2 * group * group * own_cols
    mixed = per_group(
        functools.partial(attend_kernel, factor), [qkv], bias, own_cols, group, 5 * cost
    )
    part = dot(mixed, outp_w).astype(BF)
    attn = plane_scatter(part, 6)
    x_mid = x_in + gate1 * attn
    second_f, second_back = jax.vjp(norm_mod, x_mid, shift2, scale2)
    second = plane_gather(second_f.astype(BF), 7)
    hidden_pre = dot(second, up_w)
    hidden_f, gelu_back = jax.vjp(jax.nn.gelu, hidden_pre)
    hidden = hidden_f.astype(BF)

    slope = gelu_back(jnp.ones_like(hidden_pre))[0]
    d_branch = plane_gather(after(d_branch_own, hidden), 5)
    ins = [d_branch, hidden, slope, second, first, mixed, qkv, bias, up_w, down_w, outp_w, qkv_w]
    ins += [x_mid, scale2, gate1, cotangent[0]]
    outs = backward(ins, factor, nz, 9)
    d_second, d_first, branch, d_down, d_up, d_qkv_w, d_outp = outs[:7]
    if nz != 4:
        flat = lambda g: z_scatter(g.reshape((-1,) + g.shape[2:]))
        d_down, d_up, d_qkv_w, d_outp = (flat(g) for g in outs[13:17])
        d_down, d_up = collect([d_down, d_up], 12)
        (d_qkv_w,) = collect([d_qkv_w], 13, blocks=3)
    block_out = (x_mid + gate2 * branch).astype(BF)
    d_gate2 = grad_in * branch
    d_mid_norm, d_shift2, d_scale2 = second_back(d_second)
    d_mid = grad_in + d_mid_norm
    d_gate1 = d_mid * attn
    d_in_norm, d_shift1, d_scale1 = first_back(d_first)
    grad_tokens = d_mid + d_in_norm

    tok_grads = jnp.concatenate([d_shift1, d_scale1, d_gate1, d_shift2, d_scale2, d_gate2], axis=1)
    picker = (seg_own[:, None] == jnp.arange(8, dtype=jnp.int32)[None, :]).astype(F32)
    image_grads = lax.dot_general(picker, tok_grads, (((0,), (0,)), ((), ())), precision=HIGH)
    sent = image_grads.reshape(8, devices, -1).transpose(1, 0, 2)
    mod_grads, cond_grads = mods_back(sent, mod_weight, 15)
    mod_grads = mod_grads[:, :images].reshape(2 * nz * images, -1)
    grad_mod = lax.dot_general(
        cond.astype(F32), mod_grads, (((0,), (0,)), ((), ())), precision=HIGH
    )
    cond_grads = cond_grads.reshape(2 * nz, 4, 8, width // 4)[:, :, :images]
    cond_grads = cond_grads.transpose(0, 2, 1, 3).reshape(2 * nz * images, width)
    grad_table = jax.ops.segment_sum(cond_grads, levels, num_segments=noise_table.shape[0])

    d_outp = lax.ppermute(d_outp, ALL, [(b, a) for a, b in move])
    return (
        block_out[None],
        grad_tokens[None],
        grad_table,
        grad_mod,
        d_qkv_w.astype(F32),
        d_outp.astype(F32),
        d_up.astype(F32),
        d_down.astype(F32),
    )


def solution(mesh):
    groups, blks = mesh.shape["dp"], mesh.shape["blk"]
    planes = Mesh(mesh.devices.reshape(groups // 2, 2, blks), ALL)
    dp = ("z", "y")
    whole = ("z", "y", "blk")
    placed = (
        P(dp, "blk", None),
        P(),
        P(None, whole),
        P(whole, None),
        P(whole, None),
        P(whole, None),
        P(whole, None),
        P(dp, None),
        P(dp, None),
        P(),
        P(dp, "blk", None),
    )
    return jax.shard_map(
        on_device,
        mesh=planes,
        in_specs=placed,
        out_specs=(
            P(dp, "blk", None),
            P(dp, "blk", None),
            P(),
            P(None, whole),
            P(whole, None),
            P(whole, None),
            P(whole, None),
            P(whole, None),
        ),
        check_vma=False,
    )
```

```python
import functools
import math

import jax
import jax.numpy as jnp
from jax import lax
from jax.experimental import pallas as pl
from jax.experimental.pallas import tpu as pltpu
from jax.sharding import Mesh
from jax.sharding import PartitionSpec as P

HEADS = 16
HEAD_DIM = 128
EPS = 1e-06
NEG = -1e30
HIGH = lax.Precision.HIGHEST
PLANE = 8
BF = jnp.bfloat16
F32 = jnp.float32
ALL = ("z", "y", "blk")
MIB = 1 << 20


def peer(k):
    y, b = lax.axis_index("y"), lax.axis_index("blk")
    high, low = lax.div(b, 2), lax.rem(b, 2)
    if k & 4:
        y = 1 - y
    if k & 2:
        high = 1 - high
    if k & 1:
        low = 1 - low
    return {"y": y, "blk": high * 2 + low}


def place(k):
    where = peer(k)
    return where["y"] * 4 + where["blk"]


def greet(peers):
    barrier = pltpu.get_barrier_semaphore()
    for k in peers:
        pl.semaphore_signal(
            barrier, inc=1, device_id=peer(k), device_id_type=pl.DeviceIdType.MESH
        )
    pl.semaphore_wait(barrier, len(peers))


def send(src, dst, ssem, rsem, k):
    copy = pltpu.make_async_remote_copy(
        src_ref=src,
        dst_ref=dst,
        send_sem=ssem,
        recv_sem=rsem,
        device_id=peer(k),
        device_id_type=pl.DeviceIdType.MESH,
    )
    copy.start()
    return copy


def call(kernel, ins, outs, scratch, ident, vmem=16, micros=10):
    return pl.pallas_call(
        kernel,
        out_shape=outs,
        in_specs=[pl.BlockSpec(memory_space=pl.ANY)] * len(ins),
        out_specs=jax.tree.map(lambda _: pl.BlockSpec(memory_space=pl.ANY), outs),
        scratch_shapes=scratch,
        compiler_params=pltpu.CompilerParams(
            collective_id=ident, has_side_effects=True, vmem_limit_bytes=vmem * MIB
        ),
        cost_estimate=pl.CostEstimate(
            flops=0, bytes_accessed=int(micros * 3.6e6), transcendentals=0
        ),
    )(*ins)


class Gather:
    shapes = staticmethod(lambda dma: [dma((1,)), dma((13,)), dma((13,))])

    def __init__(self, xv, o, sems):
        self.xv, self.o = xv, o
        self.lsem, self.ssem, self.rsem = sems
        self.rows = xv.shape[0]
        self.all = []

    def block(self, k, part=None):
        half = self.rows // 2
        first = k * self.rows + (half if part == 1 else 0)
        return self.o.at[pl.ds(first, self.rows if part is None else half)]

    def mine(self, part):
        half = self.rows // 2
        return self.xv.at[pl.ds(part * half, half)]

    def go(self, src, dst, k):
        i = len(self.all)
        self.all.append(send(src, dst, self.ssem.at[i], self.rsem.at[i], k))
        return self.all[-1]

    def begin(self):
        self.x_bot = self.go(self.mine(1), self.block(2, 1), 2)
        self.y_top = self.go(self.mine(0), self.block(4, 0), 4)
        self.x_top = self.go(self.mine(0), self.block(2, 0), 2)
        self.y_bot = self.go(self.mine(1), self.block(4, 1), 4)
        self.sib = self.go(self.xv, self.block(1), 1)
        self.own = pltpu.make_async_copy(self.xv, self.block(0), self.lsem.at[0])
        self.own.start()

    def relay(self):
        self.x_bot.wait_recv()
        self.dy = self.go(self.block(2, 1), self.block(6, 1), 4)
        self.late = [self.go(self.block(2, 1), self.block(3, 1), 1)]
        self.y_top.wait_recv()
        self.dx = self.go(self.block(4, 0), self.block(6, 0), 2)
        self.late.append(self.go(self.block(4, 0), self.block(5, 0), 1))

    def finish(self):
        self.x_top.wait_recv()
        self.late.append(self.go(self.block(2, 0), self.block(3, 0), 1))
        self.y_bot.wait_recv()
        self.late.append(self.go(self.block(4, 1), self.block(5, 1), 1))
        self.dx.wait_recv()
        self.late.append(self.go(self.block(6, 0), self.block(7, 0), 1))
        self.dy.wait_recv()
        self.late.append(self.go(self.block(6, 1), self.block(7, 1), 1))
        for copy in [self.sib] + self.late:
            copy.wait_recv()
        for copy in self.all:
            copy.wait_send()
        self.own.wait()


def gather_kernel(x, o, xv, load_sem, *sems):
    load = pltpu.make_async_copy(x, xv, load_sem)
    load.start()
    greet((1, 2, 4))
    load.wait()
    gather = Gather(xv, o, sems)
    gather.begin()
    gather.relay()
    gather.finish()


def plane_gather(x, ident):
    out = jax.ShapeDtypeStruct((PLANE * x.shape[0],) + x.shape[1:], x.dtype)
    dma = pltpu.SemaphoreType.DMA
    scratch = [pltpu.VMEM(x.shape, x.dtype), dma] + Gather.shapes(dma)
    return call(gather_kernel, (x,), out, scratch, ident, 8, 30)


def rows_loop(rows, body, step=16):
    def one(i, carry):
        body(pl.multiple_of(i * step, step), step)
        return carry

    lax.fori_loop(0, rows // step, one, 0)


class Scatter:
    @staticmethod
    def shapes(rows, width, dma):
        whole = pltpu.VMEM((4, rows, width), BF)
        pair = pltpu.VMEM((2, rows // 2, width), BF)
        return [whole, whole] + [pair] * 6 + [dma((4,)), dma((11,)), dma((11,))]

    def __init__(self, p, ov, scratch):
        self.p, self.ov = p, ov
        self.pv, self.rc, self.q6, self.q2, self.q4, self.d6, self.rx, self.ry = scratch[:8]
        self.lsem, self.ssem, self.rsem = scratch[8:]
        self.rows = ov.shape[0]
        self.half = self.rows // 2

    def block(self, k, first=0, count=None):
        return self.p.at[pl.ds(k * self.rows + first, count or self.rows)]

    def go(self, i, src, dst, k):
        return send(src, dst, self.ssem.at[i], self.rsem.at[i], k)

    def begin(self):
        half = self.half
        top, bot = pl.ds(0, half), pl.ds(half, half)
        self.c7t = self.go(0, self.block(7, 0, half), self.rc.at[3, top], 1)
        self.c7b = self.go(1, self.block(7, half, half), self.rc.at[3, bot], 1)
        self.c3 = self.go(2, self.block(3), self.rc.at[1], 1)
        self.c5 = self.go(3, self.block(5), self.rc.at[2], 1)
        self.c1 = self.go(4, self.block(1), self.rc.at[0], 1)

    def load(self):
        self.loads = [
            pltpu.make_async_copy(self.block(2 * i), self.pv.at[i], self.lsem.at[i])
            for i in range(4)
        ]
        for i in (3, 1, 2, 0):
            self.loads[i].start()

    def add(self, dst, i, start, more=None):
        def body(r, n):
            s = pl.ds(pl.multiple_of(start + r, 16), n)
            total = self.pv[i, s, :].astype(F32) + self.rc[i, s, :].astype(F32)
            if more is not None:
                total = total + more[pl.ds(r, n), :].astype(F32)
            dst[pl.ds(r, n), :] = total.astype(BF)

        rows_loop(self.half, body)

    def middle(self):
        half = self.half
        self.loads[3].wait()
        self.c7t.wait_recv()
        self.add(self.q6.at[0], 3, 0)
        self.s6t = self.go(5, self.q6.at[0], self.d6.at[0], 2)
        self.c7b.wait_recv()
        self.add(self.q6.at[1], 3, half)
        self.s6b = self.go(6, self.q6.at[1], self.d6.at[1], 4)
        self.loads[1].wait()
        self.c3.wait_recv()
        self.add(self.q2.at[0], 1, 0)
        self.s2t = self.go(7, self.q2.at[0], self.rx.at[0], 2)
        self.loads[2].wait()
        self.c5.wait_recv()
        self.add(self.q4.at[1], 2, half)
        self.s4b = self.go(8, self.q4.at[1], self.ry.at[1], 4)

    def relay(self):
        self.s6t.wait_recv()
        self.add(self.q4.at[0], 2, 0, self.d6.at[0])
        self.s4t = self.go(9, self.q4.at[0], self.ry.at[0], 4)
        self.s6b.wait_recv()
        self.add(self.q2.at[1], 1, self.half, self.d6.at[1])
        self.s2b = self.go(10, self.q2.at[1], self.rx.at[1], 2)

    def total(self, n):
        def body(r, count):
            s = pl.ds(pl.multiple_of(n * self.half + r, 16), count)
            r = pl.ds(r, count)
            total = self.pv[0, s, :].astype(F32) + self.rc[0, s, :].astype(F32)
            total = total + self.rx[n, r, :].astype(F32) + self.ry[n, r, :].astype(F32)
            self.ov[s, :] = total

        rows_loop(self.half, body)

    def finish(self):
        self.loads[0].wait()
        self.c1.wait_recv()
        self.s2t.wait_recv()
        self.s4t.wait_recv()
        self.total(0)
        self.s2b.wait_recv()
        self.s4b.wait_recv()
        self.total(1)
        for copy in (self.c7t, self.c7b, self.c3, self.c5, self.c1, self.s6t, self.s6b):
            copy.wait_send()
        for copy in (self.s2t, self.s4b, self.s4t, self.s2b):
            copy.wait_send()


def scatter_kernel(p, o, ov, osem, *scratch):
    greet((1, 2, 4))
    scatter = Scatter(p, ov, scratch)
    scatter.begin()
    scatter.load()
    scatter.middle()
    scatter.relay()
    scatter.finish()
    out = pltpu.make_async_copy(ov, o, osem)
    out.start()
    out.wait()


def plane_scatter(p, ident):
    rows, width = p.shape[0] // PLANE, p.shape[1]
    dma = pltpu.SemaphoreType.DMA
    scratch = [pltpu.VMEM((rows, width), F32), dma] + Scatter.shapes(rows, width, dma)
    out = jax.ShapeDtypeStruct((rows, width), F32)
    return call(scatter_kernel, (p,), out, scratch, ident, 24, 31)


def cut(weights, blocks):
    plan = []
    for i, cols in enumerate(weights):
        each = cols // blocks
        for b in range(blocks):
            plan.append((i, b * each, each // PLANE, b * (each // PLANE)))
    return plan


def spread_kernel(plan, count, *refs):
    ins, outs, held = refs[:count], refs[count : 2 * count], refs[2 * count : 3 * count]
    lsem, ssem, rsem = refs[3 * count :]
    loads = [pltpu.make_async_copy(a, v, lsem.at[i]) for i, (a, v) in enumerate(zip(ins, held))]
    for copy in loads:
        copy.start()
    greet(range(1, PLANE))
    mine = place(0)
    remotes = []
    for w, load in enumerate(loads):
        load.wait()
        rows = ins[w].shape[0]
        here = pl.ds(pl.multiple_of(mine * rows, 16), rows)
        for n, (i, base, width, col) in enumerate(plan):
            if i != w:
                continue
            for k in (6, 7, 2, 3, 4, 5, 1):
                cols = pl.ds(pl.multiple_of(base + place(k) * width, 128), width)
                remotes.append(
                    send(
                        held[w].at[:, cols],
                        outs[w].at[here, pl.ds(col, width)],
                        ssem.at[n, k],
                        rsem.at[n, k],
                        k,
                    )
                )
            cols = pl.ds(pl.multiple_of(base + mine * width, 128), width)
            copy = pltpu.make_async_copy(
                held[w].at[:, cols], outs[w].at[here, pl.ds(col, width)], ssem.at[n, 0]
            )
            copy.start()
            remotes.append(copy)
    for copy in remotes:
        copy.wait()


def spread(weights, ident, blocks=1):
    plan = cut([w.shape[1] for w in weights], blocks)
    outs = [
        jax.ShapeDtypeStruct((w.shape[0] * PLANE, w.shape[1] // PLANE), w.dtype) for w in weights
    ]
    dma = pltpu.SemaphoreType.DMA
    n = len(plan)
    scratch = [pltpu.VMEM(w.shape, w.dtype) for w in weights]
    return call(
        functools.partial(spread_kernel, plan, len(weights)),
        tuple(weights),
        outs,
        scratch + [dma((len(weights),)), dma((n, PLANE)), dma((n, PLANE))],
        ident,
        8,
        sum(w.size for w in weights) / 3e4,
    )


def collect_kernel(plan, count, *refs):
    ins, outs, held = refs[:count], refs[count : 2 * count], refs[2 * count : 3 * count]
    lsem, ssem, rsem = refs[3 * count :]
    loads = [pltpu.make_async_copy(a, v, lsem.at[i]) for i, (a, v) in enumerate(zip(ins, held))]
    for copy in loads:
        copy.start()
    greet(range(1, PLANE))
    mine = place(0)
    remotes = []
    for w, load in enumerate(loads):
        load.wait()
        rows = outs[w].shape[0]
        for n, (i, base, width, col) in enumerate(plan):
            if i != w:
                continue
            cols = pl.ds(pl.multiple_of(base + mine * width, 128), width)
            for k in (6, 7, 2, 3, 4, 5, 1):
                there = pl.ds(pl.multiple_of(place(k) * rows, 16), rows)
                remotes.append(
                    send(
                        held[w].at[there, pl.ds(col, width)],
                        outs[w].at[:, cols],
                        ssem.at[n, k],
                        rsem.at[n, k],
                        k,
                    )
                )
            here = pl.ds(pl.multiple_of(mine * rows, 16), rows)
            copy = pltpu.make_async_copy(
                held[w].at[here, pl.ds(col, width)], outs[w].at[:, cols], ssem.at[n, 0]
            )
            copy.start()
            remotes.append(copy)
    for copy in remotes:
        copy.wait()


def collect(grads, ident, blocks=1):
    plan = cut([g.shape[1] * PLANE for g in grads], blocks)
    outs = [
        jax.ShapeDtypeStruct((g.shape[0] // PLANE, g.shape[1] * PLANE), g.dtype) for g in grads
    ]
    dma = pltpu.SemaphoreType.DMA
    n = len(plan)
    scratch = [pltpu.VMEM(g.shape, g.dtype) for g in grads]
    return call(
        functools.partial(collect_kernel, plan, len(grads)),
        tuple(grads),
        outs,
        scratch + [dma((len(grads),)), dma((n, PLANE)), dma((n, PLANE))],
        ident,
        8,
        sum(g.size for g in grads) / 3e4,
    )


def flat_place():
    return lax.axis_index("z") * PLANE + lax.axis_index("y") * 4 + lax.axis_index("blk")


def flat_id(d):
    return {"z": lax.div(d, PLANE), "y": lax.rem(lax.div(d, 4), 2), "blk": lax.rem(d, 4)}


def greet_all(count):
    barrier = pltpu.get_barrier_semaphore()
    me = flat_place()

    def one(i, carry):
        pl.semaphore_signal(
            barrier,
            inc=1,
            device_id=flat_id(lax.rem(me + i, count)),
            device_id_type=pl.DeviceIdType.MESH,
        )
        return carry

    lax.fori_loop(1, count, one, 0)
    pl.semaphore_wait(barrier, count - 1)


def to_all(count, source, target, ssem, rsem):
    me = flat_place()

    def copy(i):
        d = lax.rem(me + i, count)
        return pltpu.make_async_remote_copy(
            src_ref=source(d),
            dst_ref=target.at[me],
            send_sem=ssem.at[i],
            recv_sem=rsem.at[i],
            device_id=flat_id(d),
            device_id_type=pl.DeviceIdType.MESH,
        )

    def begin(i, carry):
        copy(i).start()
        return carry

    def finish(i, carry):
        copy(i).wait()
        return carry

    lax.fori_loop(1, count, begin, 0)
    target[me] = source(me)[...]
    lax.fori_loop(1, count, finish, 0)


def exchange_kernel(count, x, o, ssem, rsem):
    greet_all(count)
    to_all(count, lambda d: x.at[d], o, ssem, rsem)


def small_call(kernel, ins, outs, scratch, ident, micros):
    vmem = pl.BlockSpec(memory_space=pltpu.VMEM)
    return pl.pallas_call(
        kernel,
        out_shape=outs,
        in_specs=[vmem] * len(ins),
        out_specs=jax.tree.map(lambda _: vmem, outs),
        scratch_shapes=scratch,
        compiler_params=pltpu.CompilerParams(
            collective_id=ident, has_side_effects=True, vmem_limit_bytes=32 * MIB
        ),
        cost_estimate=pl.CostEstimate(
            flops=0, bytes_accessed=int(micros * 3.6e6), transcendentals=0
        ),
    )(*ins)


def exchange(x, ident):
    dma = pltpu.SemaphoreType.DMA((x.shape[0],))
    return small_call(
        functools.partial(exchange_kernel, x.shape[0]),
        (x,),
        jax.ShapeDtypeStruct(x.shape, x.dtype),
        [dma, dma],
        ident,
        8,
    )


def mods_back_kernel(count, x, w, o, t, got, part, mine, s0, r0, s1, r1, s2, r2):
    greet_all(count)
    to_all(count, lambda d: x.at[d], got, s0, r0)
    groups = o.shape[0]
    for g in range(groups):
        o[g] = got[4 * g] + got[4 * g + 1] + got[4 * g + 2] + got[4 * g + 3]
    own = o[...].reshape(groups * 8, o.shape[2])
    high = own.astype(BF)
    rest = own - high.astype(F32)
    low = rest.astype(BF)
    quarter = w.shape[0] // 4
    for q in range(4):
        piece = w[q * quarter : (q + 1) * quarter, :]
        product = times_t(high, piece) + times_t(low, piece)
        for g in range(groups):
            part[4 * g + q] = product[8 * g : 8 * g + 8]
    to_all(count, lambda d: part.at[d], mine, s1, r1)

    def add(i, total):
        return total + mine[i]

    part[flat_place()] = lax.fori_loop(0, count, add, jnp.zeros(mine.shape[1:], F32))
    to_all(count, lambda d: part.at[flat_place()], t, s2, r2)


def mods_back(x, w, ident):
    count, eight, cols = x.shape
    width = w.shape[0]
    dma = pltpu.SemaphoreType.DMA((count,))
    pieces = jax.ShapeDtypeStruct((count, eight, width // 4), F32)
    return small_call(
        functools.partial(mods_back_kernel, count),
        (x, w),
        (jax.ShapeDtypeStruct((count // 4, eight, cols), F32), pieces),
        [pltpu.VMEM(x.shape, F32), pltpu.VMEM(pieces.shape, F32), pltpu.VMEM(pieces.shape, F32)]
        + [dma] * 6,
        ident,
        20,
    )


def z_gather(x):
    return lax.all_gather(x, "z", axis=0, tiled=True)


def z_scatter(g):
    return lax.psum_scatter(g, "z", scatter_dimension=0, tiled=True)


def z_peer(m):
    z = lax.axis_index("z")
    if m == 1:
        z = z + 1 - 2 * lax.rem(z, 2)
    elif m == 2:
        z = lax.rem(z + 2, 4)
    else:
        z = 3 - z
    return z


def inner_plane():
    z = lax.axis_index("z")
    return (z == 1) | (z == 2)


def outer_plane():
    z = lax.axis_index("z")
    return (z == 0) | (z == 3)


def remote(src, dst, ssem, rsem, where):
    return pltpu.make_async_remote_copy(
        src_ref=src,
        dst_ref=dst,
        send_sem=ssem,
        recv_sem=rsem,
        device_id=where,
        device_id_type=pl.DeviceIdType.MESH,
    )


class OutRows:
    def __init__(self):
        z, j = lax.axis_index("z"), place(0)
        me = z * PLANE + j
        self.slot = lax.rem(me, 4)
        self.user = self.flat(self.slot * PLANE + lax.div(me, 4))
        self.owner = self.flat(4 * j + z)
        self.away, self.home = me != 4 * j + z, me == 4 * j + z

    @staticmethod
    def flat(d):
        return flat_id(d)


def greet_more(outs):
    barrier = pltpu.get_barrier_semaphore()

    def signal(where):
        pl.semaphore_signal(
            barrier, inc=1, device_id=where, device_id_type=pl.DeviceIdType.MESH
        )

    ids = [peer(k) for k in range(1, PLANE)] + [{"z": z_peer(m)} for m in (1, 2, 3)]
    for where in ids:
        signal(where)

    @pl.when(outs.away)
    def _():
        signal(outs.user)
        signal(outs.owner)
        pl.semaphore_wait(barrier, len(ids) + 2)

    pl.when(outs.home)(lambda: pl.semaphore_wait(barrier, len(ids)))


class PlaneCopy:
    shapes = staticmethod(lambda dma: [dma((4,)), dma((4,))])

    def __init__(self, full, sems):
        self.full = full
        self.m = full.shape[0] // 4
        self.ssem, self.rsem = sems

    def copy(self, slot, t, m):
        block = self.full.at[pl.ds(pl.multiple_of(t * self.m, self.m), self.m)]
        return remote(block, block, self.ssem.at[slot], self.rsem.at[slot], {"z": z_peer(m)})

    def begin(self):
        z = lax.axis_index("z")
        self.copy(1, z, 2).start()
        self.copy(0, z, 1).start()
        pl.when(inner_plane())(lambda: self.copy(2, z, 3).start())

    def relay(self):
        @pl.when(inner_plane())
        def _():
            self.copy(1, z_peer(2), 2).wait_recv()
            self.copy(3, z_peer(2), 1).start()

    def finish(self):
        z = lax.axis_index("z")
        self.copy(0, z_peer(1), 1).wait_recv()

        @pl.when(inner_plane())
        def _():
            self.copy(2, z_peer(3), 3).wait_recv()
            self.copy(2, z, 3).wait_send()
            self.copy(3, z_peer(2), 1).wait_send()

        @pl.when(outer_plane())
        def _():
            self.copy(1, z_peer(2), 2).wait_recv()
            self.copy(3, z_peer(3), 1).wait_recv()

        self.copy(0, z, 1).wait_send()
        self.copy(1, z, 2).wait_send()


class PlaneSum:
    @staticmethod
    def shapes(m, c, dma):
        return [pltpu.VMEM((m, c), BF), dma((4,)), dma((4,))]

    def __init__(self, g, landing, scratch, temps):
        self.g, self.landing, self.temps = g, landing, temps
        self.q, self.ssem, self.rsem = scratch
        self.m, self.c = g.shape[1:]
        self.inner, self.outer = inner_plane(), outer_plane()

    def copy(self, src, slot, m):
        return pltpu.make_async_remote_copy(
            src_ref=src,
            dst_ref=self.landing.at[slot],
            send_sem=self.ssem.at[slot],
            recv_sem=self.rsem.at[slot],
            device_id={"z": z_peer(m)},
            device_id_type=pl.DeviceIdType.MESH,
        )

    def begin(self):
        far = self.g.at[z_peer(3)]
        pl.when(self.outer)(lambda: self.copy(far, 2, 1).start())
        pl.when(self.inner)(lambda: self.copy(far, 3, 3).start())

    def temp(self, i):
        return self.temps.at[i, pl.ds(0, self.m), pl.ds(0, self.c)]

    def load(self, src, i):
        copy = pltpu.make_async_copy(src, self.temp(i), self.tsem.at[i])
        copy.start()
        return copy

    def hop(self, tsem):
        self.tsem = tsem
        across = self.g.at[z_peer(2)]

        @pl.when(self.outer)
        def _():
            self.copy(across, 1, 2).start()

        @pl.when(self.inner)
        def _():
            first = self.load(across, 0)
            self.copy(across, 2, 1).wait_recv()
            second = self.load(self.landing.at[2], 1)
            first.wait()
            second.wait()

            def body(r, n):
                r = (pl.ds(r, n), pl.ds(0, self.c))
                total = self.temps[(0,) + r].astype(F32) + self.temps[(1,) + r].astype(F32)
                self.q[r] = total.astype(BF)

            rows_loop(self.m, body)
            self.copy(self.q, 1, 2).start()

        self.near = self.copy(self.g.at[z_peer(1)], 0, 1)
        self.near.start()

    def finish(self, tsem):
        self.tsem = tsem
        loads = [self.load(self.g.at[lax.axis_index("z")], 0)]
        self.near.wait_recv()
        loads.append(self.load(self.landing.at[0], 1))
        far = self.copy(self.q, 1, 2)
        far.wait_recv()
        loads.append(self.load(self.landing.at[1], 2))
        pl.when(self.inner)(lambda: self.copy(self.g.at[0], 3, 3).wait_recv())
        pl.when(self.inner)(lambda: self.load(self.landing.at[3], 3).wait())
        for copy in loads:
            copy.wait()
        far.wait_send()
        self.near.wait_send()
        pl.when(self.outer)(lambda: self.copy(self.g.at[0], 2, 1).wait_send())
        pl.when(self.inner)(lambda: self.copy(self.g.at[0], 3, 3).wait_send())

        def three(r, n):
            r = (pl.ds(r, n), pl.ds(0, self.c))
            total = self.temps[(0,) + r].astype(F32) + self.temps[(1,) + r].astype(F32)
            return r, total + self.temps[(2,) + r].astype(F32)

        def outer(r, n):
            r, total = three(r, n)
            self.q[r] = total.astype(BF)

        def inner(r, n):
            r, total = three(r, n)
            self.q[r] = (total + self.temps[(3,) + r].astype(F32)).astype(BF)

        pl.when(self.outer)(lambda: rows_loop(self.m, outer))
        pl.when(self.inner)(lambda: rows_loop(self.m, inner))


def deal(src, out, blocks, ssem, rsem):
    rows = out.shape[0]
    mine = place(0)
    copies = []
    for n, (_, base, width, col) in enumerate(cut([out.shape[1]], blocks)):
        cols = pl.ds(pl.multiple_of(base + mine * width, 128), width)
        for k in (6, 7, 2, 3, 4, 5, 1, 0):
            there = pl.ds(pl.multiple_of(place(k) * rows, 16), rows)
            piece = src.at[there, pl.ds(col, width)]
            if k:
                copies.append(send(piece, out.at[:, cols], ssem.at[n, k], rsem.at[n, k], k))
            else:
                copies.append(pltpu.make_async_copy(piece, out.at[:, cols], ssem.at[n, 0]))
                copies[-1].start()
    return copies


def pipe(body, steps, ins, outs):
    spec = lambda a: pl.BlockSpec(a[1], a[2])
    pltpu.emit_pipeline(
        body, grid=(steps,), in_specs=[spec(a) for a in ins], out_specs=[spec(a) for a in outs]
    )(*[a[0] for a in ins], *[a[0] for a in outs])


def whole(a):
    return (a, a.shape, lambda i: (0,) * len(a.shape))


def some_rows(a, n, pick=lambda i: i):
    return (a, (n, a.shape[1]), lambda i: (pick(i), 0))


def grads_mm(a, b, g):
    m = g.shape[1]

    def body(a, b, g):
        g[0] = over_rows(a[...], b[...]).astype(BF)

    pipe(
        body,
        g.shape[0],
        [(a, (a.shape[0], m), lambda i: (0, i)), whole(b)],
        [(g, (1,) + g.shape[1:], lambda i: (i, 0, 0))],
    )


def rows_mm(a, b, o, n, steps, pick=lambda i: i, transposed=False):
    def body(a, b, o):
        o[...] = (times_t if transposed else dot)(a[...], b[...]).astype(BF)

    pipe(body, steps, [some_rows(a, n, pick), whole(b)], [some_rows(o, n, pick)])


class Share:
    @staticmethod
    def shapes(w, blocks, dma):
        return [pltpu.VMEM(w, BF), dma, dma((blocks, PLANE)), dma((blocks, PLANE))]

    def __init__(self, w, full, blocks, scratch):
        self.w, self.full, self.blocks = w, full, blocks
        self.held, self.lsem, self.ssem, self.rsem = scratch
        self.load = pltpu.make_async_copy(w, self.held, self.lsem)
        self.load.start()

    def begin(self):
        self.load.wait()
        rows = self.w.shape[0]
        first = lax.axis_index("z") * (PLANE * rows) + place(0) * rows
        here = pl.ds(pl.multiple_of(first, rows), rows)
        self.copies = []
        for n, (_, base, width, col) in enumerate(cut([self.w.shape[1]], self.blocks)):
            dst = self.full.at[here, pl.ds(col, width)]
            for k in (6, 7, 2, 3, 4, 5, 1, 0):
                cols = pl.ds(pl.multiple_of(base + place(k) * width, 128), width)
                src = self.held.at[:, cols]
                if k:
                    copy = send(src, dst, self.ssem.at[n, k], self.rsem.at[n, k], k)
                else:
                    copy = pltpu.make_async_copy(src, dst, self.ssem.at[n, 0])
                    copy.start()
                self.copies.append(copy)

    def finish(self):
        for copy in self.copies:
            copy.wait()


IMAGES = 3


def whole_kernel(factor, names, *refs):
    v = dict(zip(names, refs))
    get = lambda *keys: [v[key] for key in keys]
    group_of = lambda prefix: [v[key] for key in names if key.startswith(prefix + ".")]
    cols, tok, cot, pick, mods = get("cols", "tok", "cot", "pick", "mods")
    first, second, dy, dat = get("first", "second", "dy", "dat")
    qkv, mixed, hid, slope = get("qkv", "mixed", "hid", "slope")
    du, part, part_y, dmix, dqkv = get("du", "part", "part_y", "dmix", "dqkv")
    xh, xv, xg, va, vb, vd = get("xh", "xv", "xg", "va", "vb", "vd")
    block_out, grad_tokens = get("block_out", "grad_tokens")
    acc, img, temps, temps_out, tsem = get("acc", "img", "temps", "temps_out", "tsem")
    rows, width = tok.shape
    tokens = dy.shape[0]
    group = 4 * rows
    z, y, mine = lax.axis_index("z"), lax.axis_index("y"), place(0)
    odd, even = (lambda i: 2 * i + 1), (lambda i: 2 * i)
    outs = OutRows()

    qkv_in = Share(v["qkv_w"], v["full_qkv"], 3, group_of("in_qkv"))
    up_in = Share(v["up_w"], v["full_up"], 1, group_of("in_up"))
    down_in = Share(v["down_w"], v["full_down"], 1, group_of("in_down"))
    held, lsem, osems, rsems = group_of("in_out")
    out_load = pltpu.make_async_copy(v["out_w"], held, lsem)
    out_load.start()
    out_block = v["out_w"].shape[0]
    full_out = v["full_out"]
    out_at = lambda i: full_out.at[pl.ds(pl.multiple_of(i * out_block, out_block), out_block)]
    out_in = remote(held, out_at(outs.slot), osems.at[0], rsems.at[0], outs.user)
    out_local = pltpu.make_async_copy(held, out_at(z), osems.at[0])
    greet_more(outs)

    ma, mb = get("ma", "mb")
    sa, ra, sb, rb = group_of("mod_in")
    sent = []
    for m in (1, 2, 3):
        src = cols.at[pl.ds(2 * z_peer(m), 2)]
        sent.append(remote(src, ma.at[z], sa.at[m], ra.at[m], {"z": z_peer(m)}))
        sent[-1].start()
    qkv_in.begin()
    out_load.wait()
    pl.when(outs.away)(lambda: out_in.start())
    pl.when(outs.home)(lambda: out_local.start())
    ma[z] = cols[pl.ds(2 * z, 2)]
    for copy in sent:
        copy.wait()
    sent = []
    for k in range(1, PLANE):
        src = ma.at[:, peer(k)["y"]]
        sent.append(send(src, mb.at[mine], sb.at[k], rb.at[k], k))
    mb[mine] = ma[:, y]
    for copy in sent:
        copy.wait()
    each = cols.shape[2]
    for d in range(4 * PLANE):
        mods[:, d * each : (d + 1) * each] = mb[d % PLANE, d // PLANE]

    qkv_in.finish()
    z_qkv = PlaneCopy(v["full_qkv"], group_of("z_qkv"))
    z_qkv.begin()

    def picker(r):
        hot = pick[r, 0:128]
        ones = [hot[:, i : i + 1].astype(F32) for i in range(IMAGES)]

        def mod(which):
            at = slice(which * width, (which + 1) * width)
            return sum(ones[i] * mods[i : i + 1, at] for i in range(IMAGES))

        return ones, mod

    def normed_of(x):
        inv = lax.rsqrt(jnp.mean(x * x, axis=-1, keepdims=True) + EPS)
        return inv, x * inv

    def norm_grad(inv, normed, d_normed):
        slant = jnp.mean(d_normed * normed, axis=-1, keepdims=True)
        return inv * (d_normed - normed * slant)

    def make_first(r, n):
        r = pl.ds(r, n)
        _, mod = picker(r)
        _, normed = normed_of(tok[r, :].astype(F32))
        xh[r, 0:width] = (normed * (1.0 + mod(1)) + mod(0)).astype(BF)
        xh[r, width:] = pick[r, :]
        xg[r, :] = (mod(5) * cot[r, :].astype(F32)).astype(BF)

    rows_loop(rows, make_first)
    to_first = Gather(xh, first, group_of("ga"))
    to_first.begin()
    up_in.begin()
    pl.when(outs.away)(lambda: out_in.wait())
    pl.when(outs.home)(lambda: out_local.wait())
    z_out = PlaneCopy(full_out, group_of("z_out"))
    z_out.begin()
    to_first.relay()
    to_first.finish()
    down_in.begin()
    up_in.finish()
    z_qkv.relay()
    z_out.relay()
    z_up = PlaneCopy(v["full_up"], group_of("z_up"))
    z_up.begin()
    z_qkv.finish()

    n = math.gcd(tokens, 256)

    def mm_body(a, b, o):
        o[...] = dot(a[...], b[...]).astype(BF)

    pipe(mm_body, tokens // n, [some_rows(first.at[:, 0:width], n), whole(v["full_qkv"])], [some_rows(qkv, n)])
    masks = [
        some_rows(first.at[:, width : width + 128], group),
        some_rows(first.at[:, width + 128 : width + 256], group),
    ]
    pipe(
        functools.partial(attend_kernel, factor),
        2,
        [some_rows(qkv, group)] + masks,
        [some_rows(mixed, group)],
    )
    down_in.finish()
    z_out.finish()
    rows_mm(mixed, full_out, part, rows, 4, odd)
    r_attn = Scatter(part, va, group_of("sc_a") + group_of("sems_1"))
    r_attn.begin()
    rows_mm(mixed, full_out, part, rows, 4, even)
    r_attn.load()
    r_attn.middle()
    z_down = PlaneCopy(v["full_down"], group_of("z_down"))
    z_down.begin()
    r_attn.relay()
    r_attn.finish()

    def make_second(r, n):
        r = pl.ds(r, n)
        _, mod = picker(r)
        x = tok[r, :].astype(F32) + mod(2) * va[r, :]
        vd[r, :] = x
        xv[r, :] = (normed_of(x)[1] * (1.0 + mod(4)) + mod(3)).astype(BF)

    rows_loop(rows, make_second)
    z_up.relay()
    to_second = Gather(xv, second, group_of("gb"))
    to_second.begin()
    to_second.relay()
    to_second.finish()
    to_dy = Gather(xg, dy, group_of("gc"))
    to_dy.begin()
    z_up.finish()

    def up_body(a, b, h, s):
        u = dot(a[...], b[...])
        c = math.sqrt(2.0 / math.pi)
        t = jnp.tanh(c * (u + 0.044715 * (u * u * u)))
        h[...] = (0.5 * u * (1.0 + t)).astype(BF)
        inside = c * (1.0 + (3 * 0.044715) * (u * u))
        s[...] = 0.5 * (1.0 + t) + 0.5 * u * (1.0 - t * t) * inside

    pipe(
        up_body,
        tokens // n,
        [some_rows(second, n), whole(v["full_up"])],
        [some_rows(hid, n), some_rows(slope, n)],
    )
    to_dy.relay()
    to_dy.finish()
    z_down.relay()
    sums = [
        PlaneSum(v["g_" + key], v["land_" + key], group_of("s_" + key), t)
        for key, t in (("down", temps), ("up", temps), ("qkv", temps), ("out", temps_out))
    ]
    s_down, s_up, s_qkv, s_out = sums
    grads_mm(dy, hid, v["g_down"])
    s_down.begin()
    z_down.finish()

    def du_body(a, b, s, o):
        o[...] = (dot(a[...], b[...]) * s[...]).astype(BF)

    pipe(
        du_body,
        tokens // n,
        [some_rows(dy, n), whole(v["full_down"]), some_rows(slope, n)],
        [some_rows(du, n)],
    )
    rows_mm(du, v["full_up"], part, rows, 4, odd, True)
    r_e2 = Scatter(part, vb, group_of("sc_a") + group_of("sems_2"))
    r_e2.begin()
    rows_mm(du, v["full_up"], part, rows, 4, even, True)
    s_down.hop(tsem)
    r_e2.load()
    r_e2.middle()
    grads_mm(second, du, v["g_up"])
    s_up.begin()
    r_e2.relay()
    r_e2.finish()

    def clear():
        acc[...] = jnp.zeros_like(acc)

    def tally(ones, which, value):
        for i in range(IMAGES):
            acc[which, i] += ones[i] * value

    def flush(blocks):
        for q, which in enumerate(blocks):
            for i in range(IMAGES):
                at = slice(which * width, (which + 1) * width)
                img[i : i + 1, at] = jnp.sum(acc[q, i], axis=0, keepdims=True)

    clear()

    def norm_back(r, n):
        r = pl.ds(r, n)
        ones, mod = picker(r)
        inv, normed = normed_of(vd[r, :])
        e = vb[r, :]
        d_mid = cot[r, :].astype(F32) + norm_grad(inv, normed, e * (1.0 + mod(4)))
        grad_tokens[r, :] = d_mid
        xv[r, :] = (mod(2) * d_mid).astype(BF)
        tally(ones, 0, e)
        tally(ones, 1, e * normed)
        tally(ones, 2, d_mid * va[r, :])

    rows_loop(rows, norm_back)
    to_dat = Gather(xv, dat, group_of("gd"))
    to_dat.begin()
    flush((3, 4, 2))
    rows_mm(hid, v["full_down"], part_y, rows, 8, transposed=True)
    to_dat.relay()
    s_up.hop(tsem)
    to_dat.finish()
    r_y = Scatter(part_y, va, group_of("sc_b") + group_of("sems_3"))
    r_y.begin()
    r_y.load()
    rows_mm(dat, full_out, dmix, 2 * rows, 4, transposed=True)
    r_y.middle()
    pipe(
        functools.partial(attend_back_kernel, factor),
        2,
        [some_rows(qkv, group)] + masks + [some_rows(dmix, group)],
        [some_rows(dqkv, group)],
    )
    r_y.relay()
    grads_mm(first.at[:, 0:width], dqkv, v["g_qkv"])
    s_qkv.begin()

    def out_body(a, b, g):
        g[...] = over_rows(a[...], b[...]).astype(BF).reshape(g.shape)

    step = math.gcd(width, 512)
    g_out = v["g_out"]
    pipe(
        out_body,
        width // step,
        [whole(mixed), (dat, (tokens, step), lambda i: (0, i))],
        [(g_out, g_out.shape[:2] + (step,), lambda i: (0, 0, i))],
    )
    s_out.begin()
    r_y.finish()
    rows_mm(dqkv, v["full_qkv"], part, rows, 4, odd, True)
    r_e1 = Scatter(part, vb, group_of("sc_a") + group_of("sems_4"))
    r_e1.begin()
    rows_mm(dqkv, v["full_qkv"], part, rows, 4, even, True)
    r_e1.load()
    r_e1.middle()
    s_qkv.hop(tsem)
    s_out.hop(tsem)
    r_e1.relay()
    r_e1.finish()
    clear()

    def last_norm(r, n):
        r = pl.ds(r, n)
        ones, mod = picker(r)
        inv, normed = normed_of(tok[r, :].astype(F32))
        e, out = vb[r, :], va[r, :]
        grad_tokens[r, :] += norm_grad(inv, normed, e * (1.0 + mod(1)))
        block_out[r, :] = (vd[r, :] + mod(5) * out).astype(BF)
        tally(ones, 0, e)
        tally(ones, 1, e * normed)
        tally(ones, 2, cot[r, :].astype(F32) * out)

    rows_loop(rows, last_norm)
    flush((0, 1, 5))

    pa, ga, gs, gb, pc, pd, pe, ts = get("pa", "ga_", "gs", "gb_", "pc", "pd", "pe", "ts")
    w, t_all, dm = get("mod_w", "t_all", "dm")
    sems = group_of("mod_out")
    load_w = pltpu.make_async_copy(v["mod_w_in"], w, sems[10].at[0])
    load_w.start()
    for d in range(4 * PLANE):
        pa[d % PLANE, d // PLANE] = img[:, d * each : (d + 1) * each]
    plane_sent = lambda src, dst, s, r: [
        send(src(k), dst, s.at[k], r.at[k], k) for k in range(1, PLANE)
    ]
    sent = plane_sent(lambda k: pa.at[place(k)], ga.at[mine], sems[0], sems[1])
    ga[mine] = pa[mine]
    dealt = []
    deal_sems = group_of("deal")

    def settle(s, out, blocks, sems):
        s.finish(tsem)
        dealt.extend(deal(s.q, out, blocks, *sems))

    settle(s_down, v["c_down"], 1, deal_sems[:2])
    for copy in sent:
        copy.wait()
    for g in range(2):
        gs[:, g] = ga[4 * g] + ga[4 * g + 1] + ga[4 * g + 2] + ga[4 * g + 3]
    sent = []
    for m in (1, 2, 3):
        copy = remote(
            gs.at[z_peer(m)], gb.at[z], sems[2].at[m], sems[3].at[m], {"z": z_peer(m)}
        )
        copy.start()
        sent.append(copy)
    gb[z] = gs[z]
    settle(s_up, v["c_up"], 1, deal_sems[2:4])
    s_out.finish(tsem)
    back = remote(s_out.q, v["c_out"], tsem.at[4], tsem.at[5], outs.owner)
    back_local = pltpu.make_async_copy(s_out.q, v["c_out"], tsem.at[4])
    pl.when(outs.away)(lambda: back.start())
    pl.when(outs.home)(lambda: back_local.start())
    for copy in sent:
        copy.wait()
    load_w.wait()
    for t in range(4):
        for g in range(2):
            dm[2 * t + g] = gb[t, g]
    own = dm[...].reshape(8 * 8, each)
    high = own.astype(BF)
    low = (own - high.astype(F32)).astype(BF)
    slice_of = width // PLANE
    for k in range(PLANE):
        piece = w[k * slice_of : (k + 1) * slice_of, :]
        pc[k] = times_t(high, piece) + times_t(low, piece)
    sent = plane_sent(lambda k: pc.at[place(k)], pd.at[mine], sems[4], sems[5])
    pd[mine] = pc[mine]
    settle(s_qkv, v["c_qkv"], 3, deal_sems[4:6])
    for copy in sent:
        copy.wait()
    total = pd[0]
    for k in range(1, PLANE):
        total = total + pd[k]
    pe[z] = total
    sent = []
    for m in (1, 2, 3):
        copy = remote(pe.at[z], pe.at[z], sems[6].at[m], sems[7].at[m], {"z": z_peer(m)})
        copy.start()
        sent.append(copy)
    for copy in sent:
        copy.wait()
    ts[...] = pe[0] + pe[1] + pe[2] + pe[3]
    sent = plane_sent(lambda k: ts, t_all.at[mine], sems[8], sems[9])
    t_all[mine] = ts[...]
    for copy in sent:
        copy.wait()
    for copy in dealt:
        copy.wait()
    pl.when(outs.away)(lambda: back.wait())
    pl.when(outs.home)(lambda: back_local.wait())


def whole_block(cols, tok, cot, pick, mod_w, qkv_w, out_w, up_w, down_w, factor, ident):
    rows, width = tok.shape
    nz, tokens = 4, PLANE * rows
    share = qkv_w.shape[0]
    m = share * PLANE
    wide, part, heads = up_w.shape[1] // PLANE, qkv_w.shape[1] // PLANE, nz * out_w.shape[0]
    each = cols.shape[2]
    struct, vm, dma = jax.ShapeDtypeStruct, pltpu.VMEM, pltpu.SemaphoreType.DMA
    vmem = pl.BlockSpec(memory_space=pltpu.VMEM)
    anywhere = pl.BlockSpec(memory_space=pl.ANY)
    ins = dict(cols=cols, tok=tok, cot=cot, pick=pick)
    far_ins = dict(mod_w_in=mod_w, qkv_w=qkv_w, out_w=out_w, up_w=up_w, down_w=down_w)
    near = dict(
        block_out=struct((rows, width), BF),
        grad_tokens=struct((rows, width), F32),
        dm=struct(cols.shape, F32),
        t_all=struct((PLANE, 64, width // PLANE), F32),
    )
    far = dict(
        c_down=struct((share, wide * PLANE), BF),
        c_up=struct((share, wide * PLANE), BF),
        c_qkv=struct((share, part * PLANE), BF),
        c_out=struct((heads // nz, width), BF),
        full_qkv=struct((nz * m, part), BF),
        full_out=struct((heads, width), BF),
        full_up=struct((nz * m, wide), BF),
        full_down=struct((nz * m, wide), BF),
        first=struct((tokens, width + 256), BF),
        second=struct((tokens, width), BF),
        dy=struct((tokens, width), BF),
        dat=struct((tokens, width), BF),
        qkv=struct((tokens, part), BF),
        mixed=struct((tokens, heads), BF),
        hid=struct((tokens, wide), BF),
        slope=struct((tokens, wide), F32),
        du=struct((tokens, wide), BF),
        part=struct((tokens, width), BF),
        part_y=struct((tokens, width), BF),
        dmix=struct((tokens, heads), BF),
        dqkv=struct((tokens, part), BF),
    )
    shapes = dict(
        down=(nz, m, wide), up=(nz, m, wide), qkv=(nz, m, part), out=(nz, heads // nz, width)
    )
    for key, shape in shapes.items():
        far["g_" + key] = struct(shape, BF)
        far["land_" + key] = struct(shape, BF)
    own = vm((rows, width), F32)
    scratch = dict(
        mods=vm((8, 6 * width), F32),
        img=vm((8, 6 * width), F32),
        ma=vm((nz, 2, 8, each), F32),
        mb=vm((PLANE, nz, 8, each), F32),
        xh=vm((rows, width + 256), BF),
        xv=vm((rows, width), BF),
        xg=vm((rows, width), BF),
        va=own,
        vb=own,
        vd=own,
        acc=vm((3, IMAGES, 16, width), F32),
        temps=vm((4, m, max(wide, part)), BF),
        temps_out=vm((4,) + shapes["out"][1:], BF),
        tsem=dma((6,)),
        mod_w=vm(mod_w.shape, BF),
        pa=vm((PLANE, nz, 8, each), F32),
        ga_=vm((PLANE, nz, 8, each), F32),
        gs=vm((nz, 2, 8, each), F32),
        gb_=vm((nz, 2, 8, each), F32),
        pc=vm((PLANE, 64, width // PLANE), F32),
        pd=vm((PLANE, 64, width // PLANE), F32),
        pe=vm((nz, 64, width // PLANE), F32),
        ts=vm((64, width // PLANE), F32),
    )

    def add(prefix, items):
        for i, item in enumerate(items):
            scratch[prefix + "." + str(i)] = item

    add("in_qkv", Share.shapes(qkv_w.shape, 3, dma))
    add("in_up", Share.shapes(up_w.shape, 1, dma))
    add("in_down", Share.shapes(down_w.shape, 1, dma))
    add("in_out", [vm(out_w.shape, BF), dma, dma((1,)), dma((1,))])
    add("mod_in", [dma((4,)), dma((4,)), dma((PLANE,)), dma((PLANE,))])
    add("mod_out", [dma((PLANE,))] * 10 + [dma((1,))])
    for key in ("ga", "gb", "gc", "gd"):
        add(key, Gather.shapes(dma))
    sc = Scatter.shapes(rows, width, dma)
    add("sc_a", sc[:8])
    add("sc_b", sc[:8])
    for i in range(1, 5):
        add("sems_" + str(i), sc[8:])
    for key, shape in shapes.items():
        add("z_" + key, PlaneCopy.shapes(dma))
        add("s_" + key, PlaneSum.shapes(shape[1], shape[2], dma))
    add("deal", [dma((b, PLANE)) for b in (1, 1, 1, 1, 3, 3)])
    names = list(ins) + list(far_ins) + list(near) + list(far) + list(scratch)
    outs = pl.pallas_call(
        functools.partial(whole_kernel, factor, names),
        out_shape=list(near.values()) + list(far.values()),
        in_specs=[vmem] * len(ins) + [anywhere] * len(far_ins),
        out_specs=[vmem] * len(near) + [anywhere] * len(far),
        scratch_shapes=list(scratch.values()),
        compiler_params=pltpu.CompilerParams(
            collective_id=ident, has_side_effects=True, vmem_limit_bytes=62 * MIB
        ),
        cost_estimate=pl.CostEstimate(
            flops=0, bytes_accessed=int(450 * 3.6e6), transcendentals=0
        ),
    )(*ins.values(), *far_ins.values())
    return dict(zip(list(near) + list(far), outs))


def norm_mod(value, shift, scale):
    normed = value * lax.rsqrt(jnp.mean(value * value, axis=-1, keepdims=True) + EPS)
    return normed * (1.0 + scale) + shift


def dot(a, b):
    return jnp.dot(a, b, preferred_element_type=F32)


def over_rows(left, right):
    return lax.dot_general(left, right, (((0,), (0,)), ((), ())), preferred_element_type=F32)


def times_t(left, right):
    return lax.dot_general(left, right, (((1,), (1,)), ((), ())), preferred_element_type=F32)


def allowed_pairs(seg, key, r):
    same = times_t(seg[r, :], key[...]) > 0.5
    rows = lax.broadcasted_iota(jnp.int32, same.shape, 0) + r.start
    return same | (rows == lax.broadcasted_iota(jnp.int32, same.shape, 1))


def softmax_rows(q, k, allowed, factor):
    scores = jnp.where(allowed, times_t(q, k) * factor, NEG)
    expo = jnp.exp(scores - jnp.max(scores, axis=-1, keepdims=True))
    return expo / jnp.sum(expo, axis=-1, keepdims=True)


def row_blocks(count):
    step = math.gcd(count, 256)
    return [slice(i, i + step) for i in range(0, count, step)]


def attend_kernel(factor, qkv, seg, key, o):
    n = o.shape[1]
    for r in row_blocks(o.shape[0]):
        allowed = allowed_pairs(seg, key, r)
        for c in range(0, n, HEAD_DIM):
            k = qkv[:, n + c : n + c + HEAD_DIM]
            v = qkv[:, 2 * n + c : 2 * n + c + HEAD_DIM]
            prob = softmax_rows(qkv[r, c : c + HEAD_DIM], k, allowed, factor)
            o[r, c : c + HEAD_DIM] = dot(prob.astype(BF), v).astype(BF)


def attend_back_kernel(factor, qkv, seg, key, d_o, d_qkv):
    n = d_o.shape[1]
    for c in range(0, n, HEAD_DIM):
        k = qkv[:, n + c : n + c + HEAD_DIM]
        v = qkv[:, 2 * n + c : 2 * n + c + HEAD_DIM]
        dk = dv = 0.0
        for r in row_blocks(d_o.shape[0]):
            q = qkv[r, c : c + HEAD_DIM]
            out = d_o[r, c : c + HEAD_DIM]
            prob = softmax_rows(q, k, allowed_pairs(seg, key, r), factor)
            d_prob = times_t(out, v)
            delta = jnp.sum(prob * d_prob, axis=-1, keepdims=True)
            d_scores = (prob * (d_prob - delta)).astype(BF)
            d_qkv[r, c : c + HEAD_DIM] = (dot(d_scores, k) * factor).astype(BF)
            dk = dk + over_rows(d_scores, q)
            dv = dv + over_rows(prob.astype(BF), out)
        d_qkv[:, n + c : n + c + HEAD_DIM] = (dk * factor).astype(BF)
        d_qkv[:, 2 * n + c : 2 * n + c + HEAD_DIM] = dv.astype(BF)


def per_group(kernel, qkv, first, d_o, columns, group, flops):
    last = first.shape[1] // 128
    block = lambda c: pl.BlockSpec((group, c), lambda i: (i, 0))
    mask = lambda c: pl.BlockSpec((group, 128), lambda i: (i, c))
    return pl.pallas_call(
        kernel,
        grid=(qkv.shape[0] // group,),
        out_shape=jax.ShapeDtypeStruct((qkv.shape[0], columns), BF),
        in_specs=[block(qkv.shape[1]), mask(last - 2), mask(last - 1)]
        + [block(a.shape[1]) for a in d_o],
        out_specs=block(columns),
        compiler_params=pltpu.CompilerParams(vmem_limit_bytes=48 * MIB),
        cost_estimate=pl.CostEstimate(flops=flops, bytes_accessed=0, transcendentals=0),
    )(qkv, first, first, *d_o)


def after(value, *others):
    return lax.optimization_barrier((value,) + others)[0]


def on_device(
    tokens,
    noise_table,
    mod_weight,
    qkv_weight,
    out_weight,
    up_weight,
    down_weight,
    segment,
    key_valid,
    noise_level,
    cotangent,
):
    rows, width = tokens.shape[1:]
    images = noise_level.shape[1]
    nz = lax.axis_size("z")
    blk = lax.axis_index("blk")
    groups = 2 * nz
    factor = 1.0 / math.sqrt(HEAD_DIM)
    levels = noise_level.reshape(-1)
    cond = jnp.take(noise_table, levels, axis=0)
    cols = dot(cond, mod_weight).reshape(groups, images, -1)
    cols = jnp.pad(cols, ((0, 0), (0, 8 - images), (0, 0)))

    own = lambda a: lax.dynamic_slice_in_dim(a[0], blk * rows, rows, 0)[:, None]
    lane = jnp.arange(256, dtype=jnp.int32)[None, :]
    hot = (own(segment) == lane % 128) & ((lane < 128) | (own(key_valid) == 1))
    pick = hot.astype(BF)

    args = (tokens[0], cotangent[0], pick, mod_weight)
    weights = (qkv_weight, out_weight, up_weight, down_weight)
    run = on_four_planes if nz == 4 else on_any_planes
    out = run(cols, *args, *weights, factor, images)
    block_out, grad_tokens, mod_grads, cond_grads, d_qkv_w, d_outp, d_up, d_down = out
    grad_mod = lax.dot_general(
        cond.astype(F32), mod_grads, (((0,), (0,)), ((), ())), precision=HIGH
    )
    grad_table = jax.ops.segment_sum(cond_grads, levels, num_segments=noise_table.shape[0])
    return (
        block_out[None],
        grad_tokens[None],
        grad_table,
        grad_mod,
        d_qkv_w.astype(F32),
        d_outp.astype(F32),
        d_up.astype(F32),
        d_down.astype(F32),
    )


def on_four_planes(
    cols, tok, cot, pick, mod_weight, qkv_weight, out_weight, up_weight, down_weight, factor, images
):
    out = whole_block(
        cols,
        tok,
        cot,
        pick,
        mod_weight,
        qkv_weight,
        out_weight,
        up_weight,
        down_weight,
        factor,
        1,
    )
    count, width = cols.shape[0] * images, tok.shape[1]
    mod_grads = out["dm"][:, :images].reshape(count, -1)
    cond_grads = out["t_all"].reshape(PLANE, -1, 8, width // PLANE)[:, :, :images]
    cond_grads = cond_grads.transpose(1, 2, 0, 3).reshape(count, width)
    return (
        out["block_out"],
        out["grad_tokens"],
        mod_grads,
        cond_grads,
        out["c_qkv"],
        out["c_out"],
        out["c_up"],
        out["c_down"],
    )


def on_any_planes(
    cols, tok, cot, pick, mod_weight, qkv_weight, out_weight, up_weight, down_weight, factor, images
):
    rows, width = tok.shape
    nz, blks = lax.axis_size("z"), lax.axis_size("blk")
    devices = nz * PLANE
    group = rows * blks
    own_cols = HEADS // PLANE * HEAD_DIM
    sent = jnp.broadcast_to(cols[:, None], (2 * nz, blks) + cols.shape[1:])
    mods = exchange(sent.reshape((devices,) + cols.shape[1:]), 14)[:, :images]
    mods = mods.transpose(1, 0, 2).reshape(images, 6, width)

    (qkv_part,) = spread([after(qkv_weight, mods)], 1, blocks=3)
    qkv_w = z_gather(qkv_part)
    move = [(nz * k + i, i * PLANE + k) for k in range(PLANE) for i in range(nz)]
    outp = lax.ppermute(after(out_weight, qkv_part), ALL, move)

    picker = pick[:, :images].astype(F32)
    shift1, scale1, gate1, shift2, scale2, gate2 = (
        jnp.dot(picker, mods[:, i], precision=HIGH) for i in range(6)
    )
    x_in, grad_in = tok.astype(F32), cot.astype(F32)
    first_f, first_back = jax.vjp(norm_mod, x_in, shift1, scale1)
    first = jnp.concatenate([first_f.astype(BF), pick], axis=1)
    first_all = plane_gather(after(first, qkv_part), 2)
    first = first_all[:, :width]
    up_part, down_part = spread([after(up_weight, first), down_weight], 3)
    outp_w, up_w, down_w = z_gather(outp), z_gather(up_part), z_gather(down_part)

    qkv = dot(first, qkv_w).astype(BF)
    cost = 4 * 2 * group * group * own_cols
    mixed = per_group(
        functools.partial(attend_kernel, factor), qkv, first_all, [], own_cols, group, 5 * cost
    )
    attn = plane_scatter(dot(mixed, outp_w).astype(BF), 6)
    x_mid = x_in + gate1 * attn
    second_f, second_back = jax.vjp(norm_mod, x_mid, shift2, scale2)
    second = plane_gather(second_f.astype(BF), 7)
    hidden_f, gelu_back = jax.vjp(jax.nn.gelu, dot(second, up_w))
    hidden = hidden_f.astype(BF)

    d_branch = plane_gather(after((gate2 * grad_in).astype(BF), hidden), 5)
    d_down = z_scatter(over_rows(d_branch, hidden).astype(BF))
    d_pre = gelu_back(dot(d_branch, down_w))[0].astype(BF)
    d_up = z_scatter(over_rows(second, d_pre).astype(BF))
    d_second = plane_scatter(times_t(d_pre, up_w).astype(BF), 9)
    d_mid_norm, d_shift2, d_scale2 = second_back(d_second)
    d_mid = grad_in + d_mid_norm
    d_gate1 = d_mid * attn
    d_attn = plane_gather((gate1 * d_mid).astype(BF), 10)
    d_mixed = times_t(d_attn, outp_w).astype(BF)
    d_qkv = per_group(
        functools.partial(attend_back_kernel, factor),
        qkv,
        first_all,
        [d_mixed],
        3 * own_cols,
        group,
        10 * cost,
    )
    d_qkv_w = z_scatter(over_rows(first, d_qkv).astype(BF))
    d_outp = z_scatter(over_rows(mixed, d_attn).astype(BF))
    d_first = plane_scatter(times_t(d_qkv, qkv_w).astype(BF), 11)
    d_in_norm, d_shift1, d_scale1 = first_back(d_first)
    part = times_t(after(hidden, d_first), down_w).astype(BF)
    branch = plane_scatter(part, 8)
    block_out = (x_mid + gate2 * branch).astype(BF)
    d_gate2 = grad_in * branch

    tok_grads = jnp.concatenate([d_shift1, d_scale1, d_gate1, d_shift2, d_scale2, d_gate2], axis=1)
    image_grads = lax.dot_general(
        pick[:, :8].astype(F32), tok_grads, (((0,), (0,)), ((), ())), precision=HIGH
    )
    sent = image_grads.reshape(8, devices, -1).transpose(1, 0, 2)
    mod_grads, cond_grads = mods_back(sent, mod_weight, 15)
    count = 2 * nz * images
    mod_grads = mod_grads[:, :images].reshape(count, -1)
    cond_grads = cond_grads.reshape(2 * nz, 4, 8, width // 4)[:, :, :images]
    cond_grads = cond_grads.transpose(0, 2, 1, 3).reshape(count, width)

    d_up, d_down = collect([after(d_up, sent), d_down], 12)
    (d_qkv_w,) = collect([after(d_qkv_w, d_up)], 13, blocks=3)
    d_outp = lax.ppermute(d_outp, ALL, [(b, a) for a, b in move])
    grads = (d_qkv_w, d_outp, d_up, d_down)
    return (block_out, d_mid + d_in_norm, mod_grads, cond_grads) + grads


def solution(mesh):
    groups, blks = mesh.shape["dp"], mesh.shape["blk"]
    planes = Mesh(mesh.devices.reshape(groups // 2, 2, blks), ALL)
    dp = ("z", "y")
    whole = ("z", "y", "blk")
    placed = (
        P(dp, "blk", None),
        P(),
        P(None, whole),
        P(whole, None),
        P(whole, None),
        P(whole, None),
        P(whole, None),
        P(dp, None),
        P(dp, None),
        P(),
        P(dp, "blk", None),
    )
    return jax.shard_map(
        on_device,
        mesh=planes,
        in_specs=placed,
        out_specs=(
            P(dp, "blk", None),
            P(dp, "blk", None),
            P(),
            P(None, whole),
            P(whole, None),
            P(whole, None),
            P(whole, None),
            P(whole, None),
        ),
        check_vma=False,
    )
```

```python
import functools
import math

import jax
import jax.numpy as jnp
from jax import lax
from jax.experimental import pallas as pl
from jax.experimental.pallas import tpu as pltpu
from jax.sharding import Mesh
from jax.sharding import PartitionSpec as P

HEADS = 16
HEAD_DIM = 128
EPS = 1e-06
NEG = -1e30
HIGH = lax.Precision.HIGHEST
PLANE = 8
BF = jnp.bfloat16
F32 = jnp.float32
ALL = ("z", "y", "blk")
MIB = 1 << 20


def peer(k):
    y, b = lax.axis_index("y"), lax.axis_index("blk")
    high, low = lax.div(b, 2), lax.rem(b, 2)
    if k & 4:
        y = 1 - y
    if k & 2:
        high = 1 - high
    if k & 1:
        low = 1 - low
    return {"y": y, "blk": high * 2 + low}


def place(k):
    where = peer(k)
    return where["y"] * 4 + where["blk"]


def greet(peers):
    barrier = pltpu.get_barrier_semaphore()
    for k in peers:
        pl.semaphore_signal(
            barrier, inc=1, device_id=peer(k), device_id_type=pl.DeviceIdType.MESH
        )
    pl.semaphore_wait(barrier, len(peers))


def send(src, dst, ssem, rsem, k):
    copy = pltpu.make_async_remote_copy(
        src_ref=src,
        dst_ref=dst,
        send_sem=ssem,
        recv_sem=rsem,
        device_id=peer(k),
        device_id_type=pl.DeviceIdType.MESH,
    )
    copy.start()
    return copy


def call(kernel, ins, outs, scratch, ident, vmem=16, micros=10):
    return pl.pallas_call(
        kernel,
        out_shape=outs,
        in_specs=[pl.BlockSpec(memory_space=pl.ANY)] * len(ins),
        out_specs=jax.tree.map(lambda _: pl.BlockSpec(memory_space=pl.ANY), outs),
        scratch_shapes=scratch,
        compiler_params=pltpu.CompilerParams(
            collective_id=ident, has_side_effects=True, vmem_limit_bytes=vmem * MIB
        ),
        cost_estimate=pl.CostEstimate(
            flops=0, bytes_accessed=int(micros * 3.6e6), transcendentals=0
        ),
    )(*ins)


class Gather:
    shapes = staticmethod(lambda dma: [dma((1,)), dma((13,)), dma((13,))])

    def __init__(self, xv, o, sems):
        self.xv, self.o = xv, o
        self.lsem, self.ssem, self.rsem = sems
        self.rows = xv.shape[0]
        self.all = []

    def block(self, k, part=None):
        half = self.rows // 2
        first = k * self.rows + (half if part == 1 else 0)
        return self.o.at[pl.ds(first, self.rows if part is None else half)]

    def mine(self, part):
        half = self.rows // 2
        return self.xv.at[pl.ds(part * half, half)]

    def go(self, src, dst, k):
        i = len(self.all)
        self.all.append(send(src, dst, self.ssem.at[i], self.rsem.at[i], k))
        return self.all[-1]

    def begin(self):
        self.x_bot = self.go(self.mine(1), self.block(2, 1), 2)
        self.y_top = self.go(self.mine(0), self.block(4, 0), 4)
        self.x_top = self.go(self.mine(0), self.block(2, 0), 2)
        self.y_bot = self.go(self.mine(1), self.block(4, 1), 4)
        self.sib = self.go(self.xv, self.block(1), 1)
        self.own = pltpu.make_async_copy(self.xv, self.block(0), self.lsem.at[0])
        self.own.start()

    def relay(self):
        self.x_bot.wait_recv()
        self.dy = self.go(self.block(2, 1), self.block(6, 1), 4)
        self.late = [self.go(self.block(2, 1), self.block(3, 1), 1)]
        self.y_top.wait_recv()
        self.dx = self.go(self.block(4, 0), self.block(6, 0), 2)
        self.late.append(self.go(self.block(4, 0), self.block(5, 0), 1))

    def finish(self):
        self.x_top.wait_recv()
        self.late.append(self.go(self.block(2, 0), self.block(3, 0), 1))
        self.y_bot.wait_recv()
        self.late.append(self.go(self.block(4, 1), self.block(5, 1), 1))
        self.dx.wait_recv()
        self.late.append(self.go(self.block(6, 0), self.block(7, 0), 1))
        self.dy.wait_recv()
        self.late.append(self.go(self.block(6, 1), self.block(7, 1), 1))
        for copy in [self.sib] + self.late:
            copy.wait_recv()
        for copy in self.all:
            copy.wait_send()
        self.own.wait()


def gather_kernel(x, o, xv, load_sem, *sems):
    load = pltpu.make_async_copy(x, xv, load_sem)
    load.start()
    greet((1, 2, 4))
    load.wait()
    gather = Gather(xv, o, sems)
    gather.begin()
    gather.relay()
    gather.finish()


def plane_gather(x, ident):
    out = jax.ShapeDtypeStruct((PLANE * x.shape[0],) + x.shape[1:], x.dtype)
    dma = pltpu.SemaphoreType.DMA
    scratch = [pltpu.VMEM(x.shape, x.dtype), dma] + Gather.shapes(dma)
    return call(gather_kernel, (x,), out, scratch, ident, 8, 30)


def rows_loop(rows, body, step=16):
    def one(i, carry):
        body(pl.multiple_of(i * step, step), step)
        return carry

    lax.fori_loop(0, rows // step, one, 0)


class Scatter:
    @staticmethod
    def shapes(rows, width, dma):
        whole = pltpu.VMEM((4, rows, width), BF)
        pair = pltpu.VMEM((2, rows // 2, width), BF)
        return [whole, whole] + [pair] * 6 + [dma((4,)), dma((11,)), dma((11,))]

    def __init__(self, p, ov, scratch):
        self.p, self.ov = p, ov
        self.pv, self.rc, self.q6, self.q2, self.q4, self.d6, self.rx, self.ry = scratch[:8]
        self.lsem, self.ssem, self.rsem = scratch[8:]
        self.rows = ov.shape[0]
        self.half = self.rows // 2

    def block(self, k, first=0, count=None):
        return self.p.at[pl.ds(k * self.rows + first, count or self.rows)]

    def go(self, i, src, dst, k):
        return send(src, dst, self.ssem.at[i], self.rsem.at[i], k)

    def begin(self):
        half = self.half
        top, bot = pl.ds(0, half), pl.ds(half, half)
        self.c7t = self.go(0, self.block(7, 0, half), self.rc.at[3, top], 1)
        self.c7b = self.go(1, self.block(7, half, half), self.rc.at[3, bot], 1)
        self.c3 = self.go(2, self.block(3), self.rc.at[1], 1)
        self.c5 = self.go(3, self.block(5), self.rc.at[2], 1)
        self.c1 = self.go(4, self.block(1), self.rc.at[0], 1)

    def load(self):
        self.loads = [
            pltpu.make_async_copy(self.block(2 * i), self.pv.at[i], self.lsem.at[i])
            for i in range(4)
        ]
        for i in (3, 1, 2, 0):
            self.loads[i].start()

    def add(self, dst, i, start, more=None):
        def body(r, n):
            s = pl.ds(pl.multiple_of(start + r, 16), n)
            total = self.pv[i, s, :].astype(F32) + self.rc[i, s, :].astype(F32)
            if more is not None:
                total = total + more[pl.ds(r, n), :].astype(F32)
            dst[pl.ds(r, n), :] = total.astype(BF)

        rows_loop(self.half, body)

    def middle(self):
        half = self.half
        self.loads[3].wait()
        self.c7t.wait_recv()
        self.add(self.q6.at[0], 3, 0)
        self.s6t = self.go(5, self.q6.at[0], self.d6.at[0], 2)
        self.c7b.wait_recv()
        self.add(self.q6.at[1], 3, half)
        self.s6b = self.go(6, self.q6.at[1], self.d6.at[1], 4)
        self.loads[1].wait()
        self.c3.wait_recv()
        self.add(self.q2.at[0], 1, 0)
        self.s2t = self.go(7, self.q2.at[0], self.rx.at[0], 2)
        self.loads[2].wait()
        self.c5.wait_recv()
        self.add(self.q4.at[1], 2, half)
        self.s4b = self.go(8, self.q4.at[1], self.ry.at[1], 4)

    def relay(self):
        self.s6t.wait_recv()
        self.add(self.q4.at[0], 2, 0, self.d6.at[0])
        self.s4t = self.go(9, self.q4.at[0], self.ry.at[0], 4)
        self.s6b.wait_recv()
        self.add(self.q2.at[1], 1, self.half, self.d6.at[1])
        self.s2b = self.go(10, self.q2.at[1], self.rx.at[1], 2)

    def total(self, n):
        def body(r, count):
            s = pl.ds(pl.multiple_of(n * self.half + r, 16), count)
            r = pl.ds(r, count)
            total = self.pv[0, s, :].astype(F32) + self.rc[0, s, :].astype(F32)
            total = total + self.rx[n, r, :].astype(F32) + self.ry[n, r, :].astype(F32)
            self.ov[s, :] = total

        rows_loop(self.half, body)

    def finish(self):
        self.loads[0].wait()
        self.c1.wait_recv()
        self.s2t.wait_recv()
        self.s4t.wait_recv()
        self.total(0)
        self.s2b.wait_recv()
        self.s4b.wait_recv()
        self.total(1)
        for copy in (self.c7t, self.c7b, self.c3, self.c5, self.c1, self.s6t, self.s6b):
            copy.wait_send()
        for copy in (self.s2t, self.s4b, self.s4t, self.s2b):
            copy.wait_send()


def scatter_kernel(p, o, ov, osem, *scratch):
    greet((1, 2, 4))
    scatter = Scatter(p, ov, scratch)
    scatter.begin()
    scatter.load()
    scatter.middle()
    scatter.relay()
    scatter.finish()
    out = pltpu.make_async_copy(ov, o, osem)
    out.start()
    out.wait()


def plane_scatter(p, ident):
    rows, width = p.shape[0] // PLANE, p.shape[1]
    dma = pltpu.SemaphoreType.DMA
    scratch = [pltpu.VMEM((rows, width), F32), dma] + Scatter.shapes(rows, width, dma)
    out = jax.ShapeDtypeStruct((rows, width), F32)
    return call(scatter_kernel, (p,), out, scratch, ident, 24, 31)


def cut(weights, blocks):
    plan = []
    for i, cols in enumerate(weights):
        each = cols // blocks
        for b in range(blocks):
            plan.append((i, b * each, each // PLANE, b * (each // PLANE)))
    return plan


def spread_kernel(plan, count, *refs):
    ins, outs, held = refs[:count], refs[count : 2 * count], refs[2 * count : 3 * count]
    lsem, ssem, rsem = refs[3 * count :]
    loads = [pltpu.make_async_copy(a, v, lsem.at[i]) for i, (a, v) in enumerate(zip(ins, held))]
    for copy in loads:
        copy.start()
    greet(range(1, PLANE))
    mine = place(0)
    remotes = []
    for w, load in enumerate(loads):
        load.wait()
        rows = ins[w].shape[0]
        here = pl.ds(pl.multiple_of(mine * rows, 16), rows)
        for n, (i, base, width, col) in enumerate(plan):
            if i != w:
                continue
            for k in (6, 7, 2, 3, 4, 5, 1):
                cols = pl.ds(pl.multiple_of(base + place(k) * width, 128), width)
                remotes.append(
                    send(
                        held[w].at[:, cols],
                        outs[w].at[here, pl.ds(col, width)],
                        ssem.at[n, k],
                        rsem.at[n, k],
                        k,
                    )
                )
            cols = pl.ds(pl.multiple_of(base + mine * width, 128), width)
            copy = pltpu.make_async_copy(
                held[w].at[:, cols], outs[w].at[here, pl.ds(col, width)], ssem.at[n, 0]
            )
            copy.start()
            remotes.append(copy)
    for copy in remotes:
        copy.wait()


def spread(weights, ident, blocks=1):
    plan = cut([w.shape[1] for w in weights], blocks)
    outs = [
        jax.ShapeDtypeStruct((w.shape[0] * PLANE, w.shape[1] // PLANE), w.dtype) for w in weights
    ]
    dma = pltpu.SemaphoreType.DMA
    n = len(plan)
    scratch = [pltpu.VMEM(w.shape, w.dtype) for w in weights]
    return call(
        functools.partial(spread_kernel, plan, len(weights)),
        tuple(weights),
        outs,
        scratch + [dma((len(weights),)), dma((n, PLANE)), dma((n, PLANE))],
        ident,
        8,
        sum(w.size for w in weights) / 3e4,
    )


def collect_kernel(plan, count, *refs):
    ins, outs, held = refs[:count], refs[count : 2 * count], refs[2 * count : 3 * count]
    lsem, ssem, rsem = refs[3 * count :]
    loads = [pltpu.make_async_copy(a, v, lsem.at[i]) for i, (a, v) in enumerate(zip(ins, held))]
    for copy in loads:
        copy.start()
    greet(range(1, PLANE))
    mine = place(0)
    remotes = []
    for w, load in enumerate(loads):
        load.wait()
        rows = outs[w].shape[0]
        for n, (i, base, width, col) in enumerate(plan):
            if i != w:
                continue
            cols = pl.ds(pl.multiple_of(base + mine * width, 128), width)
            for k in (6, 7, 2, 3, 4, 5, 1):
                there = pl.ds(pl.multiple_of(place(k) * rows, 16), rows)
                remotes.append(
                    send(
                        held[w].at[there, pl.ds(col, width)],
                        outs[w].at[:, cols],
                        ssem.at[n, k],
                        rsem.at[n, k],
                        k,
                    )
                )
            here = pl.ds(pl.multiple_of(mine * rows, 16), rows)
            copy = pltpu.make_async_copy(
                held[w].at[here, pl.ds(col, width)], outs[w].at[:, cols], ssem.at[n, 0]
            )
            copy.start()
            remotes.append(copy)
    for copy in remotes:
        copy.wait()


def collect(grads, ident, blocks=1):
    plan = cut([g.shape[1] * PLANE for g in grads], blocks)
    outs = [
        jax.ShapeDtypeStruct((g.shape[0] // PLANE, g.shape[1] * PLANE), g.dtype) for g in grads
    ]
    dma = pltpu.SemaphoreType.DMA
    n = len(plan)
    scratch = [pltpu.VMEM(g.shape, g.dtype) for g in grads]
    return call(
        functools.partial(collect_kernel, plan, len(grads)),
        tuple(grads),
        outs,
        scratch + [dma((len(grads),)), dma((n, PLANE)), dma((n, PLANE))],
        ident,
        8,
        sum(g.size for g in grads) / 3e4,
    )


def flat_place():
    return lax.axis_index("z") * PLANE + lax.axis_index("y") * 4 + lax.axis_index("blk")


def flat_id(d):
    return {"z": lax.div(d, PLANE), "y": lax.rem(lax.div(d, 4), 2), "blk": lax.rem(d, 4)}


def greet_all(count):
    barrier = pltpu.get_barrier_semaphore()
    me = flat_place()

    def one(i, carry):
        pl.semaphore_signal(
            barrier,
            inc=1,
            device_id=flat_id(lax.rem(me + i, count)),
            device_id_type=pl.DeviceIdType.MESH,
        )
        return carry

    lax.fori_loop(1, count, one, 0)
    pl.semaphore_wait(barrier, count - 1)


def to_all(count, source, target, ssem, rsem):
    me = flat_place()

    def copy(i):
        d = lax.rem(me + i, count)
        return pltpu.make_async_remote_copy(
            src_ref=source(d),
            dst_ref=target.at[me],
            send_sem=ssem.at[i],
            recv_sem=rsem.at[i],
            device_id=flat_id(d),
            device_id_type=pl.DeviceIdType.MESH,
        )

    def begin(i, carry):
        copy(i).start()
        return carry

    def finish(i, carry):
        copy(i).wait()
        return carry

    lax.fori_loop(1, count, begin, 0)
    target[me] = source(me)[...]
    lax.fori_loop(1, count, finish, 0)


def exchange_kernel(count, x, o, ssem, rsem):
    greet_all(count)
    to_all(count, lambda d: x.at[d], o, ssem, rsem)


def small_call(kernel, ins, outs, scratch, ident, micros):
    vmem = pl.BlockSpec(memory_space=pltpu.VMEM)
    return pl.pallas_call(
        kernel,
        out_shape=outs,
        in_specs=[vmem] * len(ins),
        out_specs=jax.tree.map(lambda _: vmem, outs),
        scratch_shapes=scratch,
        compiler_params=pltpu.CompilerParams(
            collective_id=ident, has_side_effects=True, vmem_limit_bytes=32 * MIB
        ),
        cost_estimate=pl.CostEstimate(
            flops=0, bytes_accessed=int(micros * 3.6e6), transcendentals=0
        ),
    )(*ins)


def exchange(x, ident):
    dma = pltpu.SemaphoreType.DMA((x.shape[0],))
    return small_call(
        functools.partial(exchange_kernel, x.shape[0]),
        (x,),
        jax.ShapeDtypeStruct(x.shape, x.dtype),
        [dma, dma],
        ident,
        8,
    )


def mods_back_kernel(count, x, w, o, t, got, part, mine, s0, r0, s1, r1, s2, r2):
    greet_all(count)
    to_all(count, lambda d: x.at[d], got, s0, r0)
    groups = o.shape[0]
    for g in range(groups):
        o[g] = got[4 * g] + got[4 * g + 1] + got[4 * g + 2] + got[4 * g + 3]
    own = o[...].reshape(groups * 8, o.shape[2])
    high = own.astype(BF)
    rest = own - high.astype(F32)
    low = rest.astype(BF)
    quarter = w.shape[0] // 4
    for q in range(4):
        piece = w[q * quarter : (q + 1) * quarter, :]
        product = times_t(high, piece) + times_t(low, piece)
        for g in range(groups):
            part[4 * g + q] = product[8 * g : 8 * g + 8]
    to_all(count, lambda d: part.at[d], mine, s1, r1)

    def add(i, total):
        return total + mine[i]

    part[flat_place()] = lax.fori_loop(0, count, add, jnp.zeros(mine.shape[1:], F32))
    to_all(count, lambda d: part.at[flat_place()], t, s2, r2)


def mods_back(x, w, ident):
    count, eight, cols = x.shape
    width = w.shape[0]
    dma = pltpu.SemaphoreType.DMA((count,))
    pieces = jax.ShapeDtypeStruct((count, eight, width // 4), F32)
    return small_call(
        functools.partial(mods_back_kernel, count),
        (x, w),
        (jax.ShapeDtypeStruct((count // 4, eight, cols), F32), pieces),
        [pltpu.VMEM(x.shape, F32), pltpu.VMEM(pieces.shape, F32), pltpu.VMEM(pieces.shape, F32)]
        + [dma] * 6,
        ident,
        20,
    )


def z_gather(x):
    return lax.all_gather(x, "z", axis=0, tiled=True)


def z_scatter(g):
    return lax.psum_scatter(g, "z", scatter_dimension=0, tiled=True)


def z_peer(m):
    z = lax.axis_index("z")
    if m == 1:
        z = z + 1 - 2 * lax.rem(z, 2)
    elif m == 2:
        z = lax.rem(z + 2, 4)
    else:
        z = 3 - z
    return z


def inner_plane():
    z = lax.axis_index("z")
    return (z == 1) | (z == 2)


def outer_plane():
    z = lax.axis_index("z")
    return (z == 0) | (z == 3)


def remote(src, dst, ssem, rsem, where):
    return pltpu.make_async_remote_copy(
        src_ref=src,
        dst_ref=dst,
        send_sem=ssem,
        recv_sem=rsem,
        device_id=where,
        device_id_type=pl.DeviceIdType.MESH,
    )


class OutRows:
    def __init__(self):
        z, j = lax.axis_index("z"), place(0)
        me = z * PLANE + j
        self.slot = lax.rem(me, 4)
        self.user = self.flat(self.slot * PLANE + lax.div(me, 4))
        self.owner = self.flat(4 * j + z)
        self.away, self.home = me != 4 * j + z, me == 4 * j + z

    @staticmethod
    def flat(d):
        return flat_id(d)


def greet_more(outs):
    barrier = pltpu.get_barrier_semaphore()

    def signal(where):
        pl.semaphore_signal(
            barrier, inc=1, device_id=where, device_id_type=pl.DeviceIdType.MESH
        )

    ids = [peer(k) for k in range(1, PLANE)] + [{"z": z_peer(m)} for m in (1, 2, 3)]
    for where in ids:
        signal(where)

    @pl.when(outs.away)
    def _():
        signal(outs.user)
        signal(outs.owner)
        pl.semaphore_wait(barrier, len(ids) + 2)

    pl.when(outs.home)(lambda: pl.semaphore_wait(barrier, len(ids)))


class PlaneCopy:
    shapes = staticmethod(lambda dma: [dma((4,)), dma((4,))])

    def __init__(self, full, sems):
        self.full = full
        self.m = full.shape[0] // 4
        self.ssem, self.rsem = sems

    def copy(self, slot, t, m):
        block = self.full.at[pl.ds(pl.multiple_of(t * self.m, self.m), self.m)]
        return remote(block, block, self.ssem.at[slot], self.rsem.at[slot], {"z": z_peer(m)})

    def begin(self):
        z = lax.axis_index("z")
        self.copy(1, z, 2).start()
        self.copy(0, z, 1).start()

    def relay(self):
        @pl.when(inner_plane())
        def _():
            self.copy(1, z_peer(2), 2).wait_recv()
            self.copy(3, z_peer(2), 1).start()
            self.copy(2, lax.axis_index("z"), 3).start()

    def finish(self):
        z = lax.axis_index("z")
        self.copy(0, z_peer(1), 1).wait_recv()

        @pl.when(inner_plane())
        def _():
            self.copy(2, z_peer(3), 3).wait_recv()
            self.copy(2, z, 3).wait_send()
            self.copy(3, z_peer(2), 1).wait_send()

        @pl.when(outer_plane())
        def _():
            self.copy(1, z_peer(2), 2).wait_recv()
            self.copy(3, z_peer(3), 1).wait_recv()

        self.copy(0, z, 1).wait_send()
        self.copy(1, z, 2).wait_send()


class PlaneSum:
    @staticmethod
    def shapes(m, c, dma):
        return [pltpu.VMEM((m, c), BF), dma((4,)), dma((4,))]

    def __init__(self, g, landing, scratch, temps):
        self.g, self.landing, self.temps = g, landing, temps
        self.q, self.ssem, self.rsem = scratch
        self.m, self.c = g.shape[1:]
        self.inner, self.outer = inner_plane(), outer_plane()

    def copy(self, src, slot, m):
        return pltpu.make_async_remote_copy(
            src_ref=src,
            dst_ref=self.landing.at[slot],
            send_sem=self.ssem.at[slot],
            recv_sem=self.rsem.at[slot],
            device_id={"z": z_peer(m)},
            device_id_type=pl.DeviceIdType.MESH,
        )

    def begin_far(self):
        pl.when(self.outer)(lambda: self.copy(self.g.at[z_peer(3)], 2, 1).start())

    def begin_swap(self):
        pl.when(self.inner)(lambda: self.copy(self.g.at[z_peer(3)], 3, 3).start())

    def begin(self):
        self.begin_far()
        self.begin_swap()

    def temp(self, i):
        return self.temps.at[i, pl.ds(0, self.m), pl.ds(0, self.c)]

    def load(self, src, i):
        copy = pltpu.make_async_copy(src, self.temp(i), self.tsem.at[i])
        copy.start()
        return copy

    def hop(self, tsem):
        self.tsem = tsem
        across = self.g.at[z_peer(2)]

        @pl.when(self.outer)
        def _():
            self.copy(across, 1, 2).start()

        @pl.when(self.inner)
        def _():
            first = self.load(across, 0)
            self.copy(across, 2, 1).wait_recv()
            second = self.load(self.landing.at[2], 1)
            first.wait()
            second.wait()

            def body(r, n):
                r = (pl.ds(r, n), pl.ds(0, self.c))
                total = self.temps[(0,) + r].astype(F32) + self.temps[(1,) + r].astype(F32)
                self.q[r] = total.astype(BF)

            rows_loop(self.m, body)
            self.copy(self.q, 1, 2).start()

        self.near = self.copy(self.g.at[z_peer(1)], 0, 1)
        self.near.start()

    def finish(self, tsem):
        self.tsem = tsem
        loads = [self.load(self.g.at[lax.axis_index("z")], 0)]
        self.near.wait_recv()
        loads.append(self.load(self.landing.at[0], 1))
        far = self.copy(self.q, 1, 2)
        far.wait_recv()
        loads.append(self.load(self.landing.at[1], 2))
        pl.when(self.inner)(lambda: self.copy(self.g.at[0], 3, 3).wait_recv())
        pl.when(self.inner)(lambda: self.load(self.landing.at[3], 3).wait())
        for copy in loads:
            copy.wait()
        far.wait_send()
        self.near.wait_send()
        pl.when(self.outer)(lambda: self.copy(self.g.at[0], 2, 1).wait_send())
        pl.when(self.inner)(lambda: self.copy(self.g.at[0], 3, 3).wait_send())

        def three(r, n):
            r = (pl.ds(r, n), pl.ds(0, self.c))
            total = self.temps[(0,) + r].astype(F32) + self.temps[(1,) + r].astype(F32)
            return r, total + self.temps[(2,) + r].astype(F32)

        def outer(r, n):
            r, total = three(r, n)
            self.q[r] = total.astype(BF)

        def inner(r, n):
            r, total = three(r, n)
            self.q[r] = (total + self.temps[(3,) + r].astype(F32)).astype(BF)

        pl.when(self.outer)(lambda: rows_loop(self.m, outer))
        pl.when(self.inner)(lambda: rows_loop(self.m, inner))


def deal(src, out, blocks, ssem, rsem):
    rows = out.shape[0]
    mine = place(0)
    copies = []
    for n, (_, base, width, col) in enumerate(cut([out.shape[1]], blocks)):
        cols = pl.ds(pl.multiple_of(base + mine * width, 128), width)
        for k in (6, 7, 2, 3, 4, 5, 1, 0):
            there = pl.ds(pl.multiple_of(place(k) * rows, 16), rows)
            piece = src.at[there, pl.ds(col, width)]
            if k:
                copies.append(send(piece, out.at[:, cols], ssem.at[n, k], rsem.at[n, k], k))
            else:
                copies.append(pltpu.make_async_copy(piece, out.at[:, cols], ssem.at[n, 0]))
                copies[-1].start()
    return copies


def pipe(body, steps, ins, outs):
    spec = lambda a: pl.BlockSpec(a[1], a[2])
    pltpu.emit_pipeline(
        body, grid=(steps,), in_specs=[spec(a) for a in ins], out_specs=[spec(a) for a in outs]
    )(*[a[0] for a in ins], *[a[0] for a in outs])


def whole(a):
    return (a, a.shape, lambda i: (0,) * len(a.shape))


def some_rows(a, n, pick=lambda i: i):
    return (a, (n, a.shape[1]), lambda i: (pick(i), 0))


def grads_mm(a, b, g):
    m = g.shape[1]

    def body(a, b, g):
        g[0] = over_rows(a[...], b[...]).astype(BF)

    pipe(
        body,
        g.shape[0],
        [(a, (a.shape[0], m), lambda i: (0, i)), whole(b)],
        [(g, (1,) + g.shape[1:], lambda i: (i, 0, 0))],
    )


def rows_mm(a, b, o, n, steps, pick=lambda i: i, transposed=False):
    def body(a, b, o):
        o[...] = (times_t if transposed else dot)(a[...], b[...]).astype(BF)

    pipe(body, steps, [some_rows(a, n, pick), whole(b)], [some_rows(o, n, pick)])


class Share:
    @staticmethod
    def shapes(w, blocks, dma):
        return [pltpu.VMEM(w, BF), dma, dma((blocks, PLANE)), dma((blocks, PLANE))]

    def __init__(self, w, full, blocks, scratch):
        self.w, self.full, self.blocks = w, full, blocks
        self.held, self.lsem, self.ssem, self.rsem = scratch
        self.load = pltpu.make_async_copy(w, self.held, self.lsem)
        self.load.start()

    def begin(self):
        self.load.wait()
        rows = self.w.shape[0]
        first = lax.axis_index("z") * (PLANE * rows) + place(0) * rows
        here = pl.ds(pl.multiple_of(first, rows), rows)
        self.copies = []
        for n, (_, base, width, col) in enumerate(cut([self.w.shape[1]], self.blocks)):
            dst = self.full.at[here, pl.ds(col, width)]
            for k in (6, 7, 2, 3, 4, 5, 1, 0):
                cols = pl.ds(pl.multiple_of(base + place(k) * width, 128), width)
                src = self.held.at[:, cols]
                if k:
                    copy = send(src, dst, self.ssem.at[n, k], self.rsem.at[n, k], k)
                else:
                    copy = pltpu.make_async_copy(src, dst, self.ssem.at[n, 0])
                    copy.start()
                self.copies.append(copy)

    def finish(self):
        for copy in self.copies:
            copy.wait()


IMAGES = 3


def whole_kernel(factor, names, *refs):
    v = dict(zip(names, refs))
    get = lambda *keys: [v[key] for key in keys]
    group_of = lambda prefix: [v[key] for key in names if key.startswith(prefix + ".")]
    cols, tok, cot, pick, mods = get("cols", "tok", "cot", "pick", "mods")
    first, second, dy, dat = get("first", "second", "dy", "dat")
    qkv, mixed, hid, slope = get("qkv", "mixed", "hid", "slope")
    du, part, part_y, dmix, dqkv = get("du", "part", "part_y", "dmix", "dqkv")
    xh, xv, xg, va, vb, vd = get("xh", "xv", "xg", "va", "vb", "vd")
    block_out, grad_tokens = get("block_out", "grad_tokens")
    img, temps, temps_out, tsem = get("img", "temps", "temps_out", "tsem")
    rows, width = tok.shape
    tokens = dy.shape[0]
    group = 4 * rows
    z, y, mine = lax.axis_index("z"), lax.axis_index("y"), place(0)
    odd, even = (lambda i: 2 * i + 1), (lambda i: 2 * i)
    outs = OutRows()

    qkv_in = Share(v["qkv_w"], v["full_qkv"], 3, group_of("in_qkv"))
    up_in = Share(v["up_w"], v["full_up"], 1, group_of("in_up"))
    down_in = Share(v["down_w"], v["full_down"], 1, group_of("in_down"))
    held, lsem, osems, rsems = group_of("in_out")
    out_load = pltpu.make_async_copy(v["out_w"], held, lsem)
    out_load.start()
    out_block = v["out_w"].shape[0]
    full_out = v["full_out"]
    out_at = lambda i: full_out.at[pl.ds(pl.multiple_of(i * out_block, out_block), out_block)]
    out_in = remote(held, out_at(outs.slot), osems.at[0], rsems.at[0], outs.user)
    out_local = pltpu.make_async_copy(held, out_at(z), osems.at[0])
    greet_more(outs)

    ma, mb = get("ma", "mb")
    sa, ra, sb, rb = group_of("mod_in")
    sent = []
    for m in (1, 2, 3):
        src = cols.at[pl.ds(2 * z_peer(m), 2)]
        sent.append(remote(src, ma.at[z], sa.at[m], ra.at[m], {"z": z_peer(m)}))
        sent[-1].start()
    out_load.wait()
    pl.when(outs.away)(lambda: out_in.start())
    pl.when(outs.home)(lambda: out_local.start())
    qkv_in.begin()
    ma[z] = cols[pl.ds(2 * z, 2)]
    for copy in sent:
        copy.wait()
    sent = []
    for k in range(1, PLANE):
        src = ma.at[:, peer(k)["y"]]
        sent.append(send(src, mb.at[mine], sb.at[k], rb.at[k], k))
    pl.when(outs.away)(lambda: out_in.wait())
    pl.when(outs.home)(lambda: out_local.wait())
    z_out = PlaneCopy(full_out, group_of("z_out"))
    z_out.begin()
    qkv_in.finish()
    z_qkv = PlaneCopy(v["full_qkv"], group_of("z_qkv"))
    z_qkv.begin()
    mb[mine] = ma[:, y]
    for copy in sent:
        copy.wait()
    each = cols.shape[2]
    for d in range(4 * PLANE):
        mods[:, d * each : (d + 1) * each] = mb[d % PLANE, d // PLANE]

    def picker(r):
        hot = pick[r, 0:128]
        ones = [hot[:, i : i + 1].astype(F32) for i in range(IMAGES)]

        def mod(which):
            at = slice(which * width, (which + 1) * width)
            return sum(ones[i] * mods[i : i + 1, at] for i in range(IMAGES))

        return mod

    def normed_of(x):
        inv = lax.rsqrt(jnp.mean(x * x, axis=-1, keepdims=True) + EPS)
        return inv, x * inv

    def norm_grad(inv, normed, d_normed):
        slant = jnp.mean(d_normed * normed, axis=-1, keepdims=True)
        return inv * (d_normed - normed * slant)

    def make_first(r, n):
        r = pl.ds(r, n)
        mod = picker(r)
        _, normed = normed_of(tok[r, :].astype(F32))
        xh[r, 0:width] = (normed * (1.0 + mod(1)) + mod(0)).astype(BF)
        xh[r, width:] = pick[r, :]
        xg[r, :] = (mod(5) * cot[r, :].astype(F32)).astype(BF)

    rows_loop(rows, make_first)
    to_first = Gather(xh, first, group_of("ga"))
    to_first.begin()
    up_in.begin()
    z_out.relay()
    to_first.relay()
    z_qkv.relay()
    to_first.finish()
    down_in.begin()
    up_in.finish()
    z_qkv.finish()
    z_up = PlaneCopy(v["full_up"], group_of("z_up"))
    z_up.begin()

    n = math.gcd(tokens, 256)

    def mm_body(a, b, o):
        o[...] = dot(a[...], b[...]).astype(BF)

    pipe(mm_body, tokens // n, [some_rows(first.at[:, 0:width], n), whole(v["full_qkv"])], [some_rows(qkv, n)])
    masks = [
        some_rows(first.at[:, width : width + 128], group),
        some_rows(first.at[:, width + 128 : width + 256], group),
    ]
    pipe(
        functools.partial(attend_kernel, factor),
        2,
        [some_rows(qkv, group)] + masks,
        [some_rows(mixed, group)],
    )
    down_in.finish()
    z_out.finish()
    rows_mm(mixed, full_out, part, rows, 4, odd)
    r_attn = Scatter(part, va, group_of("sc_a") + group_of("sems_1"))
    r_attn.begin()
    rows_mm(mixed, full_out, part, rows, 4, even)
    r_attn.load()
    r_attn.middle()
    r_attn.relay()
    z_up.relay()
    z_down = PlaneCopy(v["full_down"], group_of("z_down"))
    z_down.begin()
    r_attn.finish()

    def make_second(r, n):
        r = pl.ds(r, n)
        mod = picker(r)
        x = tok[r, :].astype(F32) + mod(2) * va[r, :]
        vd[r, :] = x
        xv[r, :] = (normed_of(x)[1] * (1.0 + mod(4)) + mod(3)).astype(BF)

    rows_loop(rows, make_second)
    to_second = Gather(xv, second, group_of("gb"))
    to_second.begin()
    to_second.relay()
    to_second.finish()
    to_dy = Gather(xg, dy, group_of("gc"))
    to_dy.begin()
    z_up.finish()

    def up_body(a, b, h, s):
        u = dot(a[...], b[...])
        c = math.sqrt(2.0 / math.pi)
        t = jnp.tanh(c * (u + 0.044715 * (u * u * u)))
        h[...] = (0.5 * u * (1.0 + t)).astype(BF)
        inside = c * (1.0 + (3 * 0.044715) * (u * u))
        s[...] = 0.5 * (1.0 + t) + 0.5 * u * (1.0 - t * t) * inside

    pipe(
        up_body,
        tokens // n,
        [some_rows(second, n), whole(v["full_up"])],
        [some_rows(hid, n), some_rows(slope, n)],
    )
    to_dy.relay()
    z_down.relay()
    to_dy.finish()
    sums = [
        PlaneSum(v["g_" + key], v["land_" + key], group_of("s_" + key), t)
        for key, t in (("down", temps), ("up", temps), ("qkv", temps), ("out", temps_out))
    ]
    s_down, s_up, s_qkv, s_out = sums
    grads_mm(dy, hid, v["g_down"])
    s_down.begin_far()
    z_down.finish()
    s_down.begin_swap()
    s_down.hop(tsem)

    def du_body(a, b, s, o):
        o[...] = (dot(a[...], b[...]) * s[...]).astype(BF)

    pipe(
        du_body,
        tokens // n,
        [some_rows(dy, n), whole(v["full_down"]), some_rows(slope, n)],
        [some_rows(du, n)],
    )
    rows_mm(du, v["full_up"], part, rows, 4, odd, True)
    r_e2 = Scatter(part, vb, group_of("sc_a") + group_of("sems_2"))
    r_e2.begin()
    rows_mm(du, v["full_up"], part, rows, 4, even, True)
    r_e2.load()
    r_e2.middle()
    grads_mm(second, du, v["g_up"])
    s_up.begin()
    r_e2.relay()
    r_e2.finish()

    pv = v["sc_b.0"]
    parts = [(pv.at[0], pv.at[1]), (pv.at[2], pv.at[3]), (xg, xh.at[:, 0:width])]

    def tally(which, r, value):
        high = value.astype(BF)
        parts[which][0][r, :] = high
        parts[which][1][r, :] = (value - high.astype(F32)).astype(BF)

    def flush(blocks):
        hot = pick[:, 0:128]
        for (high, low), which in zip(parts, blocks):
            total = over_rows(hot, high[...]) + over_rows(hot, low[...])
            img[:, which * width : (which + 1) * width] = total[0:8]

    def norm_back(r, n):
        r = pl.ds(r, n)
        mod = picker(r)
        inv, normed = normed_of(vd[r, :])
        e = vb[r, :]
        d_mid = cot[r, :].astype(F32) + norm_grad(inv, normed, e * (1.0 + mod(4)))
        grad_tokens[r, :] = d_mid
        xv[r, :] = (mod(2) * d_mid).astype(BF)
        tally(0, r, e)
        tally(1, r, e * normed)
        tally(2, r, d_mid * va[r, :])

    rows_loop(rows, norm_back)
    load_w = pltpu.make_async_copy(v["mod_w_in"], v["mod_w"], group_of("mod_out")[10].at[0])
    load_w.start()
    to_dat = Gather(xv, dat, group_of("gd"))
    to_dat.begin()
    flush((3, 4, 2))
    rows_mm(hid, v["full_down"], part_y, rows, 8, transposed=True)
    to_dat.relay()
    s_up.hop(tsem)
    to_dat.finish()
    r_y = Scatter(part_y, va, group_of("sc_b") + group_of("sems_3"))
    r_y.begin()
    r_y.load()
    rows_mm(dat, full_out, dmix, 2 * rows, 4, transposed=True)
    r_y.middle()
    pipe(
        functools.partial(attend_back_kernel, factor),
        2,
        [some_rows(qkv, group)] + masks + [some_rows(dmix, group)],
        [some_rows(dqkv, group)],
    )
    r_y.relay()
    grads_mm(first.at[:, 0:width], dqkv, v["g_qkv"])
    s_qkv.begin()
    dealt = []
    deal_sems = group_of("deal")

    def settle(s, out, blocks, sems):
        s.finish(tsem)
        dealt.extend(deal(s.q, out, blocks, *sems))

    r_y.finish()
    rows_mm(dqkv, v["full_qkv"], part, rows, 4, odd, True)
    r_e1 = Scatter(part, vb, group_of("sc_a") + group_of("sems_4"))
    r_e1.begin()
    rows_mm(dqkv, v["full_qkv"], part, rows, 4, even, True)
    r_e1.load()
    r_e1.middle()
    s_qkv.hop(tsem)

    def out_body(a, b, g):
        g[...] = over_rows(a[...], b[...]).astype(BF).reshape(g.shape)

    step = math.gcd(width, 512)
    g_out = v["g_out"]
    pipe(
        out_body,
        width // step,
        [whole(mixed), (dat, (tokens, step), lambda i: (0, i))],
        [(g_out, g_out.shape[:2] + (step,), lambda i: (0, 0, i))],
    )
    s_out.begin()
    r_e1.relay()
    s_out.hop(tsem)
    r_e1.finish()

    def last_norm(r, n):
        r = pl.ds(r, n)
        mod = picker(r)
        inv, normed = normed_of(tok[r, :].astype(F32))
        e, out = vb[r, :], va[r, :]
        grad_tokens[r, :] += norm_grad(inv, normed, e * (1.0 + mod(1)))
        block_out[r, :] = (vd[r, :] + mod(5) * out).astype(BF)
        tally(0, r, e)
        tally(1, r, e * normed)
        tally(2, r, cot[r, :].astype(F32) * out)

    rows_loop(rows, last_norm)
    flush((0, 1, 5))

    pa, ga, gs, gb, pc, pd, pe, ts = get("pa", "ga_", "gs", "gb_", "pc", "pd", "pe", "ts")
    w, t_all, dm = get("mod_w", "t_all", "dm")
    sems = group_of("mod_out")
    for d in range(4 * PLANE):
        t = d // PLANE * IMAGES
        pa[d % PLANE, t : t + IMAGES] = img[0:IMAGES, d * each : (d + 1) * each]
    plane_sent = lambda src, dst, s, r: [
        send(src(k), dst, s.at[k], r.at[k], k) for k in range(1, PLANE)
    ]
    sent = plane_sent(lambda k: pa.at[place(k)], ga.at[mine], sems[0], sems[1])
    ga[mine] = pa[mine]
    gs[...] = jnp.zeros_like(gs)
    settle(s_down, v["c_down"], 1, deal_sems[:2])
    for copy in sent:
        copy.wait()
    for g in range(2):
        total = ga[4 * g] + ga[4 * g + 1] + ga[4 * g + 2] + ga[4 * g + 3]
        for t in range(4):
            gs[t, g * IMAGES : (g + 1) * IMAGES] = total[t * IMAGES : (t + 1) * IMAGES]
    sent = []
    for m in (1, 2, 3):
        copy = remote(
            gs.at[z_peer(m)], gb.at[z], sems[2].at[m], sems[3].at[m], {"z": z_peer(m)}
        )
        copy.start()
        sent.append(copy)
    gb[z] = gs[z]
    s_up.finish(tsem)
    s_out.finish(tsem)
    back = remote(s_out.q, v["c_out"], tsem.at[4], tsem.at[5], outs.owner)
    back_local = pltpu.make_async_copy(s_out.q, v["c_out"], tsem.at[4])
    pl.when(outs.away)(lambda: back.start())
    pl.when(outs.home)(lambda: back_local.start())
    for copy in sent:
        copy.wait()
    load_w.wait()
    dm[...] = gb[...]
    own = dm[...].reshape(4 * 8, each)
    high = own.astype(BF)
    low = (own - high.astype(F32)).astype(BF)
    slice_of = width // PLANE
    for k in range(PLANE):
        piece = w[k * slice_of : (k + 1) * slice_of, :]
        pc[k] = times_t(high, piece) + times_t(low, piece)
    sent = plane_sent(lambda k: pc.at[place(k)], pd.at[mine], sems[4], sems[5])
    pd[mine] = pc[mine]
    dealt.extend(deal(s_up.q, v["c_up"], 1, *deal_sems[2:4]))
    for copy in sent:
        copy.wait()
    total = pd[0]
    for k in range(1, PLANE):
        total = total + pd[k]
    pe[z] = total
    sent = []
    for m in (1, 2, 3):
        copy = remote(pe.at[z], pe.at[z], sems[6].at[m], sems[7].at[m], {"z": z_peer(m)})
        copy.start()
        sent.append(copy)
    settle(s_qkv, v["c_qkv"], 3, deal_sems[4:6])
    for copy in sent:
        copy.wait()
    ts[...] = pe[0] + pe[1] + pe[2] + pe[3]
    sent = plane_sent(lambda k: ts, t_all.at[mine], sems[8], sems[9])
    t_all[mine] = ts[...]
    for copy in sent:
        copy.wait()
    for copy in dealt:
        copy.wait()
    pl.when(outs.away)(lambda: back.wait())
    pl.when(outs.home)(lambda: back_local.wait())


def whole_block(cols, tok, cot, pick, mod_w, qkv_w, out_w, up_w, down_w, factor, ident):
    rows, width = tok.shape
    nz, tokens = 4, PLANE * rows
    share = qkv_w.shape[0]
    m = share * PLANE
    wide, part, heads = up_w.shape[1] // PLANE, qkv_w.shape[1] // PLANE, nz * out_w.shape[0]
    each = cols.shape[2]
    struct, vm, dma = jax.ShapeDtypeStruct, pltpu.VMEM, pltpu.SemaphoreType.DMA
    vmem = pl.BlockSpec(memory_space=pltpu.VMEM)
    anywhere = pl.BlockSpec(memory_space=pl.ANY)
    ins = dict(cols=cols, tok=tok, cot=cot, pick=pick)
    far_ins = dict(mod_w_in=mod_w, qkv_w=qkv_w, out_w=out_w, up_w=up_w, down_w=down_w)
    near = dict(
        block_out=struct((rows, width), BF),
        grad_tokens=struct((rows, width), F32),
        dm=struct((nz, 8, each), F32),
        t_all=struct((PLANE, 32, width // PLANE), F32),
    )
    far = dict(
        c_down=struct((share, wide * PLANE), BF),
        c_up=struct((share, wide * PLANE), BF),
        c_qkv=struct((share, part * PLANE), BF),
        c_out=struct((heads // nz, width), BF),
        full_qkv=struct((nz * m, part), BF),
        full_out=struct((heads, width), BF),
        full_up=struct((nz * m, wide), BF),
        full_down=struct((nz * m, wide), BF),
        first=struct((tokens, width + 256), BF),
        second=struct((tokens, width), BF),
        dy=struct((tokens, width), BF),
        dat=struct((tokens, width), BF),
        qkv=struct((tokens, part), BF),
        mixed=struct((tokens, heads), BF),
        hid=struct((tokens, wide), BF),
        slope=struct((tokens, wide), F32),
        du=struct((tokens, wide), BF),
        part=struct((tokens, width), BF),
        part_y=struct((tokens, width), BF),
        dmix=struct((tokens, heads), BF),
        dqkv=struct((tokens, part), BF),
    )
    shapes = dict(
        down=(nz, m, wide), up=(nz, m, wide), qkv=(nz, m, part), out=(nz, heads // nz, width)
    )
    for key, shape in shapes.items():
        far["g_" + key] = struct(shape, BF)
        far["land_" + key] = struct(shape, BF)
    own = vm((rows, width), F32)
    scratch = dict(
        mods=vm((8, 6 * width), F32),
        img=vm((8, 6 * width), F32),
        ma=vm((nz, 2, 8, each), F32),
        mb=vm((PLANE, nz, 8, each), F32),
        xh=vm((rows, width + 256), BF),
        xv=vm((rows, width), BF),
        xg=vm((rows, width), BF),
        va=own,
        vb=own,
        vd=own,
        temps=vm((4, m, max(wide, part)), BF),
        temps_out=vm((4,) + shapes["out"][1:], BF),
        tsem=dma((6,)),
        mod_w=vm(mod_w.shape, BF),
        pa=vm((PLANE, 16, each), F32),
        ga_=vm((PLANE, 16, each), F32),
        gs=vm((nz, 8, each), F32),
        gb_=vm((nz, 8, each), F32),
        pc=vm((PLANE, 32, width // PLANE), F32),
        pd=vm((PLANE, 32, width // PLANE), F32),
        pe=vm((nz, 32, width // PLANE), F32),
        ts=vm((32, width // PLANE), F32),
    )

    def add(prefix, items):
        for i, item in enumerate(items):
            scratch[prefix + "." + str(i)] = item

    add("in_qkv", Share.shapes(qkv_w.shape, 3, dma))
    add("in_up", Share.shapes(up_w.shape, 1, dma))
    add("in_down", Share.shapes(down_w.shape, 1, dma))
    add("in_out", [vm(out_w.shape, BF), dma, dma((1,)), dma((1,))])
    add("mod_in", [dma((4,)), dma((4,)), dma((PLANE,)), dma((PLANE,))])
    add("mod_out", [dma((PLANE,))] * 10 + [dma((1,))])
    for key in ("ga", "gb", "gc", "gd"):
        add(key, Gather.shapes(dma))
    sc = Scatter.shapes(rows, width, dma)
    add("sc_a", sc[:8])
    add("sc_b", sc[:8])
    for i in range(1, 5):
        add("sems_" + str(i), sc[8:])
    for key, shape in shapes.items():
        add("z_" + key, PlaneCopy.shapes(dma))
        add("s_" + key, PlaneSum.shapes(shape[1], shape[2], dma))
    add("deal", [dma((b, PLANE)) for b in (1, 1, 1, 1, 3, 3)])
    names = list(ins) + list(far_ins) + list(near) + list(far) + list(scratch)
    outs = pl.pallas_call(
        functools.partial(whole_kernel, factor, names),
        out_shape=list(near.values()) + list(far.values()),
        in_specs=[vmem] * len(ins) + [anywhere] * len(far_ins),
        out_specs=[vmem] * len(near) + [anywhere] * len(far),
        scratch_shapes=list(scratch.values()),
        compiler_params=pltpu.CompilerParams(
            collective_id=ident, has_side_effects=True, vmem_limit_bytes=62 * MIB
        ),
        cost_estimate=pl.CostEstimate(
            flops=0, bytes_accessed=int(450 * 3.6e6), transcendentals=0
        ),
    )(*ins.values(), *far_ins.values())
    return dict(zip(list(near) + list(far), outs))


def norm_mod(value, shift, scale):
    normed = value * lax.rsqrt(jnp.mean(value * value, axis=-1, keepdims=True) + EPS)
    return normed * (1.0 + scale) + shift


def dot(a, b):
    return jnp.dot(a, b, preferred_element_type=F32)


def over_rows(left, right):
    return lax.dot_general(left, right, (((0,), (0,)), ((), ())), preferred_element_type=F32)


def times_t(left, right):
    return lax.dot_general(left, right, (((1,), (1,)), ((), ())), preferred_element_type=F32)


def allowed_pairs(seg, key, r):
    same = times_t(seg[r, :], key[...]) > 0.5
    rows = lax.broadcasted_iota(jnp.int32, same.shape, 0) + r.start
    return same | (rows == lax.broadcasted_iota(jnp.int32, same.shape, 1))


def softmax_rows(q, k, allowed, factor):
    scores = jnp.where(allowed, times_t(q, k) * factor, NEG)
    expo = jnp.exp(scores - jnp.max(scores, axis=-1, keepdims=True))
    return expo / jnp.sum(expo, axis=-1, keepdims=True)


def row_blocks(count):
    step = math.gcd(count, 256)
    return [slice(i, i + step) for i in range(0, count, step)]


def attend_kernel(factor, qkv, seg, key, o):
    n = o.shape[1]
    for r in row_blocks(o.shape[0]):
        allowed = allowed_pairs(seg, key, r)
        for c in range(0, n, HEAD_DIM):
            k = qkv[:, n + c : n + c + HEAD_DIM]
            v = qkv[:, 2 * n + c : 2 * n + c + HEAD_DIM]
            prob = softmax_rows(qkv[r, c : c + HEAD_DIM], k, allowed, factor)
            o[r, c : c + HEAD_DIM] = dot(prob.astype(BF), v).astype(BF)


def attend_back_kernel(factor, qkv, seg, key, d_o, d_qkv):
    n = d_o.shape[1]
    for c in range(0, n, HEAD_DIM):
        k = qkv[:, n + c : n + c + HEAD_DIM]
        v = qkv[:, 2 * n + c : 2 * n + c + HEAD_DIM]
        dk = dv = 0.0
        for r in row_blocks(d_o.shape[0]):
            q = qkv[r, c : c + HEAD_DIM]
            out = d_o[r, c : c + HEAD_DIM]
            prob = softmax_rows(q, k, allowed_pairs(seg, key, r), factor)
            d_prob = times_t(out, v)
            delta = jnp.sum(prob * d_prob, axis=-1, keepdims=True)
            d_scores = (prob * (d_prob - delta)).astype(BF)
            d_qkv[r, c : c + HEAD_DIM] = (dot(d_scores, k) * factor).astype(BF)
            dk = dk + over_rows(d_scores, q)
            dv = dv + over_rows(prob.astype(BF), out)
        d_qkv[:, n + c : n + c + HEAD_DIM] = (dk * factor).astype(BF)
        d_qkv[:, 2 * n + c : 2 * n + c + HEAD_DIM] = dv.astype(BF)


def per_group(kernel, qkv, first, d_o, columns, group, flops):
    last = first.shape[1] // 128
    block = lambda c: pl.BlockSpec((group, c), lambda i: (i, 0))
    mask = lambda c: pl.BlockSpec((group, 128), lambda i: (i, c))
    return pl.pallas_call(
        kernel,
        grid=(qkv.shape[0] // group,),
        out_shape=jax.ShapeDtypeStruct((qkv.shape[0], columns), BF),
        in_specs=[block(qkv.shape[1]), mask(last - 2), mask(last - 1)]
        + [block(a.shape[1]) for a in d_o],
        out_specs=block(columns),
        compiler_params=pltpu.CompilerParams(vmem_limit_bytes=48 * MIB),
        cost_estimate=pl.CostEstimate(flops=flops, bytes_accessed=0, transcendentals=0),
    )(qkv, first, first, *d_o)


def after(value, *others):
    return lax.optimization_barrier((value,) + others)[0]


def on_device(
    tokens,
    noise_table,
    mod_weight,
    qkv_weight,
    out_weight,
    up_weight,
    down_weight,
    segment,
    key_valid,
    noise_level,
    cotangent,
):
    rows, width = tokens.shape[1:]
    images = noise_level.shape[1]
    nz = lax.axis_size("z")
    blk = lax.axis_index("blk")
    groups = 2 * nz
    factor = 1.0 / math.sqrt(HEAD_DIM)
    levels = noise_level.reshape(-1)
    cond = jnp.take(noise_table, levels, axis=0)
    cols = dot(cond, mod_weight).reshape(groups, images, -1)
    cols = jnp.pad(cols, ((0, 0), (0, 8 - images), (0, 0)))

    own = lambda a: lax.dynamic_slice_in_dim(a[0], blk * rows, rows, 0)[:, None]
    lane = jnp.arange(256, dtype=jnp.int32)[None, :]
    hot = (own(segment) == lane % 128) & ((lane < 128) | (own(key_valid) == 1))
    pick = hot.astype(BF)

    args = (tokens[0], cotangent[0], pick, mod_weight)
    weights = (qkv_weight, out_weight, up_weight, down_weight)
    run = on_four_planes if nz == 4 else on_any_planes
    out = run(cols, *args, *weights, factor, images)
    block_out, grad_tokens, mod_grads, cond_grads, d_qkv_w, d_outp, d_up, d_down = out
    grad_mod = lax.dot_general(
        cond.astype(F32), mod_grads, (((0,), (0,)), ((), ())), precision=HIGH
    )
    grad_table = jax.ops.segment_sum(cond_grads, levels, num_segments=noise_table.shape[0])
    return (
        block_out[None],
        grad_tokens[None],
        grad_table,
        grad_mod,
        d_qkv_w.astype(F32),
        d_outp.astype(F32),
        d_up.astype(F32),
        d_down.astype(F32),
    )


def on_four_planes(
    cols, tok, cot, pick, mod_weight, qkv_weight, out_weight, up_weight, down_weight, factor, images
):
    out = whole_block(
        cols,
        tok,
        cot,
        pick,
        mod_weight,
        qkv_weight,
        out_weight,
        up_weight,
        down_weight,
        factor,
        1,
    )
    count, width = cols.shape[0] * images, tok.shape[1]
    mod_grads = out["dm"][:, : 2 * images].reshape(count, -1)
    cond_grads = out["t_all"].reshape(PLANE, 4, 8, width // PLANE)[:, :, : 2 * images]
    cond_grads = cond_grads.transpose(1, 2, 0, 3).reshape(count, width)
    return (
        out["block_out"],
        out["grad_tokens"],
        mod_grads,
        cond_grads,
        out["c_qkv"],
        out["c_out"],
        out["c_up"],
        out["c_down"],
    )


def on_any_planes(
    cols, tok, cot, pick, mod_weight, qkv_weight, out_weight, up_weight, down_weight, factor, images
):
    rows, width = tok.shape
    nz, blks = lax.axis_size("z"), lax.axis_size("blk")
    devices = nz * PLANE
    group = rows * blks
    own_cols = HEADS // PLANE * HEAD_DIM
    sent = jnp.broadcast_to(cols[:, None], (2 * nz, blks) + cols.shape[1:])
    mods = exchange(sent.reshape((devices,) + cols.shape[1:]), 14)[:, :images]
    mods = mods.transpose(1, 0, 2).reshape(images, 6, width)

    (qkv_part,) = spread([after(qkv_weight, mods)], 1, blocks=3)
    qkv_w = z_gather(qkv_part)
    move = [(nz * k + i, i * PLANE + k) for k in range(PLANE) for i in range(nz)]
    outp = lax.ppermute(after(out_weight, qkv_part), ALL, move)

    picker = pick[:, :images].astype(F32)
    shift1, scale1, gate1, shift2, scale2, gate2 = (
        jnp.dot(picker, mods[:, i], precision=HIGH) for i in range(6)
    )
    x_in, grad_in = tok.astype(F32), cot.astype(F32)
    first_f, first_back = jax.vjp(norm_mod, x_in, shift1, scale1)
    first = jnp.concatenate([first_f.astype(BF), pick], axis=1)
    first_all = plane_gather(after(first, qkv_part), 2)
    first = first_all[:, :width]
    up_part, down_part = spread([after(up_weight, first), down_weight], 3)
    outp_w, up_w, down_w = z_gather(outp), z_gather(up_part), z_gather(down_part)

    qkv = dot(first, qkv_w).astype(BF)
    cost = 4 * 2 * group * group * own_cols
    mixed = per_group(
        functools.partial(attend_kernel, factor), qkv, first_all, [], own_cols, group, 5 * cost
    )
    attn = plane_scatter(dot(mixed, outp_w).astype(BF), 6)
    x_mid = x_in + gate1 * attn
    second_f, second_back = jax.vjp(norm_mod, x_mid, shift2, scale2)
    second = plane_gather(second_f.astype(BF), 7)
    hidden_f, gelu_back = jax.vjp(jax.nn.gelu, dot(second, up_w))
    hidden = hidden_f.astype(BF)

    d_branch = plane_gather(after((gate2 * grad_in).astype(BF), hidden), 5)
    d_down = z_scatter(over_rows(d_branch, hidden).astype(BF))
    d_pre = gelu_back(dot(d_branch, down_w))[0].astype(BF)
    d_up = z_scatter(over_rows(second, d_pre).astype(BF))
    d_second = plane_scatter(times_t(d_pre, up_w).astype(BF), 9)
    d_mid_norm, d_shift2, d_scale2 = second_back(d_second)
    d_mid = grad_in + d_mid_norm
    d_gate1 = d_mid * attn
    d_attn = plane_gather((gate1 * d_mid).astype(BF), 10)
    d_mixed = times_t(d_attn, outp_w).astype(BF)
    d_qkv = per_group(
        functools.partial(attend_back_kernel, factor),
        qkv,
        first_all,
        [d_mixed],
        3 * own_cols,
        group,
        10 * cost,
    )
    d_qkv_w = z_scatter(over_rows(first, d_qkv).astype(BF))
    d_outp = z_scatter(over_rows(mixed, d_attn).astype(BF))
    d_first = plane_scatter(times_t(d_qkv, qkv_w).astype(BF), 11)
    d_in_norm, d_shift1, d_scale1 = first_back(d_first)
    part = times_t(after(hidden, d_first), down_w).astype(BF)
    branch = plane_scatter(part, 8)
    block_out = (x_mid + gate2 * branch).astype(BF)
    d_gate2 = grad_in * branch

    tok_grads = jnp.concatenate([d_shift1, d_scale1, d_gate1, d_shift2, d_scale2, d_gate2], axis=1)
    image_grads = lax.dot_general(
        pick[:, :8].astype(F32), tok_grads, (((0,), (0,)), ((), ())), precision=HIGH
    )
    sent = image_grads.reshape(8, devices, -1).transpose(1, 0, 2)
    mod_grads, cond_grads = mods_back(sent, mod_weight, 15)
    count = 2 * nz * images
    mod_grads = mod_grads[:, :images].reshape(count, -1)
    cond_grads = cond_grads.reshape(2 * nz, 4, 8, width // 4)[:, :, :images]
    cond_grads = cond_grads.transpose(0, 2, 1, 3).reshape(count, width)

    d_up, d_down = collect([after(d_up, sent), d_down], 12)
    (d_qkv_w,) = collect([after(d_qkv_w, d_up)], 13, blocks=3)
    d_outp = lax.ppermute(d_outp, ALL, [(b, a) for a, b in move])
    grads = (d_qkv_w, d_outp, d_up, d_down)
    return (block_out, d_mid + d_in_norm, mod_grads, cond_grads) + grads


def solution(mesh):
    groups, blks = mesh.shape["dp"], mesh.shape["blk"]
    planes = Mesh(mesh.devices.reshape(groups // 2, 2, blks), ALL)
    dp = ("z", "y")
    whole = ("z", "y", "blk")
    placed = (
        P(dp, "blk", None),
        P(),
        P(None, whole),
        P(whole, None),
        P(whole, None),
        P(whole, None),
        P(whole, None),
        P(dp, None),
        P(dp, None),
        P(),
        P(dp, "blk", None),
    )
    return jax.shard_map(
        on_device,
        mesh=planes,
        in_specs=placed,
        out_specs=(
            P(dp, "blk", None),
            P(dp, "blk", None),
            P(),
            P(None, whole),
            P(whole, None),
            P(whole, None),
            P(whole, None),
            P(whole, None),
        ),
        check_vma=False,
    )
```

```python
import functools
import math

import jax
import jax.numpy as jnp
from jax import lax
from jax.experimental import pallas as pl
from jax.experimental.pallas import tpu as pltpu
from jax.sharding import Mesh
from jax.sharding import PartitionSpec as P

HEADS = 16
HEAD_DIM = 128
EPS = 1e-06
NEG = -1e30
HIGH = lax.Precision.HIGHEST
PLANE = 8
BF = jnp.bfloat16
F32 = jnp.float32
ALL = ("z", "y", "blk")
MIB = 1 << 20


def peer(k):
    y, b = lax.axis_index("y"), lax.axis_index("blk")
    high, low = lax.div(b, 2), lax.rem(b, 2)
    if k & 4:
        y = 1 - y
    if k & 2:
        high = 1 - high
    if k & 1:
        low = 1 - low
    return {"y": y, "blk": high * 2 + low}


def place(k):
    where = peer(k)
    return where["y"] * 4 + where["blk"]


def greet(peers):
    barrier = pltpu.get_barrier_semaphore()
    for k in peers:
        pl.semaphore_signal(
            barrier, inc=1, device_id=peer(k), device_id_type=pl.DeviceIdType.MESH
        )
    pl.semaphore_wait(barrier, len(peers))


def send(src, dst, ssem, rsem, k):
    copy = pltpu.make_async_remote_copy(
        src_ref=src,
        dst_ref=dst,
        send_sem=ssem,
        recv_sem=rsem,
        device_id=peer(k),
        device_id_type=pl.DeviceIdType.MESH,
    )
    copy.start()
    return copy


def call(kernel, ins, outs, scratch, ident, vmem=16, micros=10):
    return pl.pallas_call(
        kernel,
        out_shape=outs,
        in_specs=[pl.BlockSpec(memory_space=pl.ANY)] * len(ins),
        out_specs=jax.tree.map(lambda _: pl.BlockSpec(memory_space=pl.ANY), outs),
        scratch_shapes=scratch,
        compiler_params=pltpu.CompilerParams(
            collective_id=ident, has_side_effects=True, vmem_limit_bytes=vmem * MIB
        ),
        cost_estimate=pl.CostEstimate(
            flops=0, bytes_accessed=int(micros * 3.6e6), transcendentals=0
        ),
    )(*ins)


class Gather:
    shapes = staticmethod(lambda dma: [dma((1,)), dma((13,)), dma((13,))])

    def __init__(self, xv, o, sems):
        self.xv, self.o = xv, o
        self.lsem, self.ssem, self.rsem = sems
        self.rows = xv.shape[0]
        self.all = []

    def block(self, k, part=None):
        half = self.rows // 2
        first = k * self.rows + (half if part == 1 else 0)
        return self.o.at[pl.ds(first, self.rows if part is None else half)]

    def mine(self, part):
        half = self.rows // 2
        return self.xv.at[pl.ds(part * half, half)]

    def go(self, src, dst, k):
        i = len(self.all)
        self.all.append(send(src, dst, self.ssem.at[i], self.rsem.at[i], k))
        return self.all[-1]

    def begin(self):
        self.x_bot = self.go(self.mine(1), self.block(2, 1), 2)
        self.y_top = self.go(self.mine(0), self.block(4, 0), 4)
        self.x_top = self.go(self.mine(0), self.block(2, 0), 2)
        self.y_bot = self.go(self.mine(1), self.block(4, 1), 4)
        self.sib = self.go(self.xv, self.block(1), 1)
        self.own = pltpu.make_async_copy(self.xv, self.block(0), self.lsem.at[0])
        self.own.start()

    def relay(self):
        self.x_bot.wait_recv()
        self.dy = self.go(self.block(2, 1), self.block(6, 1), 4)
        self.late = [self.go(self.block(2, 1), self.block(3, 1), 1)]
        self.y_top.wait_recv()
        self.dx = self.go(self.block(4, 0), self.block(6, 0), 2)
        self.late.append(self.go(self.block(4, 0), self.block(5, 0), 1))

    def finish(self):
        self.x_top.wait_recv()
        self.late.append(self.go(self.block(2, 0), self.block(3, 0), 1))
        self.y_bot.wait_recv()
        self.late.append(self.go(self.block(4, 1), self.block(5, 1), 1))
        self.dx.wait_recv()
        self.late.append(self.go(self.block(6, 0), self.block(7, 0), 1))
        self.dy.wait_recv()
        self.late.append(self.go(self.block(6, 1), self.block(7, 1), 1))
        for copy in [self.sib] + self.late:
            copy.wait_recv()
        for copy in self.all:
            copy.wait_send()
        self.own.wait()


def gather_kernel(x, o, xv, load_sem, *sems):
    load = pltpu.make_async_copy(x, xv, load_sem)
    load.start()
    greet((1, 2, 4))
    load.wait()
    gather = Gather(xv, o, sems)
    gather.begin()
    gather.relay()
    gather.finish()


def plane_gather(x, ident):
    out = jax.ShapeDtypeStruct((PLANE * x.shape[0],) + x.shape[1:], x.dtype)
    dma = pltpu.SemaphoreType.DMA
    scratch = [pltpu.VMEM(x.shape, x.dtype), dma] + Gather.shapes(dma)
    return call(gather_kernel, (x,), out, scratch, ident, 8, 30)


def rows_loop(rows, body, step=16):
    def one(i, carry):
        body(pl.multiple_of(i * step, step), step)
        return carry

    lax.fori_loop(0, rows // step, one, 0)


class Scatter:
    @staticmethod
    def shapes(rows, width, dma):
        whole = pltpu.VMEM((4, rows, width), BF)
        pair = pltpu.VMEM((2, rows // 2, width), BF)
        return [whole, whole] + [pair] * 6 + [dma((4,)), dma((11,)), dma((11,))]

    def __init__(self, p, ov, scratch):
        self.p, self.ov = p, ov
        self.pv, self.rc, self.q6, self.q2, self.q4, self.d6, self.rx, self.ry = scratch[:8]
        self.lsem, self.ssem, self.rsem = scratch[8:]
        self.rows = ov.shape[0]
        self.half = self.rows // 2

    def block(self, k, first=0, count=None):
        return self.p.at[pl.ds(k * self.rows + first, count or self.rows)]

    def go(self, i, src, dst, k):
        return send(src, dst, self.ssem.at[i], self.rsem.at[i], k)

    def begin(self):
        half = self.half
        top, bot = pl.ds(0, half), pl.ds(half, half)
        self.c7t = self.go(0, self.block(7, 0, half), self.rc.at[3, top], 1)
        self.c7b = self.go(1, self.block(7, half, half), self.rc.at[3, bot], 1)
        self.c3 = self.go(2, self.block(3), self.rc.at[1], 1)
        self.c5 = self.go(3, self.block(5), self.rc.at[2], 1)
        self.c1 = self.go(4, self.block(1), self.rc.at[0], 1)

    def load(self):
        self.loads = [
            pltpu.make_async_copy(self.block(2 * i), self.pv.at[i], self.lsem.at[i])
            for i in range(4)
        ]
        for i in (3, 1, 2, 0):
            self.loads[i].start()

    def add(self, dst, i, start, more=None):
        def body(r, n):
            s = pl.ds(pl.multiple_of(start + r, 16), n)
            total = self.pv[i, s, :].astype(F32) + self.rc[i, s, :].astype(F32)
            if more is not None:
                total = total + more[pl.ds(r, n), :].astype(F32)
            dst[pl.ds(r, n), :] = total.astype(BF)

        rows_loop(self.half, body)

    def middle(self):
        half = self.half
        self.loads[3].wait()
        self.c7t.wait_recv()
        self.add(self.q6.at[0], 3, 0)
        self.s6t = self.go(5, self.q6.at[0], self.d6.at[0], 2)
        self.c7b.wait_recv()
        self.add(self.q6.at[1], 3, half)
        self.s6b = self.go(6, self.q6.at[1], self.d6.at[1], 4)
        self.loads[1].wait()
        self.c3.wait_recv()
        self.add(self.q2.at[0], 1, 0)
        self.s2t = self.go(7, self.q2.at[0], self.rx.at[0], 2)
        self.loads[2].wait()
        self.c5.wait_recv()
        self.add(self.q4.at[1], 2, half)
        self.s4b = self.go(8, self.q4.at[1], self.ry.at[1], 4)

    def relay(self):
        self.s6t.wait_recv()
        self.add(self.q4.at[0], 2, 0, self.d6.at[0])
        self.s4t = self.go(9, self.q4.at[0], self.ry.at[0], 4)
        self.s6b.wait_recv()
        self.add(self.q2.at[1], 1, self.half, self.d6.at[1])
        self.s2b = self.go(10, self.q2.at[1], self.rx.at[1], 2)

    def total(self, n):
        def body(r, count):
            s = pl.ds(pl.multiple_of(n * self.half + r, 16), count)
            r = pl.ds(r, count)
            total = self.pv[0, s, :].astype(F32) + self.rc[0, s, :].astype(F32)
            total = total + self.rx[n, r, :].astype(F32) + self.ry[n, r, :].astype(F32)
            self.ov[s, :] = total

        rows_loop(self.half, body)

    def finish(self):
        self.loads[0].wait()
        self.c1.wait_recv()
        self.s2t.wait_recv()
        self.s4t.wait_recv()
        self.total(0)
        self.s2b.wait_recv()
        self.s4b.wait_recv()
        self.total(1)
        for copy in (self.c7t, self.c7b, self.c3, self.c5, self.c1, self.s6t, self.s6b):
            copy.wait_send()
        for copy in (self.s2t, self.s4b, self.s4t, self.s2b):
            copy.wait_send()


def scatter_kernel(p, o, ov, osem, *scratch):
    greet((1, 2, 4))
    scatter = Scatter(p, ov, scratch)
    scatter.begin()
    scatter.load()
    scatter.middle()
    scatter.relay()
    scatter.finish()
    out = pltpu.make_async_copy(ov, o, osem)
    out.start()
    out.wait()


def plane_scatter(p, ident):
    rows, width = p.shape[0] // PLANE, p.shape[1]
    dma = pltpu.SemaphoreType.DMA
    scratch = [pltpu.VMEM((rows, width), F32), dma] + Scatter.shapes(rows, width, dma)
    out = jax.ShapeDtypeStruct((rows, width), F32)
    return call(scatter_kernel, (p,), out, scratch, ident, 24, 31)


def cut(weights, blocks):
    plan = []
    for i, cols in enumerate(weights):
        each = cols // blocks
        for b in range(blocks):
            plan.append((i, b * each, each // PLANE, b * (each // PLANE)))
    return plan


def spread_kernel(plan, count, *refs):
    ins, outs, held = refs[:count], refs[count : 2 * count], refs[2 * count : 3 * count]
    lsem, ssem, rsem = refs[3 * count :]
    loads = [pltpu.make_async_copy(a, v, lsem.at[i]) for i, (a, v) in enumerate(zip(ins, held))]
    for copy in loads:
        copy.start()
    greet(range(1, PLANE))
    mine = place(0)
    remotes = []
    for w, load in enumerate(loads):
        load.wait()
        rows = ins[w].shape[0]
        here = pl.ds(pl.multiple_of(mine * rows, 16), rows)
        for n, (i, base, width, col) in enumerate(plan):
            if i != w:
                continue
            for k in (6, 7, 2, 3, 4, 5, 1):
                cols = pl.ds(pl.multiple_of(base + place(k) * width, 128), width)
                remotes.append(
                    send(
                        held[w].at[:, cols],
                        outs[w].at[here, pl.ds(col, width)],
                        ssem.at[n, k],
                        rsem.at[n, k],
                        k,
                    )
                )
            cols = pl.ds(pl.multiple_of(base + mine * width, 128), width)
            copy = pltpu.make_async_copy(
                held[w].at[:, cols], outs[w].at[here, pl.ds(col, width)], ssem.at[n, 0]
            )
            copy.start()
            remotes.append(copy)
    for copy in remotes:
        copy.wait()


def spread(weights, ident, blocks=1):
    plan = cut([w.shape[1] for w in weights], blocks)
    outs = [
        jax.ShapeDtypeStruct((w.shape[0] * PLANE, w.shape[1] // PLANE), w.dtype) for w in weights
    ]
    dma = pltpu.SemaphoreType.DMA
    n = len(plan)
    scratch = [pltpu.VMEM(w.shape, w.dtype) for w in weights]
    return call(
        functools.partial(spread_kernel, plan, len(weights)),
        tuple(weights),
        outs,
        scratch + [dma((len(weights),)), dma((n, PLANE)), dma((n, PLANE))],
        ident,
        8,
        sum(w.size for w in weights) / 3e4,
    )


def collect_kernel(plan, count, *refs):
    ins, outs, held = refs[:count], refs[count : 2 * count], refs[2 * count : 3 * count]
    lsem, ssem, rsem = refs[3 * count :]
    loads = [pltpu.make_async_copy(a, v, lsem.at[i]) for i, (a, v) in enumerate(zip(ins, held))]
    for copy in loads:
        copy.start()
    greet(range(1, PLANE))
    mine = place(0)
    remotes = []
    for w, load in enumerate(loads):
        load.wait()
        rows = outs[w].shape[0]
        for n, (i, base, width, col) in enumerate(plan):
            if i != w:
                continue
            cols = pl.ds(pl.multiple_of(base + mine * width, 128), width)
            for k in (6, 7, 2, 3, 4, 5, 1):
                there = pl.ds(pl.multiple_of(place(k) * rows, 16), rows)
                remotes.append(
                    send(
                        held[w].at[there, pl.ds(col, width)],
                        outs[w].at[:, cols],
                        ssem.at[n, k],
                        rsem.at[n, k],
                        k,
                    )
                )
            here = pl.ds(pl.multiple_of(mine * rows, 16), rows)
            copy = pltpu.make_async_copy(
                held[w].at[here, pl.ds(col, width)], outs[w].at[:, cols], ssem.at[n, 0]
            )
            copy.start()
            remotes.append(copy)
    for copy in remotes:
        copy.wait()


def collect(grads, ident, blocks=1):
    plan = cut([g.shape[1] * PLANE for g in grads], blocks)
    outs = [
        jax.ShapeDtypeStruct((g.shape[0] // PLANE, g.shape[1] * PLANE), g.dtype) for g in grads
    ]
    dma = pltpu.SemaphoreType.DMA
    n = len(plan)
    scratch = [pltpu.VMEM(g.shape, g.dtype) for g in grads]
    return call(
        functools.partial(collect_kernel, plan, len(grads)),
        tuple(grads),
        outs,
        scratch + [dma((len(grads),)), dma((n, PLANE)), dma((n, PLANE))],
        ident,
        8,
        sum(g.size for g in grads) / 3e4,
    )


def flat_place():
    return lax.axis_index("z") * PLANE + lax.axis_index("y") * 4 + lax.axis_index("blk")


def flat_id(d):
    return {"z": lax.div(d, PLANE), "y": lax.rem(lax.div(d, 4), 2), "blk": lax.rem(d, 4)}


def greet_all(count):
    barrier = pltpu.get_barrier_semaphore()
    me = flat_place()

    def one(i, carry):
        pl.semaphore_signal(
            barrier,
            inc=1,
            device_id=flat_id(lax.rem(me + i, count)),
            device_id_type=pl.DeviceIdType.MESH,
        )
        return carry

    lax.fori_loop(1, count, one, 0)
    pl.semaphore_wait(barrier, count - 1)


def to_all(count, source, target, ssem, rsem):
    me = flat_place()

    def copy(i):
        d = lax.rem(me + i, count)
        return pltpu.make_async_remote_copy(
            src_ref=source(d),
            dst_ref=target.at[me],
            send_sem=ssem.at[i],
            recv_sem=rsem.at[i],
            device_id=flat_id(d),
            device_id_type=pl.DeviceIdType.MESH,
        )

    def begin(i, carry):
        copy(i).start()
        return carry

    def finish(i, carry):
        copy(i).wait()
        return carry

    lax.fori_loop(1, count, begin, 0)
    target[me] = source(me)[...]
    lax.fori_loop(1, count, finish, 0)


def exchange_kernel(count, x, o, ssem, rsem):
    greet_all(count)
    to_all(count, lambda d: x.at[d], o, ssem, rsem)


def small_call(kernel, ins, outs, scratch, ident, micros):
    vmem = pl.BlockSpec(memory_space=pltpu.VMEM)
    return pl.pallas_call(
        kernel,
        out_shape=outs,
        in_specs=[vmem] * len(ins),
        out_specs=jax.tree.map(lambda _: vmem, outs),
        scratch_shapes=scratch,
        compiler_params=pltpu.CompilerParams(
            collective_id=ident, has_side_effects=True, vmem_limit_bytes=32 * MIB
        ),
        cost_estimate=pl.CostEstimate(
            flops=0, bytes_accessed=int(micros * 3.6e6), transcendentals=0
        ),
    )(*ins)


def exchange(x, ident):
    dma = pltpu.SemaphoreType.DMA((x.shape[0],))
    return small_call(
        functools.partial(exchange_kernel, x.shape[0]),
        (x,),
        jax.ShapeDtypeStruct(x.shape, x.dtype),
        [dma, dma],
        ident,
        8,
    )


def mods_back_kernel(count, x, w, o, t, got, part, mine, s0, r0, s1, r1, s2, r2):
    greet_all(count)
    to_all(count, lambda d: x.at[d], got, s0, r0)
    groups = o.shape[0]
    for g in range(groups):
        o[g] = got[4 * g] + got[4 * g + 1] + got[4 * g + 2] + got[4 * g + 3]
    own = o[...].reshape(groups * 8, o.shape[2])
    high = own.astype(BF)
    rest = own - high.astype(F32)
    low = rest.astype(BF)
    quarter = w.shape[0] // 4
    for q in range(4):
        piece = w[q * quarter : (q + 1) * quarter, :]
        product = times_t(high, piece) + times_t(low, piece)
        for g in range(groups):
            part[4 * g + q] = product[8 * g : 8 * g + 8]
    to_all(count, lambda d: part.at[d], mine, s1, r1)

    def add(i, total):
        return total + mine[i]

    part[flat_place()] = lax.fori_loop(0, count, add, jnp.zeros(mine.shape[1:], F32))
    to_all(count, lambda d: part.at[flat_place()], t, s2, r2)


def mods_back(x, w, ident):
    count, eight, cols = x.shape
    width = w.shape[0]
    dma = pltpu.SemaphoreType.DMA((count,))
    pieces = jax.ShapeDtypeStruct((count, eight, width // 4), F32)
    return small_call(
        functools.partial(mods_back_kernel, count),
        (x, w),
        (jax.ShapeDtypeStruct((count // 4, eight, cols), F32), pieces),
        [pltpu.VMEM(x.shape, F32), pltpu.VMEM(pieces.shape, F32), pltpu.VMEM(pieces.shape, F32)]
        + [dma] * 6,
        ident,
        20,
    )


def z_gather(x):
    return lax.all_gather(x, "z", axis=0, tiled=True)


def z_scatter(g):
    return lax.psum_scatter(g, "z", scatter_dimension=0, tiled=True)


def z_peer(m):
    z = lax.axis_index("z")
    if m == 1:
        z = z + 1 - 2 * lax.rem(z, 2)
    elif m == 2:
        z = lax.rem(z + 2, 4)
    else:
        z = 3 - z
    return z


def inner_plane():
    z = lax.axis_index("z")
    return (z == 1) | (z == 2)


def outer_plane():
    z = lax.axis_index("z")
    return (z == 0) | (z == 3)


def remote(src, dst, ssem, rsem, where):
    return pltpu.make_async_remote_copy(
        src_ref=src,
        dst_ref=dst,
        send_sem=ssem,
        recv_sem=rsem,
        device_id=where,
        device_id_type=pl.DeviceIdType.MESH,
    )


class OutRows:
    def __init__(self):
        z, j = lax.axis_index("z"), place(0)
        me = z * PLANE + j
        self.slot = lax.rem(me, 4)
        self.user = self.flat(self.slot * PLANE + lax.div(me, 4))
        self.owner = self.flat(4 * j + z)
        self.away, self.home = me != 4 * j + z, me == 4 * j + z

    @staticmethod
    def flat(d):
        return flat_id(d)


def greet_more(outs):
    barrier = pltpu.get_barrier_semaphore()

    def signal(where):
        pl.semaphore_signal(
            barrier, inc=1, device_id=where, device_id_type=pl.DeviceIdType.MESH
        )

    ids = [peer(k) for k in range(1, PLANE)] + [{"z": z_peer(m)} for m in (1, 2, 3)]
    for where in ids:
        signal(where)

    @pl.when(outs.away)
    def _():
        signal(outs.user)
        signal(outs.owner)
        pl.semaphore_wait(barrier, len(ids) + 2)

    pl.when(outs.home)(lambda: pl.semaphore_wait(barrier, len(ids)))


class PlaneCopy:
    shapes = staticmethod(lambda dma: [dma((4,)), dma((4,))])

    def __init__(self, full, sems):
        self.full = full
        self.m = full.shape[0] // 4
        self.ssem, self.rsem = sems

    def copy(self, slot, t, m):
        block = self.full.at[pl.ds(pl.multiple_of(t * self.m, self.m), self.m)]
        return remote(block, block, self.ssem.at[slot], self.rsem.at[slot], {"z": z_peer(m)})

    def begin(self):
        z = lax.axis_index("z")
        self.copy(1, z, 2).start()
        self.copy(0, z, 1).start()

    def relay(self):
        @pl.when(inner_plane())
        def _():
            self.copy(1, z_peer(2), 2).wait_recv()
            self.copy(3, z_peer(2), 1).start()
            self.copy(2, lax.axis_index("z"), 3).start()

    def finish(self):
        z = lax.axis_index("z")
        self.copy(0, z_peer(1), 1).wait_recv()

        @pl.when(inner_plane())
        def _():
            self.copy(2, z_peer(3), 3).wait_recv()
            self.copy(2, z, 3).wait_send()
            self.copy(3, z_peer(2), 1).wait_send()

        @pl.when(outer_plane())
        def _():
            self.copy(1, z_peer(2), 2).wait_recv()
            self.copy(3, z_peer(3), 1).wait_recv()

        self.copy(0, z, 1).wait_send()
        self.copy(1, z, 2).wait_send()


class PlaneSum:
    @staticmethod
    def shapes(m, c, dma):
        return [pltpu.VMEM((m, c), BF), dma((4,)), dma((4,))]

    def __init__(self, g, landing, scratch, temps):
        self.g, self.landing, self.temps = g, landing, temps
        self.q, self.ssem, self.rsem = scratch
        self.m, self.c = g.shape[1:]
        self.inner, self.outer = inner_plane(), outer_plane()

    def copy(self, src, slot, m):
        return pltpu.make_async_remote_copy(
            src_ref=src,
            dst_ref=self.landing.at[slot],
            send_sem=self.ssem.at[slot],
            recv_sem=self.rsem.at[slot],
            device_id={"z": z_peer(m)},
            device_id_type=pl.DeviceIdType.MESH,
        )

    def begin_far(self):
        pl.when(self.outer)(lambda: self.copy(self.g.at[z_peer(3)], 2, 1).start())

    def begin_swap(self):
        pl.when(self.inner)(lambda: self.copy(self.g.at[z_peer(3)], 3, 3).start())

    def begin(self):
        self.begin_far()
        self.begin_swap()

    def temp(self, i):
        return self.temps.at[i, pl.ds(0, self.m), pl.ds(0, self.c)]

    def load(self, src, i):
        copy = pltpu.make_async_copy(src, self.temp(i), self.tsem.at[i])
        copy.start()
        return copy

    def hop(self, tsem):
        self.tsem = tsem
        across = self.g.at[z_peer(2)]

        @pl.when(self.outer)
        def _():
            self.copy(across, 1, 2).start()

        @pl.when(self.inner)
        def _():
            first = self.load(across, 0)
            self.copy(across, 2, 1).wait_recv()
            second = self.load(self.landing.at[2], 1)
            first.wait()
            second.wait()

            def body(r, n):
                r = (pl.ds(r, n), pl.ds(0, self.c))
                total = self.temps[(0,) + r].astype(F32) + self.temps[(1,) + r].astype(F32)
                self.q[r] = total.astype(BF)

            rows_loop(self.m, body)
            self.copy(self.q, 1, 2).start()

        self.near = self.copy(self.g.at[z_peer(1)], 0, 1)
        self.near.start()

    def finish(self, tsem):
        self.tsem = tsem
        loads = [self.load(self.g.at[lax.axis_index("z")], 0)]
        self.near.wait_recv()
        loads.append(self.load(self.landing.at[0], 1))
        far = self.copy(self.q, 1, 2)
        far.wait_recv()
        loads.append(self.load(self.landing.at[1], 2))
        pl.when(self.inner)(lambda: self.copy(self.g.at[0], 3, 3).wait_recv())
        pl.when(self.inner)(lambda: self.load(self.landing.at[3], 3).wait())
        for copy in loads:
            copy.wait()
        far.wait_send()
        self.near.wait_send()
        pl.when(self.outer)(lambda: self.copy(self.g.at[0], 2, 1).wait_send())
        pl.when(self.inner)(lambda: self.copy(self.g.at[0], 3, 3).wait_send())

        def three(r, n):
            r = (pl.ds(r, n), pl.ds(0, self.c))
            total = self.temps[(0,) + r].astype(F32) + self.temps[(1,) + r].astype(F32)
            return r, total + self.temps[(2,) + r].astype(F32)

        def outer(r, n):
            r, total = three(r, n)
            self.q[r] = total.astype(BF)

        def inner(r, n):
            r, total = three(r, n)
            self.q[r] = (total + self.temps[(3,) + r].astype(F32)).astype(BF)

        pl.when(self.outer)(lambda: rows_loop(self.m, outer))
        pl.when(self.inner)(lambda: rows_loop(self.m, inner))


def deal(src, out, blocks, ssem, rsem):
    rows = out.shape[0]
    mine = place(0)
    copies = []
    for n, (_, base, width, col) in enumerate(cut([out.shape[1]], blocks)):
        cols = pl.ds(pl.multiple_of(base + mine * width, 128), width)
        for k in (6, 7, 2, 3, 4, 5, 1, 0):
            there = pl.ds(pl.multiple_of(place(k) * rows, 16), rows)
            piece = src.at[there, pl.ds(col, width)]
            if k:
                copies.append(send(piece, out.at[:, cols], ssem.at[n, k], rsem.at[n, k], k))
            else:
                copies.append(pltpu.make_async_copy(piece, out.at[:, cols], ssem.at[n, 0]))
                copies[-1].start()
    return copies


def pipe(body, steps, ins, outs):
    spec = lambda a: pl.BlockSpec(a[1], a[2])
    pltpu.emit_pipeline(
        body, grid=(steps,), in_specs=[spec(a) for a in ins], out_specs=[spec(a) for a in outs]
    )(*[a[0] for a in ins], *[a[0] for a in outs])


def whole(a):
    return (a, a.shape, lambda i: (0,) * len(a.shape))


def some_rows(a, n, pick=lambda i: i):
    return (a, (n, a.shape[1]), lambda i: (pick(i), 0))


def grads_mm(a, b, g):
    m = g.shape[1]

    def body(a, b, g):
        g[0] = over_rows(a[...], b[...]).astype(BF)

    pipe(
        body,
        g.shape[0],
        [(a, (a.shape[0], m), lambda i: (0, i)), whole(b)],
        [(g, (1,) + g.shape[1:], lambda i: (i, 0, 0))],
    )


def rows_mm(a, b, o, n, steps, pick=lambda i: i, transposed=False):
    def body(a, b, o):
        o[...] = (times_t if transposed else dot)(a[...], b[...]).astype(BF)

    pipe(body, steps, [some_rows(a, n, pick), whole(b)], [some_rows(o, n, pick)])


class Share:
    @staticmethod
    def shapes(w, blocks, dma):
        return [pltpu.VMEM(w, BF), dma, dma((blocks, PLANE)), dma((blocks, PLANE))]

    def __init__(self, w, full, blocks, scratch):
        self.w, self.full, self.blocks = w, full, blocks
        self.held, self.lsem, self.ssem, self.rsem = scratch
        self.load = pltpu.make_async_copy(w, self.held, self.lsem)
        self.load.start()

    def begin(self):
        self.load.wait()
        rows = self.w.shape[0]
        first = lax.axis_index("z") * (PLANE * rows) + place(0) * rows
        here = pl.ds(pl.multiple_of(first, rows), rows)
        self.copies = []
        for n, (_, base, width, col) in enumerate(cut([self.w.shape[1]], self.blocks)):
            dst = self.full.at[here, pl.ds(col, width)]
            for k in (6, 7, 2, 3, 4, 5, 1, 0):
                cols = pl.ds(pl.multiple_of(base + place(k) * width, 128), width)
                src = self.held.at[:, cols]
                if k:
                    copy = send(src, dst, self.ssem.at[n, k], self.rsem.at[n, k], k)
                else:
                    copy = pltpu.make_async_copy(src, dst, self.ssem.at[n, 0])
                    copy.start()
                self.copies.append(copy)

    def finish(self):
        for copy in self.copies:
            copy.wait()


IMAGES = 3


def whole_kernel(factor, names, *refs):
    v = dict(zip(names, refs))
    get = lambda *keys: [v[key] for key in keys]
    group_of = lambda prefix: [v[key] for key in names if key.startswith(prefix + ".")]
    cols, tok, cot, pick, mods = get("cols", "tok", "cot", "pick", "mods")
    first, second, dy, dat = get("first", "second", "dy", "dat")
    qkv, mixed, hid, slope = get("qkv", "mixed", "hid", "slope")
    du, part, part_y, dmix, dqkv = get("du", "part", "part_y", "dmix", "dqkv")
    xh, xv, xg, va, vb, vd = get("xh", "xv", "xg", "va", "vb", "vd")
    block_out, grad_tokens = get("block_out", "grad_tokens")
    img, temps, temps_out, tsem = get("img", "temps", "temps_out", "tsem")
    rows, width = tok.shape
    tokens = dy.shape[0]
    group = 4 * rows
    z, y, mine = lax.axis_index("z"), lax.axis_index("y"), place(0)
    odd, even = (lambda i: 2 * i + 1), (lambda i: 2 * i)
    outs = OutRows()

    qkv_in = Share(v["qkv_w"], v["full_qkv"], 3, group_of("in_qkv"))
    up_in = Share(v["up_w"], v["full_up"], 1, group_of("in_up"))
    down_in = Share(v["down_w"], v["full_down"], 1, group_of("in_down"))
    held, lsem, osems, rsems = group_of("in_out")
    out_load = pltpu.make_async_copy(v["out_w"], held, lsem)
    out_load.start()
    out_block = v["out_w"].shape[0]
    full_out = v["full_out"]
    out_at = lambda i: full_out.at[pl.ds(pl.multiple_of(i * out_block, out_block), out_block)]
    out_in = remote(held, out_at(outs.slot), osems.at[0], rsems.at[0], outs.user)
    out_local = pltpu.make_async_copy(held, out_at(z), osems.at[0])
    greet_more(outs)

    ma, mb = get("ma", "mb")
    sa, ra, sb, rb = group_of("mod_in")
    sent = []
    for m in (1, 2, 3):
        src = cols.at[pl.ds(2 * z_peer(m), 2)]
        sent.append(remote(src, ma.at[z], sa.at[m], ra.at[m], {"z": z_peer(m)}))
        sent[-1].start()
    out_load.wait()
    pl.when(outs.away)(lambda: out_in.start())
    pl.when(outs.home)(lambda: out_local.start())
    qkv_in.begin()
    ma[z] = cols[pl.ds(2 * z, 2)]
    for copy in sent:
        copy.wait()
    sent = []
    for k in range(1, PLANE):
        src = ma.at[:, peer(k)["y"]]
        sent.append(send(src, mb.at[mine], sb.at[k], rb.at[k], k))
    pl.when(outs.away)(lambda: out_in.wait())
    pl.when(outs.home)(lambda: out_local.wait())
    z_out = PlaneCopy(full_out, group_of("z_out"))
    z_out.begin()
    qkv_in.finish()
    z_qkv = PlaneCopy(v["full_qkv"], group_of("z_qkv"))
    z_qkv.begin()
    mb[mine] = ma[:, y]
    for copy in sent:
        copy.wait()
    each = cols.shape[2]
    for d in range(4 * PLANE):
        mods[:, d * each : (d + 1) * each] = mb[d % PLANE, d // PLANE]

    def picker(r):
        hot = pick[r, 0:128]
        ones = [hot[:, i : i + 1].astype(F32) for i in range(IMAGES)]

        def mod(which):
            at = slice(which * width, (which + 1) * width)
            return sum(ones[i] * mods[i : i + 1, at] for i in range(IMAGES))

        return mod

    def normed_of(x):
        inv = lax.rsqrt(jnp.mean(x * x, axis=-1, keepdims=True) + EPS)
        return inv, x * inv

    def norm_grad(inv, normed, d_normed):
        slant = jnp.mean(d_normed * normed, axis=-1, keepdims=True)
        return inv * (d_normed - normed * slant)

    def make_first(r, n):
        r = pl.ds(r, n)
        mod = picker(r)
        _, normed = normed_of(tok[r, :].astype(F32))
        xh[r, 0:width] = (normed * (1.0 + mod(1)) + mod(0)).astype(BF)
        xh[r, width:] = pick[r, :]
        xg[r, :] = (mod(5) * cot[r, :].astype(F32)).astype(BF)

    rows_loop(rows, make_first)
    to_first = Gather(xh, first, group_of("ga"))
    to_first.begin()
    up_in.begin()
    z_out.relay()
    to_first.relay()
    z_qkv.relay()
    to_first.finish()
    down_in.begin()
    up_in.finish()
    z_qkv.finish()
    z_up = PlaneCopy(v["full_up"], group_of("z_up"))
    z_up.begin()

    n = math.gcd(tokens, 256)

    def mm_body(a, b, o):
        o[...] = dot(a[...], b[...]).astype(BF)

    pipe(mm_body, tokens // n, [some_rows(first.at[:, 0:width], n), whole(v["full_qkv"])], [some_rows(qkv, n)])
    masks = [
        some_rows(first.at[:, width : width + 128], group),
        some_rows(first.at[:, width + 128 : width + 256], group),
    ]
    pipe(
        functools.partial(attend_kernel, factor),
        2,
        [some_rows(qkv, group)] + masks,
        [some_rows(mixed, group)],
    )
    down_in.finish()
    z_out.finish()
    rows_mm(mixed, full_out, part, rows, 4, odd)
    r_attn = Scatter(part, va, group_of("sc_a") + group_of("sems_1"))
    r_attn.begin()
    rows_mm(mixed, full_out, part, rows, 4, even)
    r_attn.load()
    r_attn.middle()
    r_attn.relay()
    z_up.relay()
    z_down = PlaneCopy(v["full_down"], group_of("z_down"))
    z_down.begin()
    r_attn.finish()

    def make_second(r, n):
        r = pl.ds(r, n)
        mod = picker(r)
        x = tok[r, :].astype(F32) + mod(2) * va[r, :]
        vd[r, :] = x
        xv[r, :] = (normed_of(x)[1] * (1.0 + mod(4)) + mod(3)).astype(BF)

    rows_loop(rows, make_second)
    to_second = Gather(xv, second, group_of("gb"))
    to_second.begin()
    to_second.relay()
    to_second.finish()
    to_dy = Gather(xg, dy, group_of("gc"))
    to_dy.begin()
    z_up.finish()

    def up_body(a, b, h, s):
        u = dot(a[...], b[...])
        c = math.sqrt(2.0 / math.pi)
        t = jnp.tanh(c * (u + 0.044715 * (u * u * u)))
        h[...] = (0.5 * u * (1.0 + t)).astype(BF)
        inside = c * (1.0 + (3 * 0.044715) * (u * u))
        s[...] = 0.5 * (1.0 + t) + 0.5 * u * (1.0 - t * t) * inside

    pipe(
        up_body,
        tokens // n,
        [some_rows(second, n), whole(v["full_up"])],
        [some_rows(hid, n), some_rows(slope, n)],
    )
    to_dy.relay()
    z_down.relay()
    to_dy.finish()
    sums = [
        PlaneSum(v["g_" + key], v["land_" + key], group_of("s_" + key), t)
        for key, t in (("down", temps), ("up", temps), ("qkv", temps), ("out", temps_out))
    ]
    s_down, s_up, s_qkv, s_out = sums
    grads_mm(dy, hid, v["g_down"])
    s_down.begin_far()
    z_down.finish()
    s_down.begin_swap()

    def du_body(a, b, s, o):
        o[...] = (dot(a[...], b[...]) * s[...]).astype(BF)

    pipe(
        du_body,
        tokens // n,
        [some_rows(dy, n), whole(v["full_down"]), some_rows(slope, n)],
        [some_rows(du, n)],
    )
    s_down.hop(tsem)
    rows_mm(du, v["full_up"], part, rows, 4, odd, True)
    r_e2 = Scatter(part, vb, group_of("sc_a") + group_of("sems_2"))
    r_e2.begin()
    rows_mm(du, v["full_up"], part, rows, 4, even, True)
    r_e2.load()
    r_e2.middle()
    grads_mm(second, du, v["g_up"])
    s_up.begin()
    r_e2.relay()
    r_e2.finish()

    pv = v["sc_b.0"]
    parts = [(pv.at[0], pv.at[1]), (pv.at[2], pv.at[3]), (xg, xh.at[:, 0:width])]

    def tally(which, r, value):
        high = value.astype(BF)
        parts[which][0][r, :] = high
        parts[which][1][r, :] = (value - high.astype(F32)).astype(BF)

    def flush(blocks):
        hot = pick[:, 0:128]
        for (high, low), which in zip(parts, blocks):
            total = over_rows(hot, high[...]) + over_rows(hot, low[...])
            img[:, which * width : (which + 1) * width] = total[0:8]

    def norm_back(r, n):
        r = pl.ds(r, n)
        mod = picker(r)
        inv, normed = normed_of(vd[r, :])
        e = vb[r, :]
        d_mid = cot[r, :].astype(F32) + norm_grad(inv, normed, e * (1.0 + mod(4)))
        grad_tokens[r, :] = d_mid
        xv[r, :] = (mod(2) * d_mid).astype(BF)
        tally(0, r, e)
        tally(1, r, e * normed)
        tally(2, r, d_mid * va[r, :])

    rows_loop(rows, norm_back)
    load_w = pltpu.make_async_copy(v["mod_w_in"], v["mod_w"], group_of("mod_out")[10].at[0])
    load_w.start()
    to_dat = Gather(xv, dat, group_of("gd"))
    to_dat.begin()
    flush((3, 4, 2))
    rows_mm(hid, v["full_down"], part_y, rows, 8, transposed=True)
    to_dat.relay()
    s_up.hop(tsem)
    to_dat.finish()
    r_y = Scatter(part_y, va, group_of("sc_b") + group_of("sems_3"))
    r_y.begin()
    r_y.load()
    rows_mm(dat, full_out, dmix, 2 * rows, 4, transposed=True)
    r_y.middle()
    pipe(
        functools.partial(attend_back_kernel, factor),
        2,
        [some_rows(qkv, group)] + masks + [some_rows(dmix, group)],
        [some_rows(dqkv, group)],
    )
    r_y.relay()
    grads_mm(first.at[:, 0:width], dqkv, v["g_qkv"])
    s_qkv.begin()
    dealt = []
    deal_sems = group_of("deal")

    def settle(s, out, blocks, sems):
        s.finish(tsem)
        dealt.extend(deal(s.q, out, blocks, *sems))

    r_y.finish()
    rows_mm(dqkv, v["full_qkv"], part, rows, 4, odd, True)
    r_e1 = Scatter(part, vb, group_of("sc_a") + group_of("sems_4"))
    r_e1.begin()
    rows_mm(dqkv, v["full_qkv"], part, rows, 4, even, True)
    r_e1.load()
    r_e1.middle()
    s_qkv.hop(tsem)

    def out_body(a, b, g):
        g[...] = over_rows(a[...], b[...]).astype(BF).reshape(g.shape)

    step = math.gcd(width, 512)
    g_out = v["g_out"]
    pipe(
        out_body,
        width // step,
        [whole(mixed), (dat, (tokens, step), lambda i: (0, i))],
        [(g_out, g_out.shape[:2] + (step,), lambda i: (0, 0, i))],
    )
    s_out.begin()
    r_e1.relay()
    s_out.hop(tsem)
    settle(s_down, v["c_down"], 1, deal_sems[:2])
    r_e1.finish()

    def last_norm(r, n):
        r = pl.ds(r, n)
        mod = picker(r)
        inv, normed = normed_of(tok[r, :].astype(F32))
        e, out = vb[r, :], va[r, :]
        grad_tokens[r, :] += norm_grad(inv, normed, e * (1.0 + mod(1)))
        block_out[r, :] = (vd[r, :] + mod(5) * out).astype(BF)
        tally(0, r, e)
        tally(1, r, e * normed)
        tally(2, r, cot[r, :].astype(F32) * out)

    rows_loop(rows, last_norm)
    flush((0, 1, 5))

    pa, ga, gs, gb, pc, pd, pe, ts = get("pa", "ga_", "gs", "gb_", "pc", "pd", "pe", "ts")
    w, t_all, dm = get("mod_w", "t_all", "dm")
    sems = group_of("mod_out")
    for d in range(4 * PLANE):
        t = d // PLANE * IMAGES
        pa[d % PLANE, t : t + IMAGES] = img[0:IMAGES, d * each : (d + 1) * each]
    plane_sent = lambda src, dst, s, r: [
        send(src(k), dst, s.at[k], r.at[k], k) for k in range(1, PLANE)
    ]
    sent = plane_sent(lambda k: pa.at[place(k)], ga.at[mine], sems[0], sems[1])
    ga[mine] = pa[mine]
    gs[...] = jnp.zeros_like(gs)
    for copy in sent:
        copy.wait()
    for g in range(2):
        total = ga[4 * g] + ga[4 * g + 1] + ga[4 * g + 2] + ga[4 * g + 3]
        for t in range(4):
            gs[t, g * IMAGES : (g + 1) * IMAGES] = total[t * IMAGES : (t + 1) * IMAGES]
    sent = []
    for m in (1, 2, 3):
        copy = remote(
            gs.at[z_peer(m)], gb.at[z], sems[2].at[m], sems[3].at[m], {"z": z_peer(m)}
        )
        copy.start()
        sent.append(copy)
    gb[z] = gs[z]
    s_up.finish(tsem)
    s_out.finish(tsem)
    back = remote(s_out.q, v["c_out"], tsem.at[4], tsem.at[5], outs.owner)
    back_local = pltpu.make_async_copy(s_out.q, v["c_out"], tsem.at[4])
    pl.when(outs.away)(lambda: back.start())
    pl.when(outs.home)(lambda: back_local.start())
    for copy in sent:
        copy.wait()
    load_w.wait()
    dm[...] = gb[...]
    own = dm[...].reshape(4 * 8, each)
    high = own.astype(BF)
    low = (own - high.astype(F32)).astype(BF)
    slice_of = width // PLANE
    for k in range(PLANE):
        piece = w[k * slice_of : (k + 1) * slice_of, :]
        pc[k] = times_t(high, piece) + times_t(low, piece)
    sent = plane_sent(lambda k: pc.at[place(k)], pd.at[mine], sems[4], sems[5])
    pd[mine] = pc[mine]
    dealt.extend(deal(s_up.q, v["c_up"], 1, *deal_sems[2:4]))
    for copy in sent:
        copy.wait()
    total = pd[0]
    for k in range(1, PLANE):
        total = total + pd[k]
    pe[z] = total
    sent = []
    for m in (1, 2, 3):
        copy = remote(pe.at[z], pe.at[z], sems[6].at[m], sems[7].at[m], {"z": z_peer(m)})
        copy.start()
        sent.append(copy)
    settle(s_qkv, v["c_qkv"], 3, deal_sems[4:6])
    for copy in sent:
        copy.wait()
    ts[...] = pe[0] + pe[1] + pe[2] + pe[3]
    sent = plane_sent(lambda k: ts, t_all.at[mine], sems[8], sems[9])
    t_all[mine] = ts[...]
    for copy in sent:
        copy.wait()
    for copy in dealt:
        copy.wait()
    pl.when(outs.away)(lambda: back.wait())
    pl.when(outs.home)(lambda: back_local.wait())


def whole_block(cols, tok, cot, pick, mod_w, qkv_w, out_w, up_w, down_w, factor, ident):
    rows, width = tok.shape
    nz, tokens = 4, PLANE * rows
    share = qkv_w.shape[0]
    m = share * PLANE
    wide, part, heads = up_w.shape[1] // PLANE, qkv_w.shape[1] // PLANE, nz * out_w.shape[0]
    each = cols.shape[2]
    struct, vm, dma = jax.ShapeDtypeStruct, pltpu.VMEM, pltpu.SemaphoreType.DMA
    vmem = pl.BlockSpec(memory_space=pltpu.VMEM)
    anywhere = pl.BlockSpec(memory_space=pl.ANY)
    ins = dict(cols=cols, tok=tok, cot=cot, pick=pick)
    far_ins = dict(mod_w_in=mod_w, qkv_w=qkv_w, out_w=out_w, up_w=up_w, down_w=down_w)
    near = dict(
        block_out=struct((rows, width), BF),
        grad_tokens=struct((rows, width), F32),
        dm=struct((nz, 8, each), F32),
        t_all=struct((PLANE, 32, width // PLANE), F32),
    )
    far = dict(
        c_down=struct((share, wide * PLANE), BF),
        c_up=struct((share, wide * PLANE), BF),
        c_qkv=struct((share, part * PLANE), BF),
        c_out=struct((heads // nz, width), BF),
        full_qkv=struct((nz * m, part), BF),
        full_out=struct((heads, width), BF),
        full_up=struct((nz * m, wide), BF),
        full_down=struct((nz * m, wide), BF),
        first=struct((tokens, width + 256), BF),
        second=struct((tokens, width), BF),
        dy=struct((tokens, width), BF),
        dat=struct((tokens, width), BF),
        qkv=struct((tokens, part), BF),
        mixed=struct((tokens, heads), BF),
        hid=struct((tokens, wide), BF),
        slope=struct((tokens, wide), F32),
        du=struct((tokens, wide), BF),
        part=struct((tokens, width), BF),
        part_y=struct((tokens, width), BF),
        dmix=struct((tokens, heads), BF),
        dqkv=struct((tokens, part), BF),
    )
    shapes = dict(
        down=(nz, m, wide), up=(nz, m, wide), qkv=(nz, m, part), out=(nz, heads // nz, width)
    )
    for key, shape in shapes.items():
        far["g_" + key] = struct(shape, BF)
        far["land_" + key] = struct(shape, BF)
    own = vm((rows, width), F32)
    scratch = dict(
        mods=vm((8, 6 * width), F32),
        img=vm((8, 6 * width), F32),
        ma=vm((nz, 2, 8, each), F32),
        mb=vm((PLANE, nz, 8, each), F32),
        xh=vm((rows, width + 256), BF),
        xv=vm((rows, width), BF),
        xg=vm((rows, width), BF),
        va=own,
        vb=own,
        vd=own,
        temps=vm((4, m, max(wide, part)), BF),
        temps_out=vm((4,) + shapes["out"][1:], BF),
        tsem=dma((6,)),
        mod_w=vm(mod_w.shape, BF),
        pa=vm((PLANE, 16, each), F32),
        ga_=vm((PLANE, 16, each), F32),
        gs=vm((nz, 8, each), F32),
        gb_=vm((nz, 8, each), F32),
        pc=vm((PLANE, 32, width // PLANE), F32),
        pd=vm((PLANE, 32, width // PLANE), F32),
        pe=vm((nz, 32, width // PLANE), F32),
        ts=vm((32, width // PLANE), F32),
    )

    def add(prefix, items):
        for i, item in enumerate(items):
            scratch[prefix + "." + str(i)] = item

    add("in_qkv", Share.shapes(qkv_w.shape, 3, dma))
    add("in_up", Share.shapes(up_w.shape, 1, dma))
    add("in_down", Share.shapes(down_w.shape, 1, dma))
    add("in_out", [vm(out_w.shape, BF), dma, dma((1,)), dma((1,))])
    add("mod_in", [dma((4,)), dma((4,)), dma((PLANE,)), dma((PLANE,))])
    add("mod_out", [dma((PLANE,))] * 10 + [dma((1,))])
    for key in ("ga", "gb", "gc", "gd"):
        add(key, Gather.shapes(dma))
    sc = Scatter.shapes(rows, width, dma)
    add("sc_a", sc[:8])
    add("sc_b", sc[:8])
    for i in range(1, 5):
        add("sems_" + str(i), sc[8:])
    for key, shape in shapes.items():
        add("z_" + key, PlaneCopy.shapes(dma))
        add("s_" + key, PlaneSum.shapes(shape[1], shape[2], dma))
    add("deal", [dma((b, PLANE)) for b in (1, 1, 1, 1, 3, 3)])
    names = list(ins) + list(far_ins) + list(near) + list(far) + list(scratch)
    outs = pl.pallas_call(
        functools.partial(whole_kernel, factor, names),
        out_shape=list(near.values()) + list(far.values()),
        in_specs=[vmem] * len(ins) + [anywhere] * len(far_ins),
        out_specs=[vmem] * len(near) + [anywhere] * len(far),
        scratch_shapes=list(scratch.values()),
        compiler_params=pltpu.CompilerParams(
            collective_id=ident, has_side_effects=True, vmem_limit_bytes=62 * MIB
        ),
        cost_estimate=pl.CostEstimate(
            flops=0, bytes_accessed=int(450 * 3.6e6), transcendentals=0
        ),
    )(*ins.values(), *far_ins.values())
    return dict(zip(list(near) + list(far), outs))


def norm_mod(value, shift, scale):
    normed = value * lax.rsqrt(jnp.mean(value * value, axis=-1, keepdims=True) + EPS)
    return normed * (1.0 + scale) + shift


def dot(a, b):
    return jnp.dot(a, b, preferred_element_type=F32)


def over_rows(left, right):
    return lax.dot_general(left, right, (((0,), (0,)), ((), ())), preferred_element_type=F32)


def times_t(left, right):
    return lax.dot_general(left, right, (((1,), (1,)), ((), ())), preferred_element_type=F32)


def allowed_pairs(seg, key, r):
    same = times_t(seg[r, :], key[...]) > 0.5
    rows = lax.broadcasted_iota(jnp.int32, same.shape, 0) + r.start
    return same | (rows == lax.broadcasted_iota(jnp.int32, same.shape, 1))


def softmax_rows(q, k, allowed, factor):
    scores = jnp.where(allowed, times_t(q, k) * factor, NEG)
    expo = jnp.exp(scores - jnp.max(scores, axis=-1, keepdims=True))
    return expo / jnp.sum(expo, axis=-1, keepdims=True)


def row_blocks(count):
    step = math.gcd(count, 256)
    return [slice(i, i + step) for i in range(0, count, step)]


def attend_kernel(factor, qkv, seg, key, o):
    n = o.shape[1]
    for r in row_blocks(o.shape[0]):
        allowed = allowed_pairs(seg, key, r)
        for c in range(0, n, HEAD_DIM):
            k = qkv[:, n + c : n + c + HEAD_DIM]
            v = qkv[:, 2 * n + c : 2 * n + c + HEAD_DIM]
            prob = softmax_rows(qkv[r, c : c + HEAD_DIM], k, allowed, factor)
            o[r, c : c + HEAD_DIM] = dot(prob.astype(BF), v).astype(BF)


def attend_back_kernel(factor, qkv, seg, key, d_o, d_qkv):
    n = d_o.shape[1]
    for c in range(0, n, HEAD_DIM):
        k = qkv[:, n + c : n + c + HEAD_DIM]
        v = qkv[:, 2 * n + c : 2 * n + c + HEAD_DIM]
        dk = dv = 0.0
        for r in row_blocks(d_o.shape[0]):
            q = qkv[r, c : c + HEAD_DIM]
            out = d_o[r, c : c + HEAD_DIM]
            prob = softmax_rows(q, k, allowed_pairs(seg, key, r), factor)
            d_prob = times_t(out, v)
            delta = jnp.sum(prob * d_prob, axis=-1, keepdims=True)
            d_scores = (prob * (d_prob - delta)).astype(BF)
            d_qkv[r, c : c + HEAD_DIM] = (dot(d_scores, k) * factor).astype(BF)
            dk = dk + over_rows(d_scores, q)
            dv = dv + over_rows(prob.astype(BF), out)
        d_qkv[:, n + c : n + c + HEAD_DIM] = (dk * factor).astype(BF)
        d_qkv[:, 2 * n + c : 2 * n + c + HEAD_DIM] = dv.astype(BF)


def per_group(kernel, qkv, first, d_o, columns, group, flops):
    last = first.shape[1] // 128
    block = lambda c: pl.BlockSpec((group, c), lambda i: (i, 0))
    mask = lambda c: pl.BlockSpec((group, 128), lambda i: (i, c))
    return pl.pallas_call(
        kernel,
        grid=(qkv.shape[0] // group,),
        out_shape=jax.ShapeDtypeStruct((qkv.shape[0], columns), BF),
        in_specs=[block(qkv.shape[1]), mask(last - 2), mask(last - 1)]
        + [block(a.shape[1]) for a in d_o],
        out_specs=block(columns),
        compiler_params=pltpu.CompilerParams(vmem_limit_bytes=48 * MIB),
        cost_estimate=pl.CostEstimate(flops=flops, bytes_accessed=0, transcendentals=0),
    )(qkv, first, first, *d_o)


def after(value, *others):
    return lax.optimization_barrier((value,) + others)[0]


def on_device(
    tokens,
    noise_table,
    mod_weight,
    qkv_weight,
    out_weight,
    up_weight,
    down_weight,
    segment,
    key_valid,
    noise_level,
    cotangent,
):
    rows, width = tokens.shape[1:]
    images = noise_level.shape[1]
    nz = lax.axis_size("z")
    blk = lax.axis_index("blk")
    groups = 2 * nz
    factor = 1.0 / math.sqrt(HEAD_DIM)
    levels = noise_level.reshape(-1)
    cond = jnp.take(noise_table, levels, axis=0)
    cols = dot(cond, mod_weight).reshape(groups, images, -1)
    cols = jnp.pad(cols, ((0, 0), (0, 8 - images), (0, 0)))

    own = lambda a: lax.dynamic_slice_in_dim(a[0], blk * rows, rows, 0)[:, None]
    lane = jnp.arange(256, dtype=jnp.int32)[None, :]
    hot = (own(segment) == lane % 128) & ((lane < 128) | (own(key_valid) == 1))
    pick = hot.astype(BF)

    args = (tokens[0], cotangent[0], pick, mod_weight)
    weights = (qkv_weight, out_weight, up_weight, down_weight)
    run = on_four_planes if nz == 4 else on_any_planes
    out = run(cols, *args, *weights, factor, images)
    block_out, grad_tokens, mod_grads, cond_grads, d_qkv_w, d_outp, d_up, d_down = out
    grad_mod = lax.dot_general(
        cond.astype(F32), mod_grads, (((0,), (0,)), ((), ())), precision=HIGH
    )
    grad_table = jax.ops.segment_sum(cond_grads, levels, num_segments=noise_table.shape[0])
    return (
        block_out[None],
        grad_tokens[None],
        grad_table,
        grad_mod,
        d_qkv_w.astype(F32),
        d_outp.astype(F32),
        d_up.astype(F32),
        d_down.astype(F32),
    )


def on_four_planes(
    cols, tok, cot, pick, mod_weight, qkv_weight, out_weight, up_weight, down_weight, factor, images
):
    out = whole_block(
        cols,
        tok,
        cot,
        pick,
        mod_weight,
        qkv_weight,
        out_weight,
        up_weight,
        down_weight,
        factor,
        1,
    )
    count, width = cols.shape[0] * images, tok.shape[1]
    mod_grads = out["dm"][:, : 2 * images].reshape(count, -1)
    cond_grads = out["t_all"].reshape(PLANE, 4, 8, width // PLANE)[:, :, : 2 * images]
    cond_grads = cond_grads.transpose(1, 2, 0, 3).reshape(count, width)
    return (
        out["block_out"],
        out["grad_tokens"],
        mod_grads,
        cond_grads,
        out["c_qkv"],
        out["c_out"],
        out["c_up"],
        out["c_down"],
    )


def on_any_planes(
    cols, tok, cot, pick, mod_weight, qkv_weight, out_weight, up_weight, down_weight, factor, images
):
    rows, width = tok.shape
    nz, blks = lax.axis_size("z"), lax.axis_size("blk")
    devices = nz * PLANE
    group = rows * blks
    own_cols = HEADS // PLANE * HEAD_DIM
    sent = jnp.broadcast_to(cols[:, None], (2 * nz, blks) + cols.shape[1:])
    mods = exchange(sent.reshape((devices,) + cols.shape[1:]), 14)[:, :images]
    mods = mods.transpose(1, 0, 2).reshape(images, 6, width)

    (qkv_part,) = spread([after(qkv_weight, mods)], 1, blocks=3)
    qkv_w = z_gather(qkv_part)
    move = [(nz * k + i, i * PLANE + k) for k in range(PLANE) for i in range(nz)]
    outp = lax.ppermute(after(out_weight, qkv_part), ALL, move)

    picker = pick[:, :images].astype(F32)
    shift1, scale1, gate1, shift2, scale2, gate2 = (
        jnp.dot(picker, mods[:, i], precision=HIGH) for i in range(6)
    )
    x_in, grad_in = tok.astype(F32), cot.astype(F32)
    first_f, first_back = jax.vjp(norm_mod, x_in, shift1, scale1)
    first = jnp.concatenate([first_f.astype(BF), pick], axis=1)
    first_all = plane_gather(after(first, qkv_part), 2)
    first = first_all[:, :width]
    up_part, down_part = spread([after(up_weight, first), down_weight], 3)
    outp_w, up_w, down_w = z_gather(outp), z_gather(up_part), z_gather(down_part)

    qkv = dot(first, qkv_w).astype(BF)
    cost = 4 * 2 * group * group * own_cols
    mixed = per_group(
        functools.partial(attend_kernel, factor), qkv, first_all, [], own_cols, group, 5 * cost
    )
    attn = plane_scatter(dot(mixed, outp_w).astype(BF), 6)
    x_mid = x_in + gate1 * attn
    second_f, second_back = jax.vjp(norm_mod, x_mid, shift2, scale2)
    second = plane_gather(second_f.astype(BF), 7)
    hidden_f, gelu_back = jax.vjp(jax.nn.gelu, dot(second, up_w))
    hidden = hidden_f.astype(BF)

    d_branch = plane_gather(after((gate2 * grad_in).astype(BF), hidden), 5)
    d_down = z_scatter(over_rows(d_branch, hidden).astype(BF))
    d_pre = gelu_back(dot(d_branch, down_w))[0].astype(BF)
    d_up = z_scatter(over_rows(second, d_pre).astype(BF))
    d_second = plane_scatter(times_t(d_pre, up_w).astype(BF), 9)
    d_mid_norm, d_shift2, d_scale2 = second_back(d_second)
    d_mid = grad_in + d_mid_norm
    d_gate1 = d_mid * attn
    d_attn = plane_gather((gate1 * d_mid).astype(BF), 10)
    d_mixed = times_t(d_attn, outp_w).astype(BF)
    d_qkv = per_group(
        functools.partial(attend_back_kernel, factor),
        qkv,
        first_all,
        [d_mixed],
        3 * own_cols,
        group,
        10 * cost,
    )
    d_qkv_w = z_scatter(over_rows(first, d_qkv).astype(BF))
    d_outp = z_scatter(over_rows(mixed, d_attn).astype(BF))
    d_first = plane_scatter(times_t(d_qkv, qkv_w).astype(BF), 11)
    d_in_norm, d_shift1, d_scale1 = first_back(d_first)
    part = times_t(after(hidden, d_first), down_w).astype(BF)
    branch = plane_scatter(part, 8)
    block_out = (x_mid + gate2 * branch).astype(BF)
    d_gate2 = grad_in * branch

    tok_grads = jnp.concatenate([d_shift1, d_scale1, d_gate1, d_shift2, d_scale2, d_gate2], axis=1)
    image_grads = lax.dot_general(
        pick[:, :8].astype(F32), tok_grads, (((0,), (0,)), ((), ())), precision=HIGH
    )
    sent = image_grads.reshape(8, devices, -1).transpose(1, 0, 2)
    mod_grads, cond_grads = mods_back(sent, mod_weight, 15)
    count = 2 * nz * images
    mod_grads = mod_grads[:, :images].reshape(count, -1)
    cond_grads = cond_grads.reshape(2 * nz, 4, 8, width // 4)[:, :, :images]
    cond_grads = cond_grads.transpose(0, 2, 1, 3).reshape(count, width)

    d_up, d_down = collect([after(d_up, sent), d_down], 12)
    (d_qkv_w,) = collect([after(d_qkv_w, d_up)], 13, blocks=3)
    d_outp = lax.ppermute(d_outp, ALL, [(b, a) for a, b in move])
    grads = (d_qkv_w, d_outp, d_up, d_down)
    return (block_out, d_mid + d_in_norm, mod_grads, cond_grads) + grads


def solution(mesh):
    groups, blks = mesh.shape["dp"], mesh.shape["blk"]
    planes = Mesh(mesh.devices.reshape(groups // 2, 2, blks), ALL)
    dp = ("z", "y")
    whole = ("z", "y", "blk")
    placed = (
        P(dp, "blk", None),
        P(),
        P(None, whole),
        P(whole, None),
        P(whole, None),
        P(whole, None),
        P(whole, None),
        P(dp, None),
        P(dp, None),
        P(),
        P(dp, "blk", None),
    )
    return jax.shard_map(
        on_device,
        mesh=planes,
        in_specs=placed,
        out_specs=(
            P(dp, "blk", None),
            P(dp, "blk", None),
            P(),
            P(None, whole),
            P(whole, None),
            P(whole, None),
            P(whole, None),
            P(whole, None),
        ),
        check_vma=False,
    )
```

```python
import functools
import math

import jax
import jax.numpy as jnp
from jax import lax
from jax.experimental import pallas as pl
from jax.experimental.pallas import tpu as pltpu
from jax.sharding import Mesh
from jax.sharding import PartitionSpec as P

HEADS = 16
HEAD_DIM = 128
EPS = 1e-06
NEG = -1e30
HIGH = lax.Precision.HIGHEST
PLANE = 8
BF = jnp.bfloat16
F32 = jnp.float32
ALL = ("z", "y", "blk")
MIB = 1 << 20


def peer(k):
    y, b = lax.axis_index("y"), lax.axis_index("blk")
    high, low = lax.div(b, 2), lax.rem(b, 2)
    if k & 4:
        y = 1 - y
    if k & 2:
        high = 1 - high
    if k & 1:
        low = 1 - low
    return {"y": y, "blk": high * 2 + low}


def place(k):
    where = peer(k)
    return where["y"] * 4 + where["blk"]


def greet(peers):
    barrier = pltpu.get_barrier_semaphore()
    for k in peers:
        pl.semaphore_signal(
            barrier, inc=1, device_id=peer(k), device_id_type=pl.DeviceIdType.MESH
        )
    pl.semaphore_wait(barrier, len(peers))


def send(src, dst, ssem, rsem, k):
    copy = pltpu.make_async_remote_copy(
        src_ref=src,
        dst_ref=dst,
        send_sem=ssem,
        recv_sem=rsem,
        device_id=peer(k),
        device_id_type=pl.DeviceIdType.MESH,
    )
    copy.start()
    return copy


def call(kernel, ins, outs, scratch, ident, vmem=16, micros=10):
    return pl.pallas_call(
        kernel,
        out_shape=outs,
        in_specs=[pl.BlockSpec(memory_space=pl.ANY)] * len(ins),
        out_specs=jax.tree.map(lambda _: pl.BlockSpec(memory_space=pl.ANY), outs),
        scratch_shapes=scratch,
        compiler_params=pltpu.CompilerParams(
            collective_id=ident, has_side_effects=True, vmem_limit_bytes=vmem * MIB
        ),
        cost_estimate=pl.CostEstimate(
            flops=0, bytes_accessed=int(micros * 3.6e6), transcendentals=0
        ),
    )(*ins)


class Gather:
    shapes = staticmethod(lambda dma: [dma((1,)), dma((13,)), dma((13,))])

    def __init__(self, xv, o, sems):
        self.xv, self.o = xv, o
        self.lsem, self.ssem, self.rsem = sems
        self.rows = xv.shape[0]
        self.all = []

    def block(self, k, part=None):
        half = self.rows // 2
        first = k * self.rows + (half if part == 1 else 0)
        return self.o.at[pl.ds(first, self.rows if part is None else half)]

    def mine(self, part):
        half = self.rows // 2
        return self.xv.at[pl.ds(part * half, half)]

    def go(self, src, dst, k):
        i = len(self.all)
        self.all.append(send(src, dst, self.ssem.at[i], self.rsem.at[i], k))
        return self.all[-1]

    def begin(self):
        self.x_bot = self.go(self.mine(1), self.block(2, 1), 2)
        self.y_top = self.go(self.mine(0), self.block(4, 0), 4)
        self.x_top = self.go(self.mine(0), self.block(2, 0), 2)
        self.y_bot = self.go(self.mine(1), self.block(4, 1), 4)
        self.sib = self.go(self.xv, self.block(1), 1)
        self.own = pltpu.make_async_copy(self.xv, self.block(0), self.lsem.at[0])
        self.own.start()

    def relay(self):
        self.x_bot.wait_recv()
        self.dy = self.go(self.block(2, 1), self.block(6, 1), 4)
        self.late = [self.go(self.block(2, 1), self.block(3, 1), 1)]
        self.y_top.wait_recv()
        self.dx = self.go(self.block(4, 0), self.block(6, 0), 2)
        self.late.append(self.go(self.block(4, 0), self.block(5, 0), 1))

    def finish(self):
        self.x_top.wait_recv()
        self.late.append(self.go(self.block(2, 0), self.block(3, 0), 1))
        self.y_bot.wait_recv()
        self.late.append(self.go(self.block(4, 1), self.block(5, 1), 1))
        self.dx.wait_recv()
        self.late.append(self.go(self.block(6, 0), self.block(7, 0), 1))
        self.dy.wait_recv()
        self.late.append(self.go(self.block(6, 1), self.block(7, 1), 1))
        for copy in [self.sib] + self.late:
            copy.wait_recv()
        for copy in self.all:
            copy.wait_send()
        self.own.wait()


def gather_kernel(x, o, xv, load_sem, *sems):
    load = pltpu.make_async_copy(x, xv, load_sem)
    load.start()
    greet((1, 2, 4))
    load.wait()
    gather = Gather(xv, o, sems)
    gather.begin()
    gather.relay()
    gather.finish()


def plane_gather(x, ident):
    out = jax.ShapeDtypeStruct((PLANE * x.shape[0],) + x.shape[1:], x.dtype)
    dma = pltpu.SemaphoreType.DMA
    scratch = [pltpu.VMEM(x.shape, x.dtype), dma] + Gather.shapes(dma)
    return call(gather_kernel, (x,), out, scratch, ident, 8, 30)


def rows_loop(rows, body, step=16):
    def one(i, carry):
        body(pl.multiple_of(i * step, step), step)
        return carry

    lax.fori_loop(0, rows // step, one, 0)


class Scatter:
    @staticmethod
    def shapes(rows, width, dma):
        whole = pltpu.VMEM((4, rows, width), BF)
        pair = pltpu.VMEM((2, rows // 2, width), BF)
        return [whole, whole] + [pair] * 6 + [dma((4,)), dma((11,)), dma((11,))]

    def __init__(self, p, ov, scratch):
        self.p, self.ov = p, ov
        self.pv, self.rc, self.q6, self.q2, self.q4, self.d6, self.rx, self.ry = scratch[:8]
        self.lsem, self.ssem, self.rsem = scratch[8:]
        self.rows = ov.shape[0]
        self.half = self.rows // 2

    def block(self, k, first=0, count=None):
        return self.p.at[pl.ds(k * self.rows + first, count or self.rows)]

    def go(self, i, src, dst, k):
        return send(src, dst, self.ssem.at[i], self.rsem.at[i], k)

    def begin(self):
        half = self.half
        top, bot = pl.ds(0, half), pl.ds(half, half)
        self.c7t = self.go(0, self.block(7, 0, half), self.rc.at[3, top], 1)
        self.c7b = self.go(1, self.block(7, half, half), self.rc.at[3, bot], 1)
        self.c3 = self.go(2, self.block(3), self.rc.at[1], 1)
        self.c5 = self.go(3, self.block(5), self.rc.at[2], 1)
        self.c1 = self.go(4, self.block(1), self.rc.at[0], 1)

    def load(self):
        self.loads = [
            pltpu.make_async_copy(self.block(2 * i), self.pv.at[i], self.lsem.at[i])
            for i in range(4)
        ]
        for i in (3, 1, 2, 0):
            self.loads[i].start()

    def add(self, dst, i, start, more=None):
        def body(r, n):
            s = pl.ds(pl.multiple_of(start + r, 16), n)
            total = self.pv[i, s, :].astype(F32) + self.rc[i, s, :].astype(F32)
            if more is not None:
                total = total + more[pl.ds(r, n), :].astype(F32)
            dst[pl.ds(r, n), :] = total.astype(BF)

        rows_loop(self.half, body)

    def middle(self):
        half = self.half
        self.loads[3].wait()
        self.c7t.wait_recv()
        self.add(self.q6.at[0], 3, 0)
        self.s6t = self.go(5, self.q6.at[0], self.d6.at[0], 2)
        self.c7b.wait_recv()
        self.add(self.q6.at[1], 3, half)
        self.s6b = self.go(6, self.q6.at[1], self.d6.at[1], 4)
        self.loads[1].wait()
        self.c3.wait_recv()
        self.add(self.q2.at[0], 1, 0)
        self.s2t = self.go(7, self.q2.at[0], self.rx.at[0], 2)
        self.loads[2].wait()
        self.c5.wait_recv()
        self.add(self.q4.at[1], 2, half)
        self.s4b = self.go(8, self.q4.at[1], self.ry.at[1], 4)

    def relay(self):
        self.s6t.wait_recv()
        self.add(self.q4.at[0], 2, 0, self.d6.at[0])
        self.s4t = self.go(9, self.q4.at[0], self.ry.at[0], 4)
        self.s6b.wait_recv()
        self.add(self.q2.at[1], 1, self.half, self.d6.at[1])
        self.s2b = self.go(10, self.q2.at[1], self.rx.at[1], 2)

    def total(self, n):
        def body(r, count):
            s = pl.ds(pl.multiple_of(n * self.half + r, 16), count)
            r = pl.ds(r, count)
            total = self.pv[0, s, :].astype(F32) + self.rc[0, s, :].astype(F32)
            total = total + self.rx[n, r, :].astype(F32) + self.ry[n, r, :].astype(F32)
            self.ov[s, :] = total

        rows_loop(self.half, body)

    def finish(self):
        self.loads[0].wait()
        self.c1.wait_recv()
        self.s2t.wait_recv()
        self.s4t.wait_recv()
        self.total(0)
        self.s2b.wait_recv()
        self.s4b.wait_recv()
        self.total(1)
        for copy in (self.c7t, self.c7b, self.c3, self.c5, self.c1, self.s6t, self.s6b):
            copy.wait_send()
        for copy in (self.s2t, self.s4b, self.s4t, self.s2b):
            copy.wait_send()


def scatter_kernel(p, o, ov, osem, *scratch):
    greet((1, 2, 4))
    scatter = Scatter(p, ov, scratch)
    scatter.begin()
    scatter.load()
    scatter.middle()
    scatter.relay()
    scatter.finish()
    out = pltpu.make_async_copy(ov, o, osem)
    out.start()
    out.wait()


def plane_scatter(p, ident):
    rows, width = p.shape[0] // PLANE, p.shape[1]
    dma = pltpu.SemaphoreType.DMA
    scratch = [pltpu.VMEM((rows, width), F32), dma] + Scatter.shapes(rows, width, dma)
    out = jax.ShapeDtypeStruct((rows, width), F32)
    return call(scatter_kernel, (p,), out, scratch, ident, 24, 31)


def cut(weights, blocks):
    plan = []
    for i, cols in enumerate(weights):
        each = cols // blocks
        for b in range(blocks):
            plan.append((i, b * each, each // PLANE, b * (each // PLANE)))
    return plan


def spread_kernel(plan, count, *refs):
    ins, outs, held = refs[:count], refs[count : 2 * count], refs[2 * count : 3 * count]
    lsem, ssem, rsem = refs[3 * count :]
    loads = [pltpu.make_async_copy(a, v, lsem.at[i]) for i, (a, v) in enumerate(zip(ins, held))]
    for copy in loads:
        copy.start()
    greet(range(1, PLANE))
    mine = place(0)
    remotes = []
    for w, load in enumerate(loads):
        load.wait()
        rows = ins[w].shape[0]
        here = pl.ds(pl.multiple_of(mine * rows, 16), rows)
        for n, (i, base, width, col) in enumerate(plan):
            if i != w:
                continue
            for k in (6, 7, 2, 3, 4, 5, 1):
                cols = pl.ds(pl.multiple_of(base + place(k) * width, 128), width)
                remotes.append(
                    send(
                        held[w].at[:, cols],
                        outs[w].at[here, pl.ds(col, width)],
                        ssem.at[n, k],
                        rsem.at[n, k],
                        k,
                    )
                )
            cols = pl.ds(pl.multiple_of(base + mine * width, 128), width)
            copy = pltpu.make_async_copy(
                held[w].at[:, cols], outs[w].at[here, pl.ds(col, width)], ssem.at[n, 0]
            )
            copy.start()
            remotes.append(copy)
    for copy in remotes:
        copy.wait()


def spread(weights, ident, blocks=1):
    plan = cut([w.shape[1] for w in weights], blocks)
    outs = [
        jax.ShapeDtypeStruct((w.shape[0] * PLANE, w.shape[1] // PLANE), w.dtype) for w in weights
    ]
    dma = pltpu.SemaphoreType.DMA
    n = len(plan)
    scratch = [pltpu.VMEM(w.shape, w.dtype) for w in weights]
    return call(
        functools.partial(spread_kernel, plan, len(weights)),
        tuple(weights),
        outs,
        scratch + [dma((len(weights),)), dma((n, PLANE)), dma((n, PLANE))],
        ident,
        8,
        sum(w.size for w in weights) / 3e4,
    )


def collect_kernel(plan, count, *refs):
    ins, outs, held = refs[:count], refs[count : 2 * count], refs[2 * count : 3 * count]
    lsem, ssem, rsem = refs[3 * count :]
    loads = [pltpu.make_async_copy(a, v, lsem.at[i]) for i, (a, v) in enumerate(zip(ins, held))]
    for copy in loads:
        copy.start()
    greet(range(1, PLANE))
    mine = place(0)
    remotes = []
    for w, load in enumerate(loads):
        load.wait()
        rows = outs[w].shape[0]
        for n, (i, base, width, col) in enumerate(plan):
            if i != w:
                continue
            cols = pl.ds(pl.multiple_of(base + mine * width, 128), width)
            for k in (6, 7, 2, 3, 4, 5, 1):
                there = pl.ds(pl.multiple_of(place(k) * rows, 16), rows)
                remotes.append(
                    send(
                        held[w].at[there, pl.ds(col, width)],
                        outs[w].at[:, cols],
                        ssem.at[n, k],
                        rsem.at[n, k],
                        k,
                    )
                )
            here = pl.ds(pl.multiple_of(mine * rows, 16), rows)
            copy = pltpu.make_async_copy(
                held[w].at[here, pl.ds(col, width)], outs[w].at[:, cols], ssem.at[n, 0]
            )
            copy.start()
            remotes.append(copy)
    for copy in remotes:
        copy.wait()


def collect(grads, ident, blocks=1):
    plan = cut([g.shape[1] * PLANE for g in grads], blocks)
    outs = [
        jax.ShapeDtypeStruct((g.shape[0] // PLANE, g.shape[1] * PLANE), g.dtype) for g in grads
    ]
    dma = pltpu.SemaphoreType.DMA
    n = len(plan)
    scratch = [pltpu.VMEM(g.shape, g.dtype) for g in grads]
    return call(
        functools.partial(collect_kernel, plan, len(grads)),
        tuple(grads),
        outs,
        scratch + [dma((len(grads),)), dma((n, PLANE)), dma((n, PLANE))],
        ident,
        8,
        sum(g.size for g in grads) / 3e4,
    )


def flat_place():
    return lax.axis_index("z") * PLANE + lax.axis_index("y") * 4 + lax.axis_index("blk")


def flat_id(d):
    return {"z": lax.div(d, PLANE), "y": lax.rem(lax.div(d, 4), 2), "blk": lax.rem(d, 4)}


def greet_all(count):
    barrier = pltpu.get_barrier_semaphore()
    me = flat_place()

    def one(i, carry):
        pl.semaphore_signal(
            barrier,
            inc=1,
            device_id=flat_id(lax.rem(me + i, count)),
            device_id_type=pl.DeviceIdType.MESH,
        )
        return carry

    lax.fori_loop(1, count, one, 0)
    pl.semaphore_wait(barrier, count - 1)


def to_all(count, source, target, ssem, rsem):
    me = flat_place()

    def copy(i):
        d = lax.rem(me + i, count)
        return pltpu.make_async_remote_copy(
            src_ref=source(d),
            dst_ref=target.at[me],
            send_sem=ssem.at[i],
            recv_sem=rsem.at[i],
            device_id=flat_id(d),
            device_id_type=pl.DeviceIdType.MESH,
        )

    def begin(i, carry):
        copy(i).start()
        return carry

    def finish(i, carry):
        copy(i).wait()
        return carry

    lax.fori_loop(1, count, begin, 0)
    target[me] = source(me)[...]
    lax.fori_loop(1, count, finish, 0)


def exchange_kernel(count, x, o, ssem, rsem):
    greet_all(count)
    to_all(count, lambda d: x.at[d], o, ssem, rsem)


def small_call(kernel, ins, outs, scratch, ident, micros):
    vmem = pl.BlockSpec(memory_space=pltpu.VMEM)
    return pl.pallas_call(
        kernel,
        out_shape=outs,
        in_specs=[vmem] * len(ins),
        out_specs=jax.tree.map(lambda _: vmem, outs),
        scratch_shapes=scratch,
        compiler_params=pltpu.CompilerParams(
            collective_id=ident, has_side_effects=True, vmem_limit_bytes=32 * MIB
        ),
        cost_estimate=pl.CostEstimate(
            flops=0, bytes_accessed=int(micros * 3.6e6), transcendentals=0
        ),
    )(*ins)


def exchange(x, ident):
    dma = pltpu.SemaphoreType.DMA((x.shape[0],))
    return small_call(
        functools.partial(exchange_kernel, x.shape[0]),
        (x,),
        jax.ShapeDtypeStruct(x.shape, x.dtype),
        [dma, dma],
        ident,
        8,
    )


def mods_back_kernel(count, x, w, o, t, got, part, mine, s0, r0, s1, r1, s2, r2):
    greet_all(count)
    to_all(count, lambda d: x.at[d], got, s0, r0)
    groups = o.shape[0]
    for g in range(groups):
        o[g] = got[4 * g] + got[4 * g + 1] + got[4 * g + 2] + got[4 * g + 3]
    own = o[...].reshape(groups * 8, o.shape[2])
    high = own.astype(BF)
    rest = own - high.astype(F32)
    low = rest.astype(BF)
    quarter = w.shape[0] // 4
    for q in range(4):
        piece = w[q * quarter : (q + 1) * quarter, :]
        product = times_t(high, piece) + times_t(low, piece)
        for g in range(groups):
            part[4 * g + q] = product[8 * g : 8 * g + 8]
    to_all(count, lambda d: part.at[d], mine, s1, r1)

    def add(i, total):
        return total + mine[i]

    part[flat_place()] = lax.fori_loop(0, count, add, jnp.zeros(mine.shape[1:], F32))
    to_all(count, lambda d: part.at[flat_place()], t, s2, r2)


def mods_back(x, w, ident):
    count, eight, cols = x.shape
    width = w.shape[0]
    dma = pltpu.SemaphoreType.DMA((count,))
    pieces = jax.ShapeDtypeStruct((count, eight, width // 4), F32)
    return small_call(
        functools.partial(mods_back_kernel, count),
        (x, w),
        (jax.ShapeDtypeStruct((count // 4, eight, cols), F32), pieces),
        [pltpu.VMEM(x.shape, F32), pltpu.VMEM(pieces.shape, F32), pltpu.VMEM(pieces.shape, F32)]
        + [dma] * 6,
        ident,
        20,
    )


def z_gather(x):
    return lax.all_gather(x, "z", axis=0, tiled=True)


def z_scatter(g):
    return lax.psum_scatter(g, "z", scatter_dimension=0, tiled=True)


def z_peer(m):
    z = lax.axis_index("z")
    if m == 1:
        z = z + 1 - 2 * lax.rem(z, 2)
    elif m == 2:
        z = lax.rem(z + 2, 4)
    else:
        z = 3 - z
    return z


def inner_plane():
    z = lax.axis_index("z")
    return (z == 1) | (z == 2)


def outer_plane():
    z = lax.axis_index("z")
    return (z == 0) | (z == 3)


def remote(src, dst, ssem, rsem, where):
    return pltpu.make_async_remote_copy(
        src_ref=src,
        dst_ref=dst,
        send_sem=ssem,
        recv_sem=rsem,
        device_id=where,
        device_id_type=pl.DeviceIdType.MESH,
    )


class OutRows:
    def __init__(self):
        z, j = lax.axis_index("z"), place(0)
        me = z * PLANE + j
        self.slot = lax.rem(me, 4)
        self.user = self.flat(self.slot * PLANE + lax.div(me, 4))
        self.owner = self.flat(4 * j + z)
        self.away, self.home = me != 4 * j + z, me == 4 * j + z

    @staticmethod
    def flat(d):
        return flat_id(d)


def greet_more(outs):
    barrier = pltpu.get_barrier_semaphore()

    def signal(where):
        pl.semaphore_signal(
            barrier, inc=1, device_id=where, device_id_type=pl.DeviceIdType.MESH
        )

    ids = [peer(k) for k in range(1, PLANE)] + [{"z": z_peer(m)} for m in (1, 2, 3)]
    for where in ids:
        signal(where)

    @pl.when(outs.away)
    def _():
        signal(outs.user)
        signal(outs.owner)
        pl.semaphore_wait(barrier, len(ids) + 2)

    pl.when(outs.home)(lambda: pl.semaphore_wait(barrier, len(ids)))


class PlaneCopy:
    shapes = staticmethod(lambda dma: [dma((4,)), dma((4,))])

    def __init__(self, full, sems):
        self.full = full
        self.m = full.shape[0] // 4
        self.ssem, self.rsem = sems

    def copy(self, slot, t, m):
        block = self.full.at[pl.ds(pl.multiple_of(t * self.m, self.m), self.m)]
        return remote(block, block, self.ssem.at[slot], self.rsem.at[slot], {"z": z_peer(m)})

    def begin(self):
        z = lax.axis_index("z")
        self.copy(1, z, 2).start()
        self.copy(0, z, 1).start()

    def relay(self):
        @pl.when(inner_plane())
        def _():
            self.copy(1, z_peer(2), 2).wait_recv()
            self.copy(3, z_peer(2), 1).start()
            self.copy(2, lax.axis_index("z"), 3).start()

    def finish(self):
        z = lax.axis_index("z")
        self.copy(0, z_peer(1), 1).wait_recv()

        @pl.when(inner_plane())
        def _():
            self.copy(2, z_peer(3), 3).wait_recv()
            self.copy(2, z, 3).wait_send()
            self.copy(3, z_peer(2), 1).wait_send()

        @pl.when(outer_plane())
        def _():
            self.copy(1, z_peer(2), 2).wait_recv()
            self.copy(3, z_peer(3), 1).wait_recv()

        self.copy(0, z, 1).wait_send()
        self.copy(1, z, 2).wait_send()


class PlaneSum:
    @staticmethod
    def shapes(m, c, dma):
        return [pltpu.VMEM((m, c), BF), dma((4,)), dma((4,))]

    def __init__(self, g, landing, scratch, temps):
        self.g, self.landing, self.temps = g, landing, temps
        self.q, self.ssem, self.rsem = scratch
        self.m, self.c = g.shape[1:]
        self.inner, self.outer = inner_plane(), outer_plane()

    def copy(self, src, slot, m):
        return pltpu.make_async_remote_copy(
            src_ref=src,
            dst_ref=self.landing.at[slot],
            send_sem=self.ssem.at[slot],
            recv_sem=self.rsem.at[slot],
            device_id={"z": z_peer(m)},
            device_id_type=pl.DeviceIdType.MESH,
        )

    def begin_far(self):
        pl.when(self.outer)(lambda: self.copy(self.g.at[z_peer(3)], 2, 1).start())

    def begin_swap(self):
        pl.when(self.inner)(lambda: self.copy(self.g.at[z_peer(3)], 3, 3).start())

    def begin(self):
        self.begin_far()
        self.begin_swap()

    def temp(self, i):
        return self.temps.at[i, pl.ds(0, self.m), pl.ds(0, self.c)]

    def load(self, src, i):
        copy = pltpu.make_async_copy(src, self.temp(i), self.tsem.at[i])
        copy.start()
        return copy

    def hop(self, tsem):
        self.tsem = tsem
        across = self.g.at[z_peer(2)]

        @pl.when(self.outer)
        def _():
            self.copy(across, 1, 2).start()

        @pl.when(self.inner)
        def _():
            first = self.load(across, 0)
            self.copy(across, 2, 1).wait_recv()
            second = self.load(self.landing.at[2], 1)
            first.wait()
            second.wait()

            def body(r, n):
                r = (pl.ds(r, n), pl.ds(0, self.c))
                total = self.temps[(0,) + r].astype(F32) + self.temps[(1,) + r].astype(F32)
                self.q[r] = total.astype(BF)

            rows_loop(self.m, body)
            self.copy(self.q, 1, 2).start()

        self.near = self.copy(self.g.at[z_peer(1)], 0, 1)
        self.near.start()

    def finish(self, tsem):
        self.tsem = tsem
        loads = [self.load(self.g.at[lax.axis_index("z")], 0)]
        self.near.wait_recv()
        loads.append(self.load(self.landing.at[0], 1))
        far = self.copy(self.q, 1, 2)
        far.wait_recv()
        loads.append(self.load(self.landing.at[1], 2))
        pl.when(self.inner)(lambda: self.copy(self.g.at[0], 3, 3).wait_recv())
        pl.when(self.inner)(lambda: self.load(self.landing.at[3], 3).wait())
        for copy in loads:
            copy.wait()
        far.wait_send()
        self.near.wait_send()
        pl.when(self.outer)(lambda: self.copy(self.g.at[0], 2, 1).wait_send())
        pl.when(self.inner)(lambda: self.copy(self.g.at[0], 3, 3).wait_send())

        def three(r, n):
            r = (pl.ds(r, n), pl.ds(0, self.c))
            total = self.temps[(0,) + r].astype(F32) + self.temps[(1,) + r].astype(F32)
            return r, total + self.temps[(2,) + r].astype(F32)

        def outer(r, n):
            r, total = three(r, n)
            self.q[r] = total.astype(BF)

        def inner(r, n):
            r, total = three(r, n)
            self.q[r] = (total + self.temps[(3,) + r].astype(F32)).astype(BF)

        pl.when(self.outer)(lambda: rows_loop(self.m, outer))
        pl.when(self.inner)(lambda: rows_loop(self.m, inner))


def deal(src, out, blocks, ssem, rsem):
    rows = out.shape[0]
    mine = place(0)
    copies = []
    for n, (_, base, width, col) in enumerate(cut([out.shape[1]], blocks)):
        cols = pl.ds(pl.multiple_of(base + mine * width, 128), width)
        for k in (6, 7, 2, 3, 4, 5, 1, 0):
            there = pl.ds(pl.multiple_of(place(k) * rows, 16), rows)
            piece = src.at[there, pl.ds(col, width)]
            if k:
                copies.append(send(piece, out.at[:, cols], ssem.at[n, k], rsem.at[n, k], k))
            else:
                copies.append(pltpu.make_async_copy(piece, out.at[:, cols], ssem.at[n, 0]))
                copies[-1].start()
    return copies


def pipe(body, steps, ins, outs):
    spec = lambda a: pl.BlockSpec(a[1], a[2])
    pltpu.emit_pipeline(
        body, grid=(steps,), in_specs=[spec(a) for a in ins], out_specs=[spec(a) for a in outs]
    )(*[a[0] for a in ins], *[a[0] for a in outs])


def whole(a):
    return (a, a.shape, lambda i: (0,) * len(a.shape))


def some_rows(a, n, pick=lambda i: i):
    return (a, (n, a.shape[1]), lambda i: (pick(i), 0))


def grads_mm(a, b, g):
    m = g.shape[1]

    def body(a, b, g):
        g[0] = over_rows(a[...], b[...]).astype(BF)

    pipe(
        body,
        g.shape[0],
        [(a, (a.shape[0], m), lambda i: (0, i)), whole(b)],
        [(g, (1,) + g.shape[1:], lambda i: (i, 0, 0))],
    )


def rows_mm(a, b, o, n, steps, pick=lambda i: i, transposed=False):
    def body(a, b, o):
        o[...] = (times_t if transposed else dot)(a[...], b[...]).astype(BF)

    pipe(body, steps, [some_rows(a, n, pick), whole(b)], [some_rows(o, n, pick)])


class Share:
    @staticmethod
    def shapes(w, blocks, dma):
        return [pltpu.VMEM(w, BF), dma, dma((blocks, PLANE)), dma((blocks, PLANE))]

    def __init__(self, w, full, blocks, scratch):
        self.w, self.full, self.blocks = w, full, blocks
        self.held, self.lsem, self.ssem, self.rsem = scratch
        self.load = pltpu.make_async_copy(w, self.held, self.lsem)
        self.load.start()

    def begin(self):
        self.load.wait()
        rows = self.w.shape[0]
        first = lax.axis_index("z") * (PLANE * rows) + place(0) * rows
        here = pl.ds(pl.multiple_of(first, rows), rows)
        self.copies = []
        for n, (_, base, width, col) in enumerate(cut([self.w.shape[1]], self.blocks)):
            dst = self.full.at[here, pl.ds(col, width)]
            for k in (6, 7, 2, 3, 4, 5, 1, 0):
                cols = pl.ds(pl.multiple_of(base + place(k) * width, 128), width)
                src = self.held.at[:, cols]
                if k:
                    copy = send(src, dst, self.ssem.at[n, k], self.rsem.at[n, k], k)
                else:
                    copy = pltpu.make_async_copy(src, dst, self.ssem.at[n, 0])
                    copy.start()
                self.copies.append(copy)

    def finish(self):
        for copy in self.copies:
            copy.wait()


IMAGES = 3


def whole_kernel(factor, names, *refs):
    v = dict(zip(names, refs))
    get = lambda *keys: [v[key] for key in keys]
    group_of = lambda prefix: [v[key] for key in names if key.startswith(prefix + ".")]
    cols, tok, cot, pick, mods = get("cols", "tok", "cot", "pick", "mods")
    first, second, dy, dat = get("first", "second", "dy", "dat")
    qkv, mixed, hid, slope = get("qkv", "mixed", "hid", "slope")
    du, part, part_y, dmix, dqkv = get("du", "part", "part_y", "dmix", "dqkv")
    xh, xv, xg, va, vb, vd = get("xh", "xv", "xg", "va", "vb", "vd")
    block_out, grad_tokens = get("block_out", "grad_tokens")
    img, temps, temps_out, tsem = get("img", "temps", "temps_out", "tsem")
    rows, width = tok.shape
    tokens = dy.shape[0]
    group = 4 * rows
    z, y, mine = lax.axis_index("z"), lax.axis_index("y"), place(0)
    odd, even = (lambda i: 2 * i + 1), (lambda i: 2 * i)
    outs = OutRows()

    qkv_in = Share(v["qkv_w"], v["full_qkv"], 3, group_of("in_qkv"))
    up_in = Share(v["up_w"], v["full_up"], 1, group_of("in_up"))
    down_in = Share(v["down_w"], v["full_down"], 1, group_of("in_down"))
    held, lsem, osems, rsems = group_of("in_out")
    out_load = pltpu.make_async_copy(v["out_w"], held, lsem)
    out_load.start()
    out_block = v["out_w"].shape[0]
    full_out = v["full_out"]
    out_at = lambda i: full_out.at[pl.ds(pl.multiple_of(i * out_block, out_block), out_block)]
    out_in = remote(held, out_at(outs.slot), osems.at[0], rsems.at[0], outs.user)
    out_local = pltpu.make_async_copy(held, out_at(z), osems.at[0])
    greet_more(outs)

    ma, mb = get("ma", "mb")
    sa, ra, sb, rb = group_of("mod_in")
    sent = []
    for m in (1, 2, 3):
        src = cols.at[pl.ds(2 * z_peer(m), 2)]
        sent.append(remote(src, ma.at[z], sa.at[m], ra.at[m], {"z": z_peer(m)}))
        sent[-1].start()
    out_load.wait()
    pl.when(outs.away)(lambda: out_in.start())
    pl.when(outs.home)(lambda: out_local.start())
    qkv_in.begin()
    ma[z] = cols[pl.ds(2 * z, 2)]
    for copy in sent:
        copy.wait()
    sent = []
    for k in range(1, PLANE):
        src = ma.at[:, peer(k)["y"]]
        sent.append(send(src, mb.at[mine], sb.at[k], rb.at[k], k))
    pl.when(outs.away)(lambda: out_in.wait())
    pl.when(outs.home)(lambda: out_local.wait())
    z_out = PlaneCopy(full_out, group_of("z_out"))
    z_out.begin()
    qkv_in.finish()
    z_qkv = PlaneCopy(v["full_qkv"], group_of("z_qkv"))
    z_qkv.begin()
    mb[mine] = ma[:, y]
    for copy in sent:
        copy.wait()
    each = cols.shape[2]
    for d in range(4 * PLANE):
        mods[:, d * each : (d + 1) * each] = mb[d % PLANE, d // PLANE]

    def picker(r):
        hot = pick[r, 0:128]
        ones = [hot[:, i : i + 1].astype(F32) for i in range(IMAGES)]

        def mod(which):
            at = slice(which * width, (which + 1) * width)
            return sum(ones[i] * mods[i : i + 1, at] for i in range(IMAGES))

        return mod

    def normed_of(x):
        inv = lax.rsqrt(jnp.mean(x * x, axis=-1, keepdims=True) + EPS)
        return inv, x * inv

    def norm_grad(inv, normed, d_normed):
        slant = jnp.mean(d_normed * normed, axis=-1, keepdims=True)
        return inv * (d_normed - normed * slant)

    def make_first(r, n):
        r = pl.ds(r, n)
        mod = picker(r)
        _, normed = normed_of(tok[r, :].astype(F32))
        xh[r, 0:width] = (normed * (1.0 + mod(1)) + mod(0)).astype(BF)
        xh[r, width:] = pick[r, :]
        xg[r, :] = (mod(5) * cot[r, :].astype(F32)).astype(BF)

    rows_loop(rows, make_first)
    to_first = Gather(xh, first, group_of("ga"))
    to_first.begin()
    up_in.begin()
    z_out.relay()
    to_first.relay()
    z_qkv.relay()
    to_first.finish()
    down_in.begin()
    up_in.finish()
    z_qkv.finish()
    z_up = PlaneCopy(v["full_up"], group_of("z_up"))
    z_up.begin()

    n = math.gcd(tokens, 256)

    def mm_body(a, b, o):
        o[...] = dot(a[...], b[...]).astype(BF)

    pipe(mm_body, tokens // n, [some_rows(first.at[:, 0:width], n), whole(v["full_qkv"])], [some_rows(qkv, n)])
    masks = [
        some_rows(first.at[:, width : width + 128], group),
        some_rows(first.at[:, width + 128 : width + 256], group),
    ]
    pipe(
        functools.partial(attend_kernel, factor),
        2,
        [some_rows(qkv, group)] + masks,
        [some_rows(mixed, group)],
    )
    down_in.finish()
    z_out.finish()
    rows_mm(mixed, full_out, part, rows, 4, odd)
    r_attn = Scatter(part, va, group_of("sc_a") + group_of("sems_1"))
    r_attn.begin()
    rows_mm(mixed, full_out, part, rows, 4, even)
    r_attn.load()
    r_attn.middle()
    r_attn.relay()
    z_up.relay()
    z_down = PlaneCopy(v["full_down"], group_of("z_down"))
    z_down.begin()
    r_attn.finish()

    def make_second(r, n):
        r = pl.ds(r, n)
        mod = picker(r)
        x = tok[r, :].astype(F32) + mod(2) * va[r, :]
        vd[r, :] = x
        xv[r, :] = (normed_of(x)[1] * (1.0 + mod(4)) + mod(3)).astype(BF)

    rows_loop(rows, make_second)
    to_second = Gather(xv, second, group_of("gb"))
    to_second.begin()
    to_second.relay()
    to_second.finish()
    to_dy = Gather(xg, dy, group_of("gc"))
    to_dy.begin()
    z_up.finish()

    def up_body(a, b, h, s):
        u = dot(a[...], b[...])
        c = math.sqrt(2.0 / math.pi)
        t = jnp.tanh(c * (u + 0.044715 * (u * u * u)))
        h[...] = (0.5 * u * (1.0 + t)).astype(BF)
        inside = c * (1.0 + (3 * 0.044715) * (u * u))
        s[...] = 0.5 * (1.0 + t) + 0.5 * u * (1.0 - t * t) * inside

    pipe(
        up_body,
        tokens // n,
        [some_rows(second, n), whole(v["full_up"])],
        [some_rows(hid, n), some_rows(slope, n)],
    )
    to_dy.relay()
    z_down.relay()
    to_dy.finish()
    sums = [
        PlaneSum(v["g_" + key], v["land_" + key], group_of("s_" + key), t)
        for key, t in (("down", temps), ("up", temps), ("qkv", temps), ("out", temps_out))
    ]
    s_down, s_up, s_qkv, s_out = sums
    grads_mm(dy, hid, v["g_down"])
    s_down.begin_far()
    z_down.finish()
    s_down.begin_swap()

    def du_body(a, b, s, o):
        o[...] = (dot(a[...], b[...]) * s[...]).astype(BF)

    pipe(
        du_body,
        tokens // n,
        [some_rows(dy, n), whole(v["full_down"]), some_rows(slope, n)],
        [some_rows(du, n)],
    )
    s_down.hop(tsem)
    rows_mm(du, v["full_up"], part, rows, 4, odd, True)
    r_e2 = Scatter(part, vb, group_of("sc_a") + group_of("sems_2"))
    r_e2.begin()
    rows_mm(du, v["full_up"], part, rows, 4, even, True)
    r_e2.load()
    r_e2.middle()
    grads_mm(second, du, v["g_up"])
    s_up.begin()
    r_e2.relay()
    r_e2.finish()

    pv = v["sc_b.0"]
    parts = [(pv.at[0], pv.at[1]), (pv.at[2], pv.at[3]), (xg, xh.at[:, 0:width])]

    def tally(which, r, value):
        high = value.astype(BF)
        parts[which][0][r, :] = high
        parts[which][1][r, :] = (value - high.astype(F32)).astype(BF)

    def flush(blocks):
        hot = pick[:, 0:128]
        for (high, low), which in zip(parts, blocks):
            total = over_rows(hot, high[...]) + over_rows(hot, low[...])
            img[:, which * width : (which + 1) * width] = total[0:8]

    def norm_back(r, n):
        r = pl.ds(r, n)
        mod = picker(r)
        inv, normed = normed_of(vd[r, :])
        e = vb[r, :]
        d_mid = cot[r, :].astype(F32) + norm_grad(inv, normed, e * (1.0 + mod(4)))
        grad_tokens[r, :] = d_mid
        xv[r, :] = (mod(2) * d_mid).astype(BF)
        tally(0, r, e)
        tally(1, r, e * normed)
        tally(2, r, d_mid * va[r, :])

    rows_loop(rows, norm_back)
    load_w = pltpu.make_async_copy(v["mod_w_in"], v["mod_w"], group_of("mod_out")[10].at[0])
    load_w.start()
    to_dat = Gather(xv, dat, group_of("gd"))
    to_dat.begin()
    flush((3, 4, 2))
    rows_mm(hid, v["full_down"], part_y, rows, 8, transposed=True)
    to_dat.relay()
    to_dat.finish()
    s_up.hop(tsem)
    r_y = Scatter(part_y, va, group_of("sc_b") + group_of("sems_3"))
    r_y.begin()
    r_y.load()
    rows_mm(dat, full_out, dmix, 2 * rows, 4, transposed=True)
    r_y.middle()
    pipe(
        functools.partial(attend_back_kernel, factor),
        2,
        [some_rows(qkv, group)] + masks + [some_rows(dmix, group)],
        [some_rows(dqkv, group)],
    )
    r_y.relay()
    grads_mm(first.at[:, 0:width], dqkv, v["g_qkv"])
    s_qkv.begin()
    dealt = []
    deal_sems = group_of("deal")

    def settle(s, out, blocks, sems):
        s.finish(tsem)
        dealt.extend(deal(s.q, out, blocks, *sems))

    r_y.finish()
    rows_mm(dqkv, v["full_qkv"], part, rows, 4, odd, True)
    r_e1 = Scatter(part, vb, group_of("sc_a") + group_of("sems_4"))
    r_e1.begin()
    rows_mm(dqkv, v["full_qkv"], part, rows, 4, even, True)
    r_e1.load()
    r_e1.middle()
    s_qkv.hop(tsem)

    def out_body(a, b, g):
        g[...] = over_rows(a[...], b[...]).astype(BF).reshape(g.shape)

    step = math.gcd(width, 512)
    g_out = v["g_out"]
    pipe(
        out_body,
        width // step,
        [whole(mixed), (dat, (tokens, step), lambda i: (0, i))],
        [(g_out, g_out.shape[:2] + (step,), lambda i: (0, 0, i))],
    )
    s_out.begin()
    r_e1.relay()
    s_out.hop(tsem)
    settle(s_down, v["c_down"], 1, deal_sems[:2])
    r_e1.finish()

    def last_norm(r, n):
        r = pl.ds(r, n)
        mod = picker(r)
        inv, normed = normed_of(tok[r, :].astype(F32))
        e, out = vb[r, :], va[r, :]
        grad_tokens[r, :] += norm_grad(inv, normed, e * (1.0 + mod(1)))
        block_out[r, :] = (vd[r, :] + mod(5) * out).astype(BF)
        tally(0, r, e)
        tally(1, r, e * normed)
        tally(2, r, cot[r, :].astype(F32) * out)

    rows_loop(rows, last_norm)
    flush((0, 1, 5))

    pa, ga, gs, gb, pc, pd, pe, ts = get("pa", "ga_", "gs", "gb_", "pc", "pd", "pe", "ts")
    w, t_all, dm = get("mod_w", "t_all", "dm")
    sems = group_of("mod_out")
    for d in range(4 * PLANE):
        t = d // PLANE * IMAGES
        pa[d % PLANE, t : t + IMAGES] = img[0:IMAGES, d * each : (d + 1) * each]
    plane_sent = lambda src, dst, s, r: [
        send(src(k), dst, s.at[k], r.at[k], k) for k in range(1, PLANE)
    ]
    sent = plane_sent(lambda k: pa.at[place(k)], ga.at[mine], sems[0], sems[1])
    ga[mine] = pa[mine]
    gs[...] = jnp.zeros_like(gs)
    for copy in sent:
        copy.wait()
    for g in range(2):
        total = ga[4 * g] + ga[4 * g + 1] + ga[4 * g + 2] + ga[4 * g + 3]
        for t in range(4):
            gs[t, g * IMAGES : (g + 1) * IMAGES] = total[t * IMAGES : (t + 1) * IMAGES]
    sent = []
    for m in (1, 2, 3):
        copy = remote(
            gs.at[z_peer(m)], gb.at[z], sems[2].at[m], sems[3].at[m], {"z": z_peer(m)}
        )
        copy.start()
        sent.append(copy)
    gb[z] = gs[z]
    s_up.finish(tsem)
    s_out.finish(tsem)
    back = remote(s_out.q, v["c_out"], tsem.at[4], tsem.at[5], outs.owner)
    back_local = pltpu.make_async_copy(s_out.q, v["c_out"], tsem.at[4])
    pl.when(outs.away)(lambda: back.start())
    pl.when(outs.home)(lambda: back_local.start())
    for copy in sent:
        copy.wait()
    load_w.wait()
    dm[...] = gb[...]
    own = dm[...].reshape(4 * 8, each)
    high = own.astype(BF)
    low = (own - high.astype(F32)).astype(BF)
    slice_of = width // PLANE
    for k in range(PLANE):
        piece = w[k * slice_of : (k + 1) * slice_of, :]
        pc[k] = times_t(high, piece) + times_t(low, piece)
    sent = plane_sent(lambda k: pc.at[place(k)], pd.at[mine], sems[4], sems[5])
    pd[mine] = pc[mine]
    dealt.extend(deal(s_up.q, v["c_up"], 1, *deal_sems[2:4]))
    for copy in sent:
        copy.wait()
    total = pd[0]
    for k in range(1, PLANE):
        total = total + pd[k]
    pe[z] = total
    sent = []
    for m in (1, 2, 3):
        copy = remote(pe.at[z], pe.at[z], sems[6].at[m], sems[7].at[m], {"z": z_peer(m)})
        copy.start()
        sent.append(copy)
    settle(s_qkv, v["c_qkv"], 3, deal_sems[4:6])
    for copy in sent:
        copy.wait()
    ts[...] = pe[0] + pe[1] + pe[2] + pe[3]
    sent = plane_sent(lambda k: ts, t_all.at[mine], sems[8], sems[9])
    t_all[mine] = ts[...]
    for copy in sent:
        copy.wait()
    for copy in dealt:
        copy.wait()
    pl.when(outs.away)(lambda: back.wait())
    pl.when(outs.home)(lambda: back_local.wait())


def whole_block(cols, tok, cot, pick, mod_w, qkv_w, out_w, up_w, down_w, factor, ident):
    rows, width = tok.shape
    nz, tokens = 4, PLANE * rows
    share = qkv_w.shape[0]
    m = share * PLANE
    wide, part, heads = up_w.shape[1] // PLANE, qkv_w.shape[1] // PLANE, nz * out_w.shape[0]
    each = cols.shape[2]
    struct, vm, dma = jax.ShapeDtypeStruct, pltpu.VMEM, pltpu.SemaphoreType.DMA
    vmem = pl.BlockSpec(memory_space=pltpu.VMEM)
    anywhere = pl.BlockSpec(memory_space=pl.ANY)
    ins = dict(cols=cols, tok=tok, cot=cot, pick=pick)
    far_ins = dict(mod_w_in=mod_w, qkv_w=qkv_w, out_w=out_w, up_w=up_w, down_w=down_w)
    near = dict(
        block_out=struct((rows, width), BF),
        grad_tokens=struct((rows, width), F32),
        dm=struct((nz, 8, each), F32),
        t_all=struct((PLANE, 32, width // PLANE), F32),
    )
    far = dict(
        c_down=struct((share, wide * PLANE), BF),
        c_up=struct((share, wide * PLANE), BF),
        c_qkv=struct((share, part * PLANE), BF),
        c_out=struct((heads // nz, width), BF),
        full_qkv=struct((nz * m, part), BF),
        full_out=struct((heads, width), BF),
        full_up=struct((nz * m, wide), BF),
        full_down=struct((nz * m, wide), BF),
        first=struct((tokens, width + 256), BF),
        second=struct((tokens, width), BF),
        dy=struct((tokens, width), BF),
        dat=struct((tokens, width), BF),
        qkv=struct((tokens, part), BF),
        mixed=struct((tokens, heads), BF),
        hid=struct((tokens, wide), BF),
        slope=struct((tokens, wide), F32),
        du=struct((tokens, wide), BF),
        part=struct((tokens, width), BF),
        part_y=struct((tokens, width), BF),
        dmix=struct((tokens, heads), BF),
        dqkv=struct((tokens, part), BF),
    )
    shapes = dict(
        down=(nz, m, wide), up=(nz, m, wide), qkv=(nz, m, part), out=(nz, heads // nz, width)
    )
    for key, shape in shapes.items():
        far["g_" + key] = struct(shape, BF)
        far["land_" + key] = struct(shape, BF)
    own = vm((rows, width), F32)
    scratch = dict(
        mods=vm((8, 6 * width), F32),
        img=vm((8, 6 * width), F32),
        ma=vm((nz, 2, 8, each), F32),
        mb=vm((PLANE, nz, 8, each), F32),
        xh=vm((rows, width + 256), BF),
        xv=vm((rows, width), BF),
        xg=vm((rows, width), BF),
        va=own,
        vb=own,
        vd=own,
        temps=vm((4, m, max(wide, part)), BF),
        temps_out=vm((4,) + shapes["out"][1:], BF),
        tsem=dma((6,)),
        mod_w=vm(mod_w.shape, BF),
        pa=vm((PLANE, 16, each), F32),
        ga_=vm((PLANE, 16, each), F32),
        gs=vm((nz, 8, each), F32),
        gb_=vm((nz, 8, each), F32),
        pc=vm((PLANE, 32, width // PLANE), F32),
        pd=vm((PLANE, 32, width // PLANE), F32),
        pe=vm((nz, 32, width // PLANE), F32),
        ts=vm((32, width // PLANE), F32),
    )

    def add(prefix, items):
        for i, item in enumerate(items):
            scratch[prefix + "." + str(i)] = item

    add("in_qkv", Share.shapes(qkv_w.shape, 3, dma))
    add("in_up", Share.shapes(up_w.shape, 1, dma))
    add("in_down", Share.shapes(down_w.shape, 1, dma))
    add("in_out", [vm(out_w.shape, BF), dma, dma((1,)), dma((1,))])
    add("mod_in", [dma((4,)), dma((4,)), dma((PLANE,)), dma((PLANE,))])
    add("mod_out", [dma((PLANE,))] * 10 + [dma((1,))])
    for key in ("ga", "gb", "gc", "gd"):
        add(key, Gather.shapes(dma))
    sc = Scatter.shapes(rows, width, dma)
    add("sc_a", sc[:8])
    add("sc_b", sc[:8])
    for i in range(1, 5):
        add("sems_" + str(i), sc[8:])
    for key, shape in shapes.items():
        add("z_" + key, PlaneCopy.shapes(dma))
        add("s_" + key, PlaneSum.shapes(shape[1], shape[2], dma))
    add("deal", [dma((b, PLANE)) for b in (1, 1, 1, 1, 3, 3)])
    names = list(ins) + list(far_ins) + list(near) + list(far) + list(scratch)
    outs = pl.pallas_call(
        functools.partial(whole_kernel, factor, names),
        out_shape=list(near.values()) + list(far.values()),
        in_specs=[vmem] * len(ins) + [anywhere] * len(far_ins),
        out_specs=[vmem] * len(near) + [anywhere] * len(far),
        scratch_shapes=list(scratch.values()),
        compiler_params=pltpu.CompilerParams(
            collective_id=ident, has_side_effects=True, vmem_limit_bytes=62 * MIB
        ),
        cost_estimate=pl.CostEstimate(
            flops=0, bytes_accessed=int(450 * 3.6e6), transcendentals=0
        ),
    )(*ins.values(), *far_ins.values())
    return dict(zip(list(near) + list(far), outs))


def norm_mod(value, shift, scale):
    normed = value * lax.rsqrt(jnp.mean(value * value, axis=-1, keepdims=True) + EPS)
    return normed * (1.0 + scale) + shift


def dot(a, b):
    return jnp.dot(a, b, preferred_element_type=F32)


def over_rows(left, right):
    return lax.dot_general(left, right, (((0,), (0,)), ((), ())), preferred_element_type=F32)


def times_t(left, right):
    return lax.dot_general(left, right, (((1,), (1,)), ((), ())), preferred_element_type=F32)


def allowed_pairs(seg, key, r):
    same = times_t(seg[r, :], key[...]) > 0.5
    rows = lax.broadcasted_iota(jnp.int32, same.shape, 0) + r.start
    return same | (rows == lax.broadcasted_iota(jnp.int32, same.shape, 1))


def softmax_rows(q, k, allowed, factor):
    scores = jnp.where(allowed, times_t(q, k) * factor, NEG)
    expo = jnp.exp(scores - jnp.max(scores, axis=-1, keepdims=True))
    return expo / jnp.sum(expo, axis=-1, keepdims=True)


def row_blocks(count):
    step = math.gcd(count, 256)
    return [slice(i, i + step) for i in range(0, count, step)]


def attend_kernel(factor, qkv, seg, key, o):
    n = o.shape[1]
    for r in row_blocks(o.shape[0]):
        allowed = allowed_pairs(seg, key, r)
        for c in range(0, n, HEAD_DIM):
            k = qkv[:, n + c : n + c + HEAD_DIM]
            v = qkv[:, 2 * n + c : 2 * n + c + HEAD_DIM]
            prob = softmax_rows(qkv[r, c : c + HEAD_DIM], k, allowed, factor)
            o[r, c : c + HEAD_DIM] = dot(prob.astype(BF), v).astype(BF)


def attend_back_kernel(factor, qkv, seg, key, d_o, d_qkv):
    n = d_o.shape[1]
    for c in range(0, n, HEAD_DIM):
        k = qkv[:, n + c : n + c + HEAD_DIM]
        v = qkv[:, 2 * n + c : 2 * n + c + HEAD_DIM]
        dk = dv = 0.0
        for r in row_blocks(d_o.shape[0]):
            q = qkv[r, c : c + HEAD_DIM]
            out = d_o[r, c : c + HEAD_DIM]
            prob = softmax_rows(q, k, allowed_pairs(seg, key, r), factor)
            d_prob = times_t(out, v)
            delta = jnp.sum(prob * d_prob, axis=-1, keepdims=True)
            d_scores = (prob * (d_prob - delta)).astype(BF)
            d_qkv[r, c : c + HEAD_DIM] = (dot(d_scores, k) * factor).astype(BF)
            dk = dk + over_rows(d_scores, q)
            dv = dv + over_rows(prob.astype(BF), out)
        d_qkv[:, n + c : n + c + HEAD_DIM] = (dk * factor).astype(BF)
        d_qkv[:, 2 * n + c : 2 * n + c + HEAD_DIM] = dv.astype(BF)


def per_group(kernel, qkv, first, d_o, columns, group, flops):
    last = first.shape[1] // 128
    block = lambda c: pl.BlockSpec((group, c), lambda i: (i, 0))
    mask = lambda c: pl.BlockSpec((group, 128), lambda i: (i, c))
    return pl.pallas_call(
        kernel,
        grid=(qkv.shape[0] // group,),
        out_shape=jax.ShapeDtypeStruct((qkv.shape[0], columns), BF),
        in_specs=[block(qkv.shape[1]), mask(last - 2), mask(last - 1)]
        + [block(a.shape[1]) for a in d_o],
        out_specs=block(columns),
        compiler_params=pltpu.CompilerParams(vmem_limit_bytes=48 * MIB),
        cost_estimate=pl.CostEstimate(flops=flops, bytes_accessed=0, transcendentals=0),
    )(qkv, first, first, *d_o)


def after(value, *others):
    return lax.optimization_barrier((value,) + others)[0]


def on_device(
    tokens,
    noise_table,
    mod_weight,
    qkv_weight,
    out_weight,
    up_weight,
    down_weight,
    segment,
    key_valid,
    noise_level,
    cotangent,
):
    rows, width = tokens.shape[1:]
    images = noise_level.shape[1]
    nz = lax.axis_size("z")
    blk = lax.axis_index("blk")
    groups = 2 * nz
    factor = 1.0 / math.sqrt(HEAD_DIM)
    levels = noise_level.reshape(-1)
    cond = jnp.take(noise_table, levels, axis=0)
    cols = dot(cond, mod_weight).reshape(groups, images, -1)
    cols = jnp.pad(cols, ((0, 0), (0, 8 - images), (0, 0)))

    own = lambda a: lax.dynamic_slice_in_dim(a[0], blk * rows, rows, 0)[:, None]
    lane = jnp.arange(256, dtype=jnp.int32)[None, :]
    hot = (own(segment) == lane % 128) & ((lane < 128) | (own(key_valid) == 1))
    pick = hot.astype(BF)

    args = (tokens[0], cotangent[0], pick, mod_weight)
    weights = (qkv_weight, out_weight, up_weight, down_weight)
    run = on_four_planes if nz == 4 else on_any_planes
    out = run(cols, *args, *weights, factor, images)
    block_out, grad_tokens, mod_grads, cond_grads, d_qkv_w, d_outp, d_up, d_down = out
    grad_mod = lax.dot_general(
        cond.astype(F32), mod_grads, (((0,), (0,)), ((), ())), precision=HIGH
    )
    grad_table = jax.ops.segment_sum(cond_grads, levels, num_segments=noise_table.shape[0])
    return (
        block_out[None],
        grad_tokens[None],
        grad_table,
        grad_mod,
        d_qkv_w.astype(F32),
        d_outp.astype(F32),
        d_up.astype(F32),
        d_down.astype(F32),
    )


def on_four_planes(
    cols, tok, cot, pick, mod_weight, qkv_weight, out_weight, up_weight, down_weight, factor, images
):
    out = whole_block(
        cols,
        tok,
        cot,
        pick,
        mod_weight,
        qkv_weight,
        out_weight,
        up_weight,
        down_weight,
        factor,
        1,
    )
    count, width = cols.shape[0] * images, tok.shape[1]
    mod_grads = out["dm"][:, : 2 * images].reshape(count, -1)
    cond_grads = out["t_all"].reshape(PLANE, 4, 8, width // PLANE)[:, :, : 2 * images]
    cond_grads = cond_grads.transpose(1, 2, 0, 3).reshape(count, width)
    return (
        out["block_out"],
        out["grad_tokens"],
        mod_grads,
        cond_grads,
        out["c_qkv"],
        out["c_out"],
        out["c_up"],
        out["c_down"],
    )


def on_any_planes(
    cols, tok, cot, pick, mod_weight, qkv_weight, out_weight, up_weight, down_weight, factor, images
):
    rows, width = tok.shape
    nz, blks = lax.axis_size("z"), lax.axis_size("blk")
    devices = nz * PLANE
    group = rows * blks
    own_cols = HEADS // PLANE * HEAD_DIM
    sent = jnp.broadcast_to(cols[:, None], (2 * nz, blks) + cols.shape[1:])
    mods = exchange(sent.reshape((devices,) + cols.shape[1:]), 14)[:, :images]
    mods = mods.transpose(1, 0, 2).reshape(images, 6, width)

    (qkv_part,) = spread([after(qkv_weight, mods)], 1, blocks=3)
    qkv_w = z_gather(qkv_part)
    move = [(nz * k + i, i * PLANE + k) for k in range(PLANE) for i in range(nz)]
    outp = lax.ppermute(after(out_weight, qkv_part), ALL, move)

    picker = pick[:, :images].astype(F32)
    shift1, scale1, gate1, shift2, scale2, gate2 = (
        jnp.dot(picker, mods[:, i], precision=HIGH) for i in range(6)
    )
    x_in, grad_in = tok.astype(F32), cot.astype(F32)
    first_f, first_back = jax.vjp(norm_mod, x_in, shift1, scale1)
    first = jnp.concatenate([first_f.astype(BF), pick], axis=1)
    first_all = plane_gather(after(first, qkv_part), 2)
    first = first_all[:, :width]
    up_part, down_part = spread([after(up_weight, first), down_weight], 3)
    outp_w, up_w, down_w = z_gather(outp), z_gather(up_part), z_gather(down_part)

    qkv = dot(first, qkv_w).astype(BF)
    cost = 4 * 2 * group * group * own_cols
    mixed = per_group(
        functools.partial(attend_kernel, factor), qkv, first_all, [], own_cols, group, 5 * cost
    )
    attn = plane_scatter(dot(mixed, outp_w).astype(BF), 6)
    x_mid = x_in + gate1 * attn
    second_f, second_back = jax.vjp(norm_mod, x_mid, shift2, scale2)
    second = plane_gather(second_f.astype(BF), 7)
    hidden_f, gelu_back = jax.vjp(jax.nn.gelu, dot(second, up_w))
    hidden = hidden_f.astype(BF)

    d_branch = plane_gather(after((gate2 * grad_in).astype(BF), hidden), 5)
    d_down = z_scatter(over_rows(d_branch, hidden).astype(BF))
    d_pre = gelu_back(dot(d_branch, down_w))[0].astype(BF)
    d_up = z_scatter(over_rows(second, d_pre).astype(BF))
    d_second = plane_scatter(times_t(d_pre, up_w).astype(BF), 9)
    d_mid_norm, d_shift2, d_scale2 = second_back(d_second)
    d_mid = grad_in + d_mid_norm
    d_gate1 = d_mid * attn
    d_attn = plane_gather((gate1 * d_mid).astype(BF), 10)
    d_mixed = times_t(d_attn, outp_w).astype(BF)
    d_qkv = per_group(
        functools.partial(attend_back_kernel, factor),
        qkv,
        first_all,
        [d_mixed],
        3 * own_cols,
        group,
        10 * cost,
    )
    d_qkv_w = z_scatter(over_rows(first, d_qkv).astype(BF))
    d_outp = z_scatter(over_rows(mixed, d_attn).astype(BF))
    d_first = plane_scatter(times_t(d_qkv, qkv_w).astype(BF), 11)
    d_in_norm, d_shift1, d_scale1 = first_back(d_first)
    part = times_t(after(hidden, d_first), down_w).astype(BF)
    branch = plane_scatter(part, 8)
    block_out = (x_mid + gate2 * branch).astype(BF)
    d_gate2 = grad_in * branch

    tok_grads = jnp.concatenate([d_shift1, d_scale1, d_gate1, d_shift2, d_scale2, d_gate2], axis=1)
    image_grads = lax.dot_general(
        pick[:, :8].astype(F32), tok_grads, (((0,), (0,)), ((), ())), precision=HIGH
    )
    sent = image_grads.reshape(8, devices, -1).transpose(1, 0, 2)
    mod_grads, cond_grads = mods_back(sent, mod_weight, 15)
    count = 2 * nz * images
    mod_grads = mod_grads[:, :images].reshape(count, -1)
    cond_grads = cond_grads.reshape(2 * nz, 4, 8, width // 4)[:, :, :images]
    cond_grads = cond_grads.transpose(0, 2, 1, 3).reshape(count, width)

    d_up, d_down = collect([after(d_up, sent), d_down], 12)
    (d_qkv_w,) = collect([after(d_qkv_w, d_up)], 13, blocks=3)
    d_outp = lax.ppermute(d_outp, ALL, [(b, a) for a, b in move])
    grads = (d_qkv_w, d_outp, d_up, d_down)
    return (block_out, d_mid + d_in_norm, mod_grads, cond_grads) + grads


def solution(mesh):
    groups, blks = mesh.shape["dp"], mesh.shape["blk"]
    planes = Mesh(mesh.devices.reshape(groups // 2, 2, blks), ALL)
    dp = ("z", "y")
    whole = ("z", "y", "blk")
    placed = (
        P(dp, "blk", None),
        P(),
        P(None, whole),
        P(whole, None),
        P(whole, None),
        P(whole, None),
        P(whole, None),
        P(dp, None),
        P(dp, None),
        P(),
        P(dp, "blk", None),
    )
    return jax.shard_map(
        on_device,
        mesh=planes,
        in_specs=placed,
        out_specs=(
            P(dp, "blk", None),
            P(dp, "blk", None),
            P(),
            P(None, whole),
            P(whole, None),
            P(whole, None),
            P(whole, None),
            P(whole, None),
        ),
        check_vma=False,
    )
```
